32 devices in a mesh: dp: 8 (over z, x), mp: 4 (over y, core).
Axes of the slice: x: 2, y: 2, z: 4, core: 2. Of those that a mesh axis runs over, the one named last changes fastest.
Arguments:
- states: bfloat16 [16, 1024, 768], P('dp'), may hold values from -6 to 6
- span_count: int32 [8], P('dp'), may hold values from 1 to 2, as said below
- qkv_weight: bfloat16 [768, 3, 768], P(None, None, 'mp'), may hold values from -0.21875 to 0.21875
- q_bias: float32 [768], P('mp'), may hold values from -1.5 to 1.5
- v_bias: float32 [768], P('mp'), may hold values from -1.5 to 1.5
- out_weight: bfloat16 [768, 768], P(None, 'mp'), may hold values from -3.5 to 3.5
- out_bias: float32 [768], replicated, may hold values from -1.5 to 1.5
- gain_one: float32 [768], replicated, may hold values from 0.5 to 1.5
- shift_one: float32 [768], replicated, may hold values from -1.5 to 1.5
- up_weight: bfloat16 [768, 3072], P(None, 'mp'), may hold values from -0.21875 to 0.21875
- up_bias: float32 [3072], P('mp'), may hold values from -1.5 to 1.5
- down_weight: bfloat16 [768, 3072], P(None, 'mp'), may hold values from -0.109375 to 0.109375
- down_bias: float32 [768], replicated, may hold values from -1.5 to 1.5
- gain_two: float32 [768], replicated, may hold values from 0.5 to 1.5
- shift_two: float32 [768], replicated, may hold values from -1.5 to 1.5
- cotangent: bfloat16 [16, 1024, 768], P('dp'), may hold values from -6 to 6
Outputs:
- states_out: bfloat16 [16, 1024, 768], P('dp')
- states_grad: bfloat16 [16, 1024, 768], P('dp')
- qkv_weight_grad: float32 [768, 3, 768], P(None, None, 'mp')
- q_bias_grad: float32 [768], P('mp')
- v_bias_grad: float32 [768], P('mp')
- out_weight_grad: float32 [768, 768], P(None, 'mp')
- out_bias_grad: float32 [768], replicated
- gain_one_grad: float32 [768], replicated
- shift_one_grad: float32 [768], replicated
- up_weight_grad: float32 [768, 3072], P(None, 'mp')
- up_bias_grad: float32 [3072], P('mp')
- down_weight_grad: float32 [768, 3072], P(None, 'mp')
- down_bias_grad: float32 [768], replicated
- gain_two_grad: float32 [768], replicated
- shift_two_grad: float32 [768], replicated
The draws below stay inside these ranges and needn't reach their ends.
Inputs may be any that keep to these rules, and one draw needn't show every extreme that they name: Slots 0 to span_count[g] - 1 of dp index g hold live spans, the rest padding; some index has 2 live spans and some one.
All inputs are finite; a program needn't handle non-finite values.
Results may differ from the reference program's by a relative error of at most 0.022.
Values may be sent and summed in bfloat16 or wider, within the bound.
No kernel may reach another device: no remote copies, remote signals or barrier semaphores. Data moves between devices by JAX's collectives and lax.ppermute only.
A program may use at most 192 MiB of HBM per device.

```python
import jax
import jax.numpy as jnp
from jax import lax

D = 768
HEADS = 12
HEAD = 64
FF = 3072
SPAN = 1024
SLOTS = 2
GROUPS = 8
SPANS = 16
N_MP = 4


def draw_span_count(key, part):
    key = jax.random.fold_in(key, 11)
    first_key, second_key, third_key = jax.random.split(key, 3)
    counts = jax.random.randint(first_key, (GROUPS,), 1, SLOTS + 1)
    fullest = jax.random.randint(second_key, (), 0, GROUPS)
    lightest = (fullest + jax.random.randint(third_key, (), 1, GROUPS)) % GROUPS
    counts = counts.at[fullest].set(SLOTS).at[lightest].set(1)
    return counts.astype(jnp.int32)


def level_of(rng, shape, cuts, least, high):
    level = 1.0
    for dim, parts in cuts:
        steps = jax.random.uniform(jax.random.fold_in(jax.random.fold_in(rng, 6), dim), (parts,), jnp.float32, least / len(cuts), high / len(cuts))
        level = level * jnp.repeat(jnp.exp(steps), shape[dim] // parts).reshape((-1,) + (1,) * (len(shape) - 1 - dim))
    return level


def gaussian(own_key, extent, deviation, bound, shards=(), kind=jnp.bfloat16):
    drawn = jax.random.normal(own_key, extent, jnp.float32) * deviation
    if len(shards) > 0:
        drawn = level_of(own_key, extent, shards, -0.22, 0.18) * drawn
    return jnp.clip(drawn, min=-bound, max=bound).astype(kind)


def setup_inputs(seed: int = 0) -> dict:
    key_of = jax.random.split(jax.random.key(seed), 17)
    states = gaussian(key_of[0], (SPANS, SPAN, D), 1.0, 6.0, ((0, 8),))
    span_count = draw_span_count(jax.random.fold_in(key_of[16], 71), 0)
    qkv_weight = gaussian(key_of[2], (D, 3, HEADS * HEAD), D ** -0.5, 0.21875, ((2, 4),))
    q_bias = gaussian(key_of[3], (HEADS * HEAD,), 0.3, 1.5, ((0, 4),), jnp.float32)
    v_bias = gaussian(key_of[4], (HEADS * HEAD,), 0.3, 1.5, ((0, 4),), jnp.float32)
    out_weight = gaussian(key_of[5], (D, HEADS * HEAD), (max(D // 256, 1)) ** -0.5, 3.5, ((1, 4),))
    out_bias = gaussian(key_of[6], (D,), 0.3, 1.5, (), jnp.float32)
    gain_one = jnp.clip(1.0 + 0.1 * jax.random.normal(key_of[7], (D,), jnp.float32), 0.5, 1.5)
    shift_one = gaussian(key_of[8], (D,), 0.3, 1.5, (), jnp.float32)
    up_weight = gaussian(key_of[9], (D, FF), D ** -0.5, 0.21875, ((1, 4),))
    up_bias = gaussian(key_of[10], (FF,), 0.3, 1.5, ((0, 4),), jnp.float32)
    down_weight = gaussian(key_of[11], (D, FF), FF ** -0.5, 0.109375, ((1, 4),))
    down_bias = gaussian(key_of[12], (D,), 0.3, 1.5, (), jnp.float32)
    gain_two = jnp.clip(1.0 + 0.1 * jax.random.normal(key_of[13], (D,), jnp.float32), 0.5, 1.5)
    shift_two = gaussian(key_of[14], (D,), 0.3, 1.5, (), jnp.float32)
    cotangent = gaussian(key_of[15], (SPANS, SPAN, D), 1.0, 6.0, ((0, 8),))
    return dict(states=states, span_count=span_count, qkv_weight=qkv_weight, q_bias=q_bias, v_bias=v_bias, out_weight=out_weight, out_bias=out_bias, gain_one=gain_one, shift_one=shift_one, up_weight=up_weight, up_bias=up_bias, down_weight=down_weight, down_bias=down_bias, gain_two=gain_two, shift_two=shift_two, cotangent=cotangent)


@jax.custom_vjp
def low(v):
    return lax.optimization_barrier(v.astype(jnp.bfloat16)).astype(jnp.float32)

@jax.custom_vjp
def low_back(v):
    return v

def low_keep(v):
    return (low(v), None)

def low_pass(kept, grad):
    return (grad,)

def back_keep(v):
    return (v, None)

def back_low(kept, grad):
    return (low(grad),)
low.defvjp(low_keep, low_pass)
low_back.defvjp(back_keep, back_low)
EPS = 1e-05
HIGH = lax.Precision.HIGHEST

def layer_norm(inputs, gain, shift):
    centre = inputs - lax.optimization_barrier(jnp.mean(inputs, axis=-1, keepdims=True))
    spread = lax.optimization_barrier(jnp.mean(centre * centre, axis=-1, keepdims=True))
    return centre * lax.rsqrt(spread + EPS) * gain + shift

def gelu_exact(inputs):
    return jax.nn.gelu(inputs, approximate=False)

def span_attention(blocks):
    queries, key_rows, values = blocks
    count = queries.shape[0]
    query_heads = queries.reshape(count, HEADS, HEAD)
    key_heads = key_rows.reshape(count, HEADS, HEAD)
    value_heads = values.reshape(count, HEADS, HEAD)
    scores = jnp.einsum('qhd,khd->hqk', query_heads, key_heads, precision=HIGH) * HEAD ** (-0.5)
    scores = low_back(scores)
    probabilities = jax.nn.softmax(scores, axis=-1)
    context = jnp.einsum('hqk,khd->qhd', low(probabilities), value_heads, precision=HIGH)
    return context.reshape(count, HEADS * HEAD)

def encoder_layer(params, inputs, live_slots):
    qkv_w, q_b, v_b, out_w, out_b, gain_one, shift_one, up_w, up_b, down_w, down_b, gain_two, shift_two = params
    flat_rows = inputs.reshape(-1, D)
    full_width = HEADS * HEAD
    queries = low(low_back(jnp.dot(flat_rows, qkv_w[:, 0], precision=HIGH) + q_b))
    key_rows = low(low_back(jnp.dot(flat_rows, qkv_w[:, 1], precision=HIGH)))
    values = low(low_back(jnp.dot(flat_rows, qkv_w[:, 2], precision=HIGH) + v_b))
    context = lax.map(jax.checkpoint(span_attention), (queries.reshape(-1, SPAN, full_width), key_rows.reshape(-1, SPAN, full_width), values.reshape(-1, SPAN, full_width)))
    context = low(low_back(context.reshape(-1, full_width)))
    group_cols = full_width // N_MP
    head_terms = jnp.einsum('rgc,dgc->grd', context.reshape(-1, N_MP, group_cols), out_w.reshape(D, N_MP, group_cols), precision=HIGH)
    attn_branch = low_back(lax.optimization_barrier(jnp.sum(low(head_terms), axis=0))) + out_b
    first = layer_norm(flat_rows + attn_branch, gain_one, shift_one)
    hidden = low_back(jnp.dot(low(first), up_w, precision=HIGH) + up_b)
    activated = low(gelu_exact(hidden))
    group_units = FF // N_MP
    unit_terms = jnp.einsum('rgf,dgf->grd', activated.reshape(-1, N_MP, group_units), down_w.reshape(D, N_MP, group_units), precision=HIGH)
    ffn_branch = low_back(lax.optimization_barrier(jnp.sum(low(unit_terms), axis=0))) + down_b
    result = layer_norm(first + ffn_branch, gain_two, shift_two)
    return result.reshape(inputs.shape) * live_slots[:, None, None]

def reference(states, span_count, qkv_weight, q_bias, v_bias, out_weight, out_bias, gain_one, shift_one, up_weight, up_bias, down_weight, down_bias, gain_two, shift_two, cotangent):
    params = tuple((item.astype(jnp.float32) for item in (qkv_weight, q_bias, v_bias, out_weight, out_bias, gain_one, shift_one, up_weight, up_bias, down_weight, down_bias, gain_two, shift_two)))
    grouped = states.astype(jnp.float32).reshape(GROUPS, SLOTS, SPAN, D)
    grouped_grad = cotangent.astype(jnp.float32).reshape(GROUPS, SLOTS, SPAN, D)

    def one_group(totals, item):
        inputs, upstream, count = item
        live_slots = (jnp.arange(SLOTS, dtype=jnp.int32) < count).astype(jnp.float32)
        result, pull = jax.vjp(lambda weights, data: encoder_layer(weights, data, live_slots), params, inputs)
        weight_grads, input_grad = pull(upstream)
        totals = jax.tree.map(jnp.add, totals, weight_grads)
        return (totals, (result.astype(jnp.bfloat16), input_grad.astype(jnp.bfloat16)))
    start = jax.tree.map(jnp.zeros_like, params)
    totals, (outputs, input_grads) = lax.scan(one_group, start, (grouped, grouped_grad, span_count))
    return (outputs.reshape(SPANS, SPAN, D), input_grads.reshape(SPANS, SPAN, D), totals[0], totals[1], totals[2], totals[3], totals[4], totals[5], totals[6], totals[7], totals[8], totals[9], totals[10], totals[11], totals[12])
```

```python
import jax
import jax.numpy as jnp
from jax import lax
from jax.sharding import PartitionSpec as P

HEAD = 64
EPS = 1e-05
F32 = jnp.float32
BF16 = jnp.bfloat16
CORE, ROW, SIDE = 1, 2, 4


def norm_forward(inputs):
    centre = inputs - jnp.mean(inputs, axis=-1, keepdims=True)
    spread = jnp.mean(centre * centre, axis=-1, keepdims=True)
    scale = lax.rsqrt(spread + EPS)
    return centre * scale, scale


def norm_backward(grad, normed, scale, gain):
    scaled = grad * gain
    mean_one = jnp.mean(scaled, axis=-1, keepdims=True)
    mean_two = jnp.mean(scaled * normed, axis=-1, keepdims=True)
    return scale * (scaled - mean_one - normed * mean_two)


def split_heads(matrix):
    return matrix.reshape(matrix.shape[0], matrix.shape[1] // HEAD, HEAD)


def attend_forward(rows, weight, q_bias, v_bias):
    projected = jnp.einsum("rd,dtc->trc", rows, weight, preferred_element_type=F32)
    queries = (projected[0] + q_bias).astype(BF16)
    key_rows = projected[1].astype(BF16)
    values = (projected[2] + v_bias).astype(BF16)
    scores = jnp.einsum("qhd,khd->hqk", split_heads(queries), split_heads(key_rows), preferred_element_type=F32) * HEAD**-0.5
    highest = jnp.max(scores, axis=-1, keepdims=True)
    raised = jnp.exp(scores - highest)
    totals = jnp.sum(raised, axis=-1, keepdims=True)
    probabilities = (raised / totals).astype(BF16)
    context = jnp.einsum("hqk,khd->qhd", probabilities, split_heads(values), preferred_element_type=F32)
    return queries, key_rows, values, context.reshape(queries.shape).astype(BF16), highest + jnp.log(totals)


def attend_backward(kept, context_grad):
    queries, key_rows, values, _, log_total = kept
    query_heads, key_heads, value_heads, grad_heads = map(split_heads, (queries, key_rows, values, context_grad))
    scores = jnp.einsum("qhd,khd->hqk", query_heads, key_heads, preferred_element_type=F32) * HEAD**-0.5
    probabilities = jnp.exp(scores - log_total)
    value_grad = jnp.einsum("hqk,qhd->khd", probabilities.astype(BF16), grad_heads, preferred_element_type=F32)
    prob_grad = jnp.einsum("qhd,khd->hqk", grad_heads, value_heads, preferred_element_type=F32)
    inner = jnp.sum(prob_grad * probabilities, axis=-1, keepdims=True)
    score_grad = (probabilities * (prob_grad - inner)).astype(BF16)
    query_grad = jnp.einsum("hqk,khd->qhd", score_grad, key_heads, preferred_element_type=F32) * HEAD**-0.5
    key_grad = jnp.einsum("hqk,qhd->khd", score_grad, query_heads, preferred_element_type=F32) * HEAD**-0.5
    return jnp.stack([g.reshape(queries.shape) for g in (query_grad, key_grad, value_grad)]).astype(BF16)


def build(mesh):
    n_dp, n_mp = mesh.shape["dp"], mesh.shape["mp"]
    dp_flips = []
    step = n_mp
    while step < n_dp * n_mp:
        dp_flips.append(step)
        step *= 2

    def flip(value, bit):
        pairs = [(i, i ^ bit) for i in range(n_dp * n_mp)]
        return lax.ppermute(value, ("dp", "mp"), pairs)

    def body(
        states, span_count, qkv_weight, q_bias, v_bias, out_weight, out_bias, gain_one, shift_one,
        up_weight, up_bias, down_weight, down_bias, gain_two, shift_two, cotangent,
    ):
        place = lax.axis_index("dp") * n_mp + lax.axis_index("mp")
        slot = (place // ROW) % 2
        core = place % 2

        def half(value, bit, mine):
            which = (place // bit) % 2
            which = which if mine else 1 - which
            size = value.shape[0] // 2
            return lax.dynamic_slice_in_dim(value, which * size, size, 0)

        def join(value, bit):
            other = flip(value, bit)
            first = (place // bit) % 2 == 0
            return jnp.concatenate([jnp.where(first, value, other), jnp.where(first, other, value)], axis=0)

        def total_dp(value):
            for bit in dp_flips:
                value = (half(value, bit, True).astype(F32) + flip(half(value, bit, False), bit).astype(F32)).astype(BF16)
            for bit in reversed(dp_flips):
                value = join(value, bit)
            return value

        def total_group(own, other):
            own = (own.astype(F32) + flip(other, ROW).astype(F32)).astype(BF16)
            return total_dp(own).astype(F32)

        def total_small(value):
            for bit in dp_flips:
                value = value + flip(value, bit)
            return value

        rows = lax.dynamic_index_in_dim(states, slot, 0, False)
        cot = lax.dynamic_index_in_dim(cotangent, slot, 0, False)
        live = (slot < span_count[0]).astype(F32)
        q_bias_o, v_bias_o, up_bias_o = jnp.split(flip(jnp.concatenate([q_bias, v_bias, up_bias]), ROW), [192, 384])
        qkv_o = flip(qkv_weight, ROW)
        out_o = flip(out_weight, ROW)
        up_o = flip(up_weight, ROW)
        down_o = flip(down_weight, ROW)

        kept = attend_forward(rows, qkv_weight, q_bias, v_bias)
        kept_o = attend_forward(rows, qkv_o, q_bias_o, v_bias_o)
        context = jnp.concatenate([kept[3], kept_o[3]], axis=1)
        out_both = jnp.concatenate([out_weight, out_o], axis=1)
        terms = jnp.einsum("rc,dc->rd", context, out_both, preferred_element_type=F32).astype(BF16)
        attn_branch = terms.astype(F32) + flip(terms, CORE).astype(F32) + out_bias
        normed_one, scale_one = norm_forward(rows.astype(F32) + attn_branch)
        first = normed_one * gain_one + shift_one
        first_low = first.astype(BF16)
        up_both = jnp.concatenate([up_weight, up_o], axis=1)
        down_both = jnp.concatenate([down_weight, down_o], axis=1)
        hidden = jnp.dot(first_low, up_both, preferred_element_type=F32) + jnp.concatenate([up_bias, up_bias_o])
        activated, gelu_pull = jax.vjp(lambda h: jax.nn.gelu(h, approximate=False), hidden)
        act_low = activated.astype(BF16)
        terms = jnp.einsum("rf,df->rd", act_low, down_both, preferred_element_type=F32).astype(BF16)
        ffn_branch = terms.astype(F32) + flip(terms, CORE).astype(F32) + down_bias
        normed_two, scale_two = norm_forward(first + ffn_branch)
        out_rows = ((normed_two * gain_two + shift_two) * live).astype(BF16)

        def share_rows(span):
            other = join(flip(half(span, CORE, True), ROW), CORE)
            lower = slot == 0
            return jnp.stack([jnp.where(lower, span, other), jnp.where(lower, other, span)])

        states_out = share_rows(out_rows)
        upstream = cot.astype(F32) * live
        gain_two_grad = jnp.sum(upstream * normed_two, axis=0)
        shift_two_grad = jnp.sum(upstream, axis=0)
        second_grad = norm_backward(upstream, normed_two, scale_two, gain_two)
        down_bias_grad = jnp.sum(second_grad, axis=0)
        branch_low = second_grad.astype(BF16)
        act_grad = jnp.dot(branch_low, down_both, preferred_element_type=F32)
        down_grad = jnp.einsum("rd,rf->df", branch_low, act_low, preferred_element_type=F32).astype(BF16)
        hidden_low = gelu_pull(act_grad)[0].astype(BF16)
        up_bias_both = jnp.sum(hidden_low.astype(F32), axis=0)
        up_grad = jnp.einsum("rd,rf->df", first_low, hidden_low, preferred_element_type=F32).astype(BF16)
        terms = jnp.einsum("rf,df->rd", hidden_low, up_both, preferred_element_type=F32).astype(BF16)
        first_grad = second_grad + (terms.astype(F32) + flip(terms, CORE).astype(F32))
        gain_one_grad = jnp.sum(first_grad * normed_one, axis=0)
        shift_one_grad = jnp.sum(first_grad, axis=0)
        entry_grad = norm_backward(first_grad, normed_one, scale_one, gain_one)
        out_bias_grad = jnp.sum(entry_grad, axis=0)
        attn_low = entry_grad.astype(BF16)
        context_grad = jnp.dot(attn_low, out_both, preferred_element_type=F32).astype(BF16)
        out_grad = jnp.einsum("rd,rc->dc", attn_low, context, preferred_element_type=F32).astype(BF16)
        proj = attend_backward(kept, context_grad[:, :192])
        proj_o = attend_backward(kept_o, context_grad[:, 192:])
        qkv_grad = jnp.einsum("rd,trc->dtc", rows, proj, preferred_element_type=F32).astype(BF16)
        qkv_grad_o = jnp.einsum("rd,trc->dtc", rows, proj_o, preferred_element_type=F32).astype(BF16)
        terms = jnp.einsum("trc,dtc->rd", proj, qkv_weight, preferred_element_type=F32)
        terms = (terms + jnp.einsum("trc,dtc->rd", proj_o, qkv_o, preferred_element_type=F32)).astype(BF16)
        in_rows = (entry_grad + (terms.astype(F32) + flip(terms, CORE).astype(F32))).astype(BF16)
        states_grad = share_rows(in_rows)

        ff = up_weight.shape[1]
        down_total = total_group(down_grad[:, :ff], down_grad[:, ff:])
        up_total = total_group(up_grad[:, :ff], up_grad[:, ff:])
        out_total = total_group(out_grad[:, :192], out_grad[:, 192:])
        qkv_total = total_group(qkv_grad, qkv_grad_o)
        common = [out_bias_grad, gain_one_grad, shift_one_grad, down_bias_grad, gain_two_grad, shift_two_grad]
        width = common[0].shape[0]
        bias = lambda p: [jnp.sum(p[0].astype(F32), axis=0), jnp.sum(p[2].astype(F32), axis=0)]
        mine = jnp.concatenate(common + [up_bias_both[:ff]] + bias(proj))
        theirs = jnp.concatenate(common + [up_bias_both[ff:]] + bias(proj_o))
        small = total_small(mine + flip(theirs, ROW))
        small = small.astype(BF16).astype(F32)
        parts = jnp.split(small, [width * i for i in range(1, 7)] + [6 * width + ff, 6 * width + ff + 192])
        return (
            states_out, states_grad, qkv_total, parts[7], parts[8], out_total, parts[0], parts[1], parts[2],
            up_total, parts[6], down_total, parts[3], parts[4], parts[5],
        )

    return body


def solution(mesh):
    split = P("dp", None, None)
    in_specs = (
        split, P("dp"), P(None, None, "mp"), P("mp"), P("mp"), P(None, "mp"), P(), P(), P(),
        P(None, "mp"), P("mp"), P(None, "mp"), P(), P(), P(), split,
    )
    out_specs = (
        split, split, P(None, None, "mp"), P("mp"), P("mp"), P(None, "mp"), P(), P(), P(),
        P(None, "mp"), P("mp"), P(None, "mp"), P(), P(), P(),
    )
    return jax.shard_map(build(mesh), mesh=mesh, in_specs=in_specs, out_specs=out_specs, check_vma=False)
```

```python
import jax
import jax.numpy as jnp
from jax import lax
from jax.experimental import pallas as pl
from jax.experimental.pallas import tpu as pltpu
from jax.sharding import PartitionSpec as P

HEAD = 64
EPS = 1e-05
F32 = jnp.float32
BF16 = jnp.bfloat16
LIMIT = 24 * 2**20
QBLOCK = 512
CORE, ROW, SIDE = 1, 2, 4


def dot(a, b, ca, cb):
    return lax.dot_general(a, b, (((ca,), (cb,)), ((), ())), preferred_element_type=F32)


def sds(shape, dtype):
    return jax.ShapeDtypeStruct(shape, dtype)


def whole(array):
    shape = array.shape
    return pl.BlockSpec(shape, lambda i, s: (0,) * len(shape))


def tiled(rows, cols):
    return pl.BlockSpec((rows, cols), lambda i, s: (i, 0))


def upper_rows(rows, cols, grid):
    return pl.BlockSpec((rows, cols), lambda i, s: (jnp.minimum(i, grid // 2 - 1), 0))


def lower_rows(rows, cols, grid):
    return pl.BlockSpec((rows, cols), lambda i, s: (jnp.maximum(i - grid // 2, 0), 0))


def block_of(array, which):
    return pl.BlockSpec((array.shape[0] // 2, array.shape[1]), lambda i, s: (which, 0))


def slot_rows(array, rows):
    return pl.BlockSpec((None, rows, array.shape[2]), lambda i, s: (s[0], i, 0))


def launch(kernel, info, args, in_specs, out_shapes, out_specs=None, grid=1, deps=(), scratch=(), limit=LIMIT):
    count, extra = len(args), len(deps)

    def inner(info_ref, *refs):
        kernel(info_ref, *refs[:count], *refs[count + extra :])

    specs = [whole(a) if s is None else s for a, s in zip(args, in_specs)]
    out_specs = [None] * len(out_shapes) if out_specs is None else out_specs
    return pl.pallas_call(
        inner,
        out_shape=out_shapes,
        grid_spec=pltpu.PrefetchScalarGridSpec(
            num_scalar_prefetch=1,
            grid=(grid,),
            in_specs=specs + [pl.BlockSpec(memory_space=pl.ANY)] * extra,
            out_specs=[whole(a) if s is None else s for a, s in zip(out_shapes, out_specs)],
            scratch_shapes=scratch,
        ),
        compiler_params=pltpu.CompilerParams(vmem_limit_bytes=limit),
        cost_estimate=pl.CostEstimate(flops=1, bytes_accessed=0, transcendentals=0),
    )(info, *args, *deps)


def norm_forward(inputs):
    centre = inputs - jnp.mean(inputs, axis=-1, keepdims=True)
    spread = jnp.mean(centre * centre, axis=-1, keepdims=True)
    scale = lax.rsqrt(spread + EPS)
    return centre * scale, scale


def norm_backward(grad, normed, scale, gain):
    scaled = grad * gain
    mean_one = jnp.mean(scaled, axis=-1, keepdims=True)
    mean_two = jnp.mean(scaled * normed, axis=-1, keepdims=True)
    return scale * (scaled - mean_one - normed * mean_two)


def column(row, width):
    return jnp.broadcast_to(row, (width, row.shape[1])).T[:, :1]


def wide(value):
    return value.astype(F32)


def attend_kernel(info, rows_ref, weight_ref, pack_ref, proj_ref, ctx_ref, log_ref):
    rows = rows_ref[...]
    cols = weight_ref.shape[0] // 3
    q_bias = column(pack_ref[7:8, :cols], 128)
    v_bias = column(pack_ref[7:8, cols : 2 * cols], 128)
    proj_ref[:cols] = (dot(weight_ref[:cols], rows, 1, 1) + q_bias).astype(BF16)
    proj_ref[cols : 2 * cols] = dot(weight_ref[cols : 2 * cols], rows, 1, 1).astype(BF16)
    proj_ref[2 * cols :] = (dot(weight_ref[2 * cols :], rows, 1, 1) + v_bias).astype(BF16)
    length = rows.shape[0]
    for head in range(cols // HEAD):
        lo = head * HEAD
        keys = proj_ref[cols + lo : cols + lo + HEAD]
        values = proj_ref[2 * cols + lo : 2 * cols + lo + HEAD]
        for block in range(length // QBLOCK):
            span = slice(block * QBLOCK, (block + 1) * QBLOCK)
            queries = proj_ref[lo : lo + HEAD, span] * BF16(HEAD**-0.5)
            scores = dot(keys, queries, 0, 0)
            highest = jnp.max(scores, axis=0, keepdims=True)
            raised = jnp.exp(scores - highest)
            totals = jnp.sum(raised, axis=0, keepdims=True)
            probs = (raised * (1.0 / totals)).astype(BF16)
            ctx_ref[lo : lo + HEAD, span] = dot(values, probs, 1, 0).astype(BF16)
            log_ref[head : head + 1, span] = highest + jnp.log(totals)


def attend(info, states, weight, pack, deps=()):
    length = states.shape[1]
    cols = weight.shape[0] // 3
    return launch(
        attend_kernel, info, [states, weight, pack], [slot_rows(states, length), None, None],
        [sds((3 * cols, length), BF16), sds((cols, length), BF16), sds((8, length), F32)], deps=deps,
    )


def project_kernel(info, left_ref, left_o_ref, right_ref, right_o_ref, upper_ref, lower_ref):
    half = upper_ref.shape[0]
    for part, into in enumerate((upper_ref, lower_ref)):
        span = slice(part * half, (part + 1) * half)
        terms = dot(left_ref[:, span], right_ref[...], 0, 0) + dot(left_o_ref[:, span], right_o_ref[...], 0, 0)
        into[...] = terms.astype(BF16)


def project(info, left, left_o, right, right_o, deps=()):
    shape = sds((left.shape[1] // 2, right.shape[1]), BF16)
    return launch(project_kernel, info, [left, left_o, right, right_o], [None] * 4, [shape, shape], deps=deps)


def pair(upper_ref, lower_ref):
    return wide(jnp.where(2 * pl.program_id(0) < pl.num_programs(0), upper_ref[...], lower_ref[...]))


def put_pair(value, upper_ref, lower_ref):
    first = 2 * pl.program_id(0) < pl.num_programs(0)

    @pl.when(first)
    def _():
        upper_ref[...] = value

    @pl.when(jnp.logical_not(first))
    def _():
        lower_ref[...] = value


def entry_rows(rows_ref, term_a, term_b, recv_a, recv_b, pack_ref):
    branch = pair(term_a, term_b) + pair(recv_a, recv_b) + pack_ref[0:1]
    return norm_forward(wide(rows_ref[...]) + branch)


def unit_pass(low, up_ref, pack_ref, down_ref, act_ref, slope_ref):
    total = None
    half = up_ref.shape[1] // 2
    for part in range(2):
        cols = slice(part * half, (part + 1) * half)
        hidden = dot(low, up_ref[:, cols], 1, 0) + pack_ref[6:7, cols]
        cdf = 0.5 + 0.5 * lax.erf(hidden * (0.5**0.5))
        pdf = jnp.exp(hidden * hidden * -0.5) * ((2 * jnp.pi) ** -0.5)
        act = (hidden * cdf).astype(BF16)
        act_ref[:, cols] = act
        slope_ref[:, cols] = (cdf + hidden * pdf).astype(BF16)
        term = dot(act, down_ref[:, cols], 1, 1)
        total = term if total is None else total + term
    return total


def feed_own_kernel(
    info, rows_ref, term_a, term_b, recv_a, recv_b, pack_ref, up_ref, down_ref,
    first_ref, low_ref, act_ref, slope_ref, part_ref,
):
    normed, _ = entry_rows(rows_ref, term_a, term_b, recv_a, recv_b, pack_ref)
    first = normed * pack_ref[1:2] + pack_ref[2:3]
    first_ref[...] = first
    low = first.astype(BF16)
    low_ref[...] = low
    part_ref[...] = unit_pass(low, up_ref, pack_ref, down_ref, act_ref, slope_ref)


def feed_own(info, states, terms, recv, pack, up, down, deps=()):
    _, length, width = states.shape
    half, units = length // 2, up.shape[1]
    return launch(
        feed_own_kernel, info, [states, *terms, *recv, pack, up, down],
        [slot_rows(states, half)] + [None] * 7,
        [sds((length, width), F32), sds((length, width), BF16), sds((length, units), BF16), sds((length, units), BF16), sds((length, width), F32)],
        [tiled(half, width), tiled(half, width), tiled(half, units), tiled(half, units), tiled(half, width)], grid=2, deps=deps,
    )


def feed_other_kernel(info, low_ref, part_ref, up_ref, pack_ref, down_ref, act_ref, slope_ref, upper_ref, lower_ref):
    total = part_ref[...] + unit_pass(low_ref[...], up_ref, pack_ref, down_ref, act_ref, slope_ref)
    put_pair(total.astype(BF16), upper_ref, lower_ref)


def feed_other(info, low, part, both, pack, deps=()):
    length, width = low.shape
    half, units = length // 2, both.shape[1]
    return launch(
        feed_other_kernel, info, [low, part, both, pack, both],
        [tiled(half, width), tiled(half, width), block_of(both, 0), None, block_of(both, 1)],
        [sds((length, units), BF16), sds((length, units), BF16), sds((half, width), BF16), sds((half, width), BF16)],
        [tiled(half, units), tiled(half, units), None, None], grid=2, deps=deps,
    )


def add_rows(ref, row, value):
    ref[row : row + 1, :] += jnp.sum(value, axis=0, keepdims=True)


def clear_first(ref):
    @pl.when(pl.program_id(0) == 0)
    def _():
        ref[...] = jnp.zeros_like(ref)


def turn_kernel(
    info, first_ref, term_a, term_b, recv_a, recv_b, cot_ref, pack_ref,
    out_ref, grad_ref, low_ref, sums_ref,
):
    live = jnp.where(info[0] < info[1], 1.0, 0.0).astype(F32)
    branch = pair(term_a, term_b) + pair(recv_a, recv_b) + pack_ref[3:4]
    normed, scale = norm_forward(first_ref[...] + branch)
    out_ref[...] = ((normed * pack_ref[4:5] + pack_ref[5:6]) * live).astype(BF16)
    upstream = wide(cot_ref[...]) * live
    grad = norm_backward(upstream, normed, scale, pack_ref[4:5])
    grad_ref[...] = grad
    low_ref[...] = grad.astype(BF16)
    clear_first(sums_ref)
    add_rows(sums_ref, 0, upstream * normed)
    add_rows(sums_ref, 1, upstream)
    add_rows(sums_ref, 2, grad)


def turn(info, first, terms, recv, cotangent, pack, deps=()):
    length, width = first.shape
    half = length // 2
    tile = tiled(half, width)
    return launch(
        turn_kernel, info, [first, *terms, *recv, cotangent, pack],
        [tile, None, None, None, None, slot_rows(cotangent, half), None],
        [sds((length, width), BF16), sds((length, width), F32), sds((length, width), BF16), sds((8, width), F32)],
        [tile, tile, tile, None], grid=2, deps=deps,
    )


def cross_kernel(info, left_ref, right_ref, right_o_ref, keep_ref, send_ref):
    side = info[2]
    half = keep_ref.shape[1]
    for which, ref in ((side, keep_ref), (1 - side, send_ref)):
        left = left_ref[:, pl.ds(pl.multiple_of(which * half, 128), half)]
        ref[0] = dot(left, right_ref[...], 0, 0).astype(BF16)
        ref[1] = dot(left, right_o_ref[...], 0, 0).astype(BF16)


def cross(info, left, right, right_o, deps=()):
    shape = sds((2, left.shape[1] // 2, right.shape[1]), BF16)
    return launch(cross_kernel, info, [left, right, right_o], [None] * 3, [shape, shape], deps=deps)


def plain_cross_kernel(info, left_ref, right_ref, right_o_ref, own_ref, other_ref):
    for right, into in ((right_ref, own_ref), (right_o_ref, other_ref)):
        into[...] = dot(left_ref[...], right[...], 0, 0).astype(BF16)


def plain_cross(info, left, right, right_o, deps=()):
    shape = sds((left.shape[1], right.shape[1]), BF16)
    return launch(plain_cross_kernel, info, [left, right, right_o], [None] * 3, [shape, shape], deps=deps)


def back_kernel(
    info, low_ref, slope_ref, slope_o_ref, up_ref, up_o_ref, down_ref, down_o_ref,
    hidden_ref, hidden_o_ref, upper_ref, lower_ref, sums_ref,
):
    low = low_ref[...]
    units = up_ref.shape[1]
    half = units // 2
    clear_first(sums_ref)
    total = None
    for which, (slope, up, down, into) in enumerate(
        ((slope_ref, up_ref, down_ref, hidden_ref), (slope_o_ref, up_o_ref, down_o_ref, hidden_o_ref))
    ):
        for part in range(2):
            cols = slice(part * half, (part + 1) * half)
            hidden = (wide(slope[:, cols]) * dot(low, down[:, cols], 1, 0)).astype(BF16)
            into[:, cols] = hidden
            sums_ref[0:1, which * units + part * half : which * units + (part + 1) * half] += jnp.sum(
                wide(hidden), axis=0, keepdims=True
            )
            term = dot(hidden, up[:, cols], 1, 1)
            total = term if total is None else total + term
    put_pair(total.astype(BF16), upper_ref, lower_ref)


def back(info, low, slope, slope_o, up, down, both, deps=()):
    length, width = low.shape
    units = slope.shape[1]
    half, tile, grid = length // 2, length // 4, 4
    return launch(
        back_kernel, info, [low, slope, slope_o, up, both, down, both],
        [tiled(tile, width), tiled(tile, units), tiled(tile, units), None, block_of(both, 0), None, block_of(both, 1)],
        [sds((length, units), BF16), sds((length, units), BF16), sds((half, width), BF16), sds((half, width), BF16), sds((8, 2 * units), F32)],
        [tiled(tile, units), tiled(tile, units), upper_rows(tile, width, grid), lower_rows(tile, width, grid), None], grid=grid, deps=deps,
    )


def entry_kernel(
    info, rows_ref, term_a, term_b, recv_a, recv_b, pack_ref, second_ref, back_a, back_b, got_a, got_b,
    entry_ref, low_ref, sums_ref,
):
    normed, scale = entry_rows(rows_ref, term_a, term_b, recv_a, recv_b, pack_ref)
    grad = second_ref[...] + (pair(back_a, back_b) + pair(got_a, got_b))
    entry = norm_backward(grad, normed, scale, pack_ref[1:2])
    entry_ref[...] = entry
    low_ref[...] = entry.astype(BF16)
    clear_first(sums_ref)
    add_rows(sums_ref, 0, entry)
    add_rows(sums_ref, 1, grad * normed)
    add_rows(sums_ref, 2, grad)


def entry(info, states, terms, recv, pack, second, back_terms, back_recv, deps=()):
    _, length, width = states.shape
    half = length // 2
    tile = tiled(half, width)
    return launch(
        entry_kernel, info, [states, *terms, *recv, pack, second, *back_terms, *back_recv],
        [slot_rows(states, half), None, None, None, None, None, tile, None, None, None, None],
        [sds((length, width), F32), sds((length, width), BF16), sds((8, width), F32)], [tile, tile, None], grid=2, deps=deps,
    )


def attend_back_kernel(info, rows_ref, proj_ref, ctx_ref, log_ref, low_ref, out_ref, grads_ref, dproj_ref, sums_ref, cgrad):
    length = rows_ref.shape[0]
    cols = ctx_ref.shape[0]
    low = low_ref[...]
    cgrad[...] = dot(out_ref[...], low, 1, 1).astype(BF16)
    scale = HEAD**-0.5
    for head in range(cols // HEAD):
        lo = head * HEAD
        key_rows = slice(cols + lo, cols + lo + HEAD)
        value_rows = slice(2 * cols + lo, 2 * cols + lo + HEAD)
        keys = proj_ref[key_rows]
        values = proj_ref[value_rows]
        key_total = None
        value_total = None
        for block in range(length // QBLOCK):
            span = slice(block * QBLOCK, (block + 1) * QBLOCK)
            queries = proj_ref[lo : lo + HEAD, span] * BF16(scale)
            upstream = cgrad[lo : lo + HEAD, span]
            scores = dot(keys, queries, 0, 0)
            probs = jnp.exp(scores - log_ref[head : head + 1, span])
            value_term = dot(upstream, probs.astype(BF16), 1, 1)
            prob_grad = dot(values, upstream, 0, 0)
            inner = jnp.sum(prob_grad * probs, axis=0, keepdims=True)
            score_grad = (probs * (prob_grad - inner)).astype(BF16)
            dproj_ref[lo : lo + HEAD, span] = (dot(keys, score_grad, 1, 0) * scale).astype(BF16)
            key_term = dot(queries, score_grad, 1, 1)
            key_total = key_term if key_total is None else key_total + key_term
            value_total = value_term if value_total is None else value_total + value_term
        dproj_ref[key_rows] = key_total.astype(BF16)
        dproj_ref[value_rows] = value_total.astype(BF16)
    rows = rows_ref[...]
    grads_ref[: 3 * cols] = dot(dproj_ref[...], rows, 1, 0).astype(BF16)
    grads_ref[3 * cols :] = dot(ctx_ref[...], low, 1, 0).astype(BF16)
    sums_ref[...] = dot(jnp.ones((8, length), BF16), dproj_ref[...], 1, 1)


def attend_back(info, states, proj, ctx, log_total, low, out, deps=()):
    _, length, width = states.shape
    cols = ctx.shape[0]
    return launch(
        attend_back_kernel, info, [states, proj, ctx, log_total, low, out], [slot_rows(states, length)] + [None] * 5,
        [sds((4 * cols, width), BF16), sds((3 * cols, length), BF16), sds((8, 3 * cols), F32)], deps=deps,
        scratch=[pltpu.VMEM((cols, length), BF16)],
    )


def build(mesh):
    n_dp, n_mp = mesh.shape["dp"], mesh.shape["mp"]
    n_z = n_dp // 2
    z_bits = []
    while n_mp * 2 << len(z_bits) < n_dp * n_mp:
        z_bits.append(n_mp * 2 << len(z_bits))

    def flip(value, bit):
        pairs = [(i, i ^ bit) for i in range(n_dp * n_mp)]
        return lax.ppermute(value, ("dp", "mp"), pairs)

    def swap(values):
        return [flip(v, CORE) for v in values]

    def body(
        states, span_count, qkv_weight, q_bias, v_bias, out_weight, out_bias, gain_one, shift_one,
        up_weight, up_bias, down_weight, down_bias, gain_two, shift_two, cotangent,
    ):
        dp, mp = lax.axis_index("dp"), lax.axis_index("mp")
        place = dp * n_mp + mp
        slot, core = mp // ROW, mp % ROW
        info = jnp.stack([slot, span_count[0], dp % 2, dp // 2]).astype(jnp.int32)
        width, _, cols = qkv_weight.shape
        units = up_weight.shape[1]

        def halves(value, bit):
            side = (place // bit) % 2
            rows = value.shape[0] // 2
            return tuple(lax.dynamic_slice_in_dim(value, w * rows, rows, 0) for w in (side, 1 - side))

        def add(one, two):
            return (wide(one) + wide(two)).astype(BF16)

        def join(value, bit):
            other = flip(value, bit)
            lower = (place // bit) % 2 == 0
            return jnp.concatenate([jnp.where(lower, value, other), jnp.where(lower, other, value)], axis=0)

        def fold(value, bit):
            mine, theirs = halves(value, bit)
            return add(mine, flip(theirs, bit))

        def total_z(value):
            for bit in z_bits:
                value = fold(value, bit)
            for bit in reversed(z_bits):
                value = join(value, bit)
            return wide(join(value, SIDE))

        def total_small(value):
            value = value + flip(value, SIDE)
            for bit in z_bits:
                value = value + flip(value, bit)
            return value

        joined = jnp.concatenate([q_bias, v_bias, jnp.zeros((width - 2 * cols,), F32)])
        pack = jnp.stack([out_bias, gain_one, shift_one, down_bias, gain_two, shift_two, up_bias, joined])
        qkv = qkv_weight.transpose(1, 2, 0).reshape(3 * cols, width)
        out = out_weight.T
        pack_o = flip(pack, ROW)
        qkv_o = flip(qkv, ROW)
        out_o = flip(out, ROW)

        proj, ctx, logs = attend(info, states, qkv, pack)
        up_send, down_send, qkv_o, pack_o, out_o, _ = lax.optimization_barrier((up_weight, down_weight, qkv_o, pack_o, out_o, logs))
        both_o = flip(jnp.concatenate([up_send, down_send], axis=0), ROW)
        proj_o, ctx_o, logs_o = attend(info, states, qkv_o, pack_o, deps=[logs])
        terms = project(info, ctx, ctx_o, out, out_o)
        recv = swap(terms)
        first, low, act, slope, part = feed_own(
            info, states, terms, recv, pack, up_weight, down_weight,
        )
        act_o, slope_o, *feed_terms = feed_other(info, low, part, both_o, pack_o)
        out_rows, second, branch_low, sums_two = turn(
            info, first, feed_terms, swap(feed_terms), cotangent, pack,
        )

        def half_rows(span):
            size = span.shape[0] // 2
            return lax.dynamic_slice_in_dim(span, core * size, size, 0)

        def both_spans(span, got):
            again = flip(got, CORE)
            other = jnp.concatenate([jnp.where(core == 0, got, again), jnp.where(core == 0, again, got)], axis=0)
            return jnp.stack([jnp.where(slot == 0, span, other), jnp.where(slot == 0, other, span)])

        out_got = flip(half_rows(out_rows), ROW)
        down_own, down_other = plain_cross(info, branch_low, act, act_o)
        down_recv = flip(down_other, ROW)
        hidden, hidden_o, *rest = back(info, branch_low, slope, slope_o, up_weight, down_weight, both_o, deps=[down_own])
        back_terms, unit_sums = rest[:2], rest[2]
        back_recv = swap(back_terms)
        up_keep, up_send = cross(info, low, hidden, hidden_o)
        up_recv = flip(up_send, SIDE)
        entry_grad, attn_low, sums_one = entry(
            info, states, terms, recv, pack, second, back_terms, back_recv, deps=[up_keep],
        )
        states_out = both_spans(out_rows, out_got)
        heads_other, dproj_o, head_sums_o = attend_back(
            info, states, proj_o, ctx_o, logs_o, attn_low, out_o,
        )
        heads_recv = flip(heads_other, ROW)
        down_sum = add(down_own, down_recv)
        heads_own, dproj, head_sums = attend_back(
            info, states, proj, ctx, logs, attn_low, out, deps=[down_sum, heads_other],
        )
        up_other = add(up_keep[1], up_recv[1])
        in_terms = project(info, dproj, dproj_o, qkv, qkv_o, deps=[up_other])
        in_recv = swap(in_terms)

        down_out = total_z(fold(down_sum, SIDE))
        up_out = total_z(add(add(up_keep[0], up_recv[0]), flip(up_other, ROW)))
        heads_out = total_z(fold(add(heads_own, heads_recv), SIDE))
        qkv_out, out_out = heads_out[: 3 * cols], heads_out[3 * cols :]

        in_rows = jnp.concatenate(
            [wide(a) + wide(b) for a, b in zip(in_terms, in_recv)], axis=0
        )
        in_rows = (entry_grad + in_rows).astype(BF16)
        states_grad = both_spans(in_rows, flip(half_rows(in_rows), ROW))

        common = [sums_one[0], sums_one[1], sums_one[2], sums_two[2], sums_two[0], sums_two[1]]
        pick = lambda s: [s[0, :cols], s[0, 2 * cols :]]
        mine = jnp.concatenate(common + [unit_sums[0, :units]] + pick(head_sums))
        theirs = jnp.concatenate(common + [unit_sums[0, units:]] + pick(head_sums_o))
        small = total_small(mine + flip(theirs, ROW))
        small = wide(small.astype(BF16))
        parts = jnp.split(small, [width * i for i in range(1, 7)] + [6 * width + units, 6 * width + units + cols])
        qkv_out = qkv_out.reshape(3, cols, width).transpose(2, 0, 1)
        return (
            states_out, states_grad, qkv_out, parts[7], parts[8], out_out.T, parts[0], parts[1], parts[2],
            up_out, parts[6], down_out, parts[3], parts[4], parts[5],
        )

    return body


def solution(mesh):
    split = P("dp", None, None)
    in_specs = (
        split, P("dp"), P(None, None, "mp"), P("mp"), P("mp"), P(None, "mp"), P(), P(), P(),
        P(None, "mp"), P("mp"), P(None, "mp"), P(), P(), P(), split,
    )
    out_specs = (
        split, split, P(None, None, "mp"), P("mp"), P("mp"), P(None, "mp"), P(), P(), P(),
        P(None, "mp"), P("mp"), P(None, "mp"), P(), P(), P(),
    )
    return jax.shard_map(build(mesh), mesh=mesh, in_specs=in_specs, out_specs=out_specs, check_vma=False)
```

```python
import jax
import jax.numpy as jnp
from jax import lax
from jax.experimental import pallas as pl
from jax.experimental.pallas import tpu as pltpu
from jax.sharding import PartitionSpec as P

HEAD = 64
EPS = 1e-05
F32 = jnp.float32
BF16 = jnp.bfloat16
LIMIT = 24 * 2**20
QBLOCK = 512
CORE, ROW, SIDE = 1, 2, 4


def dot(a, b, ca, cb):
    return lax.dot_general(a, b, (((ca,), (cb,)), ((), ())), preferred_element_type=F32)


def sds(shape, dtype):
    return jax.ShapeDtypeStruct(shape, dtype)


def whole(array):
    shape = array.shape
    return pl.BlockSpec(shape, lambda i, s: (0,) * len(shape))


def tiled(rows, cols):
    return pl.BlockSpec((rows, cols), lambda i, s: (i, 0))


def slot_rows(array, rows):
    return pl.BlockSpec((None, rows, array.shape[2]), lambda i, s: (s[0], i, 0))


def launch(kernel, info, args, in_specs, out_shapes, out_specs=None, grid=1, deps=(), scratch=(), limit=LIMIT):
    count, extra = len(args), len(deps)

    def inner(info_ref, *refs):
        kernel(info_ref, *refs[:count], *refs[count + extra :])

    specs = [whole(a) if s is None else s for a, s in zip(args, in_specs)]
    out_specs = [None] * len(out_shapes) if out_specs is None else out_specs
    return pl.pallas_call(
        inner,
        out_shape=out_shapes,
        grid_spec=pltpu.PrefetchScalarGridSpec(
            num_scalar_prefetch=1,
            grid=(grid,),
            in_specs=specs + [pl.BlockSpec(memory_space=pl.ANY)] * extra,
            out_specs=[whole(a) if s is None else s for a, s in zip(out_shapes, out_specs)],
            scratch_shapes=scratch,
        ),
        compiler_params=pltpu.CompilerParams(vmem_limit_bytes=limit),
        cost_estimate=pl.CostEstimate(flops=1, bytes_accessed=0, transcendentals=0),
    )(info, *args, *deps)


def norm_forward(inputs):
    centre = inputs - jnp.mean(inputs, axis=-1, keepdims=True)
    spread = jnp.mean(centre * centre, axis=-1, keepdims=True)
    scale = lax.rsqrt(spread + EPS)
    return centre * scale, scale


def norm_backward(grad, normed, scale, gain):
    scaled = grad * gain
    mean_one = jnp.mean(scaled, axis=-1, keepdims=True)
    mean_two = jnp.mean(scaled * normed, axis=-1, keepdims=True)
    return scale * (scaled - mean_one - normed * mean_two)


def column(row, width):
    return jnp.broadcast_to(row, (width, row.shape[1])).T[:, :1]


def wide(value):
    return value.astype(F32)


def attend_kernel(info, rows_ref, weight_ref, pack_ref, proj_ref, ctx_ref, log_ref):
    rows = rows_ref[...]
    cols = weight_ref.shape[0] // 3
    q_bias = column(pack_ref[7:8, :cols], 128)
    v_bias = column(pack_ref[7:8, cols : 2 * cols], 128)
    proj_ref[:cols] = (dot(weight_ref[:cols], rows, 1, 1) + q_bias).astype(BF16)
    proj_ref[cols : 2 * cols] = dot(weight_ref[cols : 2 * cols], rows, 1, 1).astype(BF16)
    proj_ref[2 * cols :] = (dot(weight_ref[2 * cols :], rows, 1, 1) + v_bias).astype(BF16)
    length = rows.shape[0]

    @pl.loop(0, cols // HEAD)
    def _(head):
        rows_of = lambda base: pl.ds(pl.multiple_of(base + head * HEAD, HEAD), HEAD)
        keys = proj_ref[rows_of(cols)]
        values = proj_ref[rows_of(2 * cols)]
        for block in range(length // QBLOCK):
            span = slice(block * QBLOCK, (block + 1) * QBLOCK)
            queries = proj_ref[rows_of(0), span] * BF16(HEAD**-0.5)
            scores = dot(keys, queries, 0, 0)
            highest = jnp.max(scores, axis=0, keepdims=True)
            raised = jnp.exp(scores - highest)
            totals = jnp.sum(raised, axis=0, keepdims=True)
            probs = (raised * (1.0 / totals)).astype(BF16)
            ctx_ref[rows_of(0), span] = dot(values, probs, 1, 0).astype(BF16)
            log_ref[pl.ds(head, 1), span] = highest + jnp.log(totals)


def attend(info, states, weight, pack, deps=()):
    length = states.shape[1]
    cols = weight.shape[0] // 3
    return launch(
        attend_kernel, info, [states, weight, pack], [slot_rows(states, length), None, None],
        [kept((3 * cols, length), BF16), sds((cols, length), BF16), sds((8, length), F32)], deps=deps,
    )


def project_kernel(info, left_ref, left_o_ref, right_ref, right_o_ref, *out_refs):
    size = out_refs[0].shape[0]
    for part, into in enumerate(out_refs):
        span = slice(part * size, (part + 1) * size)
        terms = dot(left_ref[:, span], right_ref[...], 0, 0) + dot(left_o_ref[:, span], right_o_ref[...], 0, 0)
        into[...] = terms.astype(BF16)


def project(info, left, left_o, right, right_o, count, deps=()):
    return launch(
        project_kernel, info, [left, left_o, right, right_o], [None] * 4, chunks(left.shape[1], right.shape[1], count), deps=deps,
    )


def read(refs, steps):
    per = len(refs) // steps
    step = pl.program_id(0)
    parts = []
    for t in range(per):
        value = refs[t][...]
        for k in range(1, steps):
            value = jnp.where(step == k, refs[k * per + t][...], value)
        parts.append(value)
    return wide(jnp.concatenate(parts, axis=0) if per > 1 else parts[0])


def write(refs, steps, value):
    per, rows = max(len(refs) // steps, 1), value.shape[0]
    for k in range(steps):

        @pl.when(pl.program_id(0) == k)
        def _():
            if len(refs) < steps:
                at = k % (steps // len(refs)) * rows
                refs[k * len(refs) // steps][at : at + rows] = value
            else:
                for t in range(per):
                    refs[k * per + t][...] = value[t * rows // per : (t + 1) * rows // per]


def chunks(length, width, count):
    return [sds((length // count, width), BF16)] * count


def kept(shape, dtype):
    return pltpu.HBM(shape, dtype)


def unit_pass(low, up_ref, pack_ref, down_ref, act_ref, slope_ref):
    total = None
    half = up_ref.shape[1] // 2
    for part in range(2):
        cols = slice(part * half, (part + 1) * half)
        hidden = dot(low, up_ref[:, cols], 1, 0) + pack_ref[6:7, cols]
        cdf = 0.5 + 0.5 * lax.erf(hidden * (0.5**0.5))
        pdf = jnp.exp(hidden * hidden * -0.5) * ((2 * jnp.pi) ** -0.5)
        act = (hidden * cdf).astype(BF16)
        act_ref[:, cols] = act
        slope_ref[:, cols] = (cdf + hidden * pdf).astype(BF16)
        term = dot(act, down_ref[:, cols], 1, 1)
        total = term if total is None else total + term
    return total


def feed_own_kernel(info, rows_ref, pack_ref, up_ref, down_ref, *refs):
    first_ref, low_ref, act_ref, slope_ref, part_ref, entry_ref = refs[-6:]
    count = (len(refs) - 6) // 2
    inputs = wide(rows_ref[...]) + (read(refs[:count], 4) + read(refs[count : 2 * count], 4) + pack_ref[0:1])
    entry_ref[...] = inputs
    normed, _ = norm_forward(inputs)
    first = normed * pack_ref[1:2] + pack_ref[2:3]
    first_ref[...] = first
    low = first.astype(BF16)
    low_ref[...] = low
    part_ref[...] = unit_pass(low, up_ref, pack_ref, down_ref, act_ref, slope_ref)


def feed_own(info, states, terms, recv, pack, up, down, deps=()):
    _, length, width = states.shape
    half, units = length // 4, up.shape[1]
    return launch(
        feed_own_kernel, info, [states, pack, up, down, *terms, *recv],
        [slot_rows(states, half)] + [None] * (3 + 2 * len(terms)),
        [sds((length, width), F32), sds((length, width), BF16), sds((length, units), BF16), sds((length, units), BF16), sds((length, width), F32), kept((length, width), F32)],
        [tiled(half, width), tiled(half, width), tiled(half, units), tiled(half, units), tiled(half, width), tiled(half, width)], grid=4, deps=deps,
    )


def places(info, size):
    return [pl.multiple_of(2 * size * info[2], 128), size, pl.multiple_of(2 * size * (1 - info[2]), 128)]


def feed_other_kernel(info, low_ref, part_ref, pack_ref, *refs):
    act_ref, slope_ref = refs[3:5]
    low = low_ref[...]
    total = part_ref[...]
    size = refs[0].shape[1]
    width = low.shape[1]
    for ref, place in zip(refs[:3], places(info, size)):
        cols = pl.ds(place, size)
        hidden = dot(low, ref[:width], 1, 0) + pack_ref[6:7, cols]
        cdf = 0.5 + 0.5 * lax.erf(hidden * (0.5**0.5))
        pdf = jnp.exp(hidden * hidden * -0.5) * ((2 * jnp.pi) ** -0.5)
        act = (hidden * cdf).astype(BF16)
        act_ref[:, cols] = act
        slope_ref[:, cols] = (cdf + hidden * pdf).astype(BF16)
        total = total + dot(act, ref[width:], 1, 1)
    write(refs[5:], 4, total.astype(BF16))


def feed_other(info, low, part, pieces, pack, deps=()):
    length, width = low.shape
    half, units = length // 4, 3 * pieces[0].shape[1]
    return launch(
        feed_other_kernel, info, [low, part, pack, *pieces],
        [tiled(half, width), tiled(half, width), None, None, None, None],
        [sds((length, units), BF16), sds((length, units), BF16)] + chunks(length, width, 2),
        [tiled(half, units), tiled(half, units), None, None], grid=4, deps=deps,
    )


def add_rows(ref, row, value):
    ref[row : row + 1, :] += jnp.sum(value, axis=0, keepdims=True)


def clear_first(ref):
    @pl.when(pl.program_id(0) == 0)
    def _():
        ref[...] = jnp.zeros_like(ref)


def turn_kernel(info, first_ref, *refs):
    terms, recv = refs[:2], refs[2:4]
    cot_ref, pack_ref, out_ref, grad_ref, low_ref, sums_ref = refs[4:]
    live = jnp.where(info[0] < info[1], 1.0, 0.0).astype(F32)
    branch = read(terms, 2) + read(recv, 2) + pack_ref[3:4]
    normed, scale = norm_forward(first_ref[...] + branch)
    out_ref[...] = ((normed * pack_ref[4:5] + pack_ref[5:6]) * live).astype(BF16)
    upstream = wide(cot_ref[...]) * live
    grad = norm_backward(upstream, normed, scale, pack_ref[4:5])
    grad_ref[...] = grad
    low_ref[...] = grad.astype(BF16)
    clear_first(sums_ref)
    add_rows(sums_ref, 0, upstream * normed)
    add_rows(sums_ref, 1, upstream)
    add_rows(sums_ref, 2, grad)


def turn(info, first, terms, recv, cotangent, pack, deps=()):
    length, width = first.shape
    half = length // 2
    tile = tiled(half, width)
    return launch(
        turn_kernel, info, [first, *terms, *recv, cotangent, pack],
        [tile] + [None] * 4 + [slot_rows(cotangent, half), None],
        [kept((length, width), BF16), kept((length, width), F32), sds((length, width), BF16), sds((8, width), F32)],
        [tile, tile, tile, None], grid=2, deps=deps,
    )


def cross_kernel(info, left_ref, right_ref, right_o_ref, keep_ref, send_ref):
    side = info[2]
    half = keep_ref.shape[1]
    for which, ref in ((side, keep_ref), (1 - side, send_ref)):
        left = left_ref[:, pl.ds(pl.multiple_of(which * half, 128), half)]
        ref[0] = dot(left, right_ref[...], 0, 0).astype(BF16)
        ref[1] = dot(left, right_o_ref[...], 0, 0).astype(BF16)


def cross(info, left, right, right_o, deps=()):
    shape = sds((2, left.shape[1] // 2, right.shape[1]), BF16)
    return launch(cross_kernel, info, [left, right, right_o], [None] * 3, [shape, shape], deps=deps)


def plain_cross_kernel(info, left_ref, right_ref, right_o_ref, own_ref, other_ref, sums_ref, sums_o_ref):
    ones = jnp.ones((8, right_ref.shape[0]), BF16)
    for right, into, sums in ((right_ref, own_ref, sums_ref), (right_o_ref, other_ref, sums_o_ref)):
        into[...] = dot(left_ref[...], right[...], 0, 0).astype(BF16)
        sums[...] = dot(ones, right[...], 1, 0)


def plain_cross(info, left, right, right_o, deps=()):
    shape = sds((left.shape[1], right.shape[1]), BF16)
    sums = sds((8, right.shape[1]), F32)
    return launch(plain_cross_kernel, info, [left, right, right_o], [None] * 3, [shape, shape, sums, sums], deps=deps)


def back_own_kernel(info, low_ref, slope_ref, up_ref, down_ref, hidden_ref, part_ref):
    low = low_ref[...]
    half = up_ref.shape[1] // 2
    total = None
    for part in range(2):
        cols = slice(part * half, (part + 1) * half)
        hidden = (wide(slope_ref[:, cols]) * dot(low, down_ref[:, cols], 1, 0)).astype(BF16)
        hidden_ref[:, cols] = hidden
        term = dot(hidden, up_ref[:, cols], 1, 1)
        total = term if total is None else total + term
    part_ref[...] = total


def back_own(info, low, slope, up, down, deps=()):
    length, width = low.shape
    half, units = length // 4, slope.shape[1]
    return launch(
        back_own_kernel, info, [low, slope, up, down], [tiled(half, width), tiled(half, units), None, None],
        [sds((length, units), BF16), sds((length, width), F32)], [tiled(half, units), tiled(half, width)], grid=4, deps=deps,
    )


def back_other_kernel(info, low_ref, slope_ref, part_ref, *refs):
    hidden_ref = refs[3]
    low = low_ref[...]
    width = low.shape[1]
    size = refs[0].shape[1]
    total = part_ref[...]
    for ref, place in zip(refs[:3], places(info, size)):
        cols = pl.ds(place, size)
        hidden = (wide(slope_ref[:, cols]) * dot(low, ref[width:], 1, 0)).astype(BF16)
        hidden_ref[:, cols] = hidden
        total = total + dot(hidden, ref[:width], 1, 1)
    write(refs[4:], 4, total.astype(BF16))


def back_other(info, low, slope, part, pieces, deps=()):
    length, width = low.shape
    half, units = length // 4, slope.shape[1]
    return launch(
        back_other_kernel, info, [low, slope, part, *pieces],
        [tiled(half, width), tiled(half, units), tiled(half, width), None, None, None],
        [sds((length, units), BF16)] + chunks(length, width, 2), [tiled(half, units), None, None], grid=4, deps=deps,
    )


def entry_kernel(info, inputs_ref, second_ref, pack_ref, term_a, term_b, recv_a, recv_b, entry_ref, low_ref, sums_ref):
    normed, scale = norm_forward(inputs_ref[...])
    grad = second_ref[...] + (read([term_a, term_b], 2) + read([recv_a, recv_b], 2))
    entry = norm_backward(grad, normed, scale, pack_ref[1:2])
    entry_ref[...] = entry
    low_ref[...] = entry.astype(BF16)
    clear_first(sums_ref)
    add_rows(sums_ref, 0, entry)
    add_rows(sums_ref, 1, grad * normed)
    add_rows(sums_ref, 2, grad)


def entry(info, inputs, second, pack, back_terms, back_recv, deps=()):
    length, width = inputs.shape
    tile = tiled(length // 2, width)
    return launch(
        entry_kernel, info, [inputs, second, pack, *back_terms, *back_recv], [tile, tile] + [None] * 5,
        [kept((length, width), F32), sds((length, width), BF16), sds((8, width), F32)], [tile, tile, None], grid=2, deps=deps,
    )


def attend_back_kernel(info, rows_ref, proj_ref, ctx_ref, log_ref, low_ref, out_ref, grads_ref, dproj_ref, sums_ref, cgrad):
    length = rows_ref.shape[0]
    cols = ctx_ref.shape[0]
    low = low_ref[...]
    cgrad[...] = dot(out_ref[...], low, 1, 1).astype(BF16)
    scale = HEAD**-0.5

    @pl.loop(0, cols // HEAD)
    def _(head):
        query_rows, key_rows, value_rows = (pl.ds(pl.multiple_of(k * cols + head * HEAD, HEAD), HEAD) for k in range(3))
        keys = proj_ref[key_rows]
        values = proj_ref[value_rows]
        key_total = None
        value_total = None
        for block in range(length // QBLOCK):
            span = slice(block * QBLOCK, (block + 1) * QBLOCK)
            queries = proj_ref[query_rows, span] * BF16(scale)
            upstream = cgrad[query_rows, span]
            scores = dot(keys, queries, 0, 0)
            probs = jnp.exp(scores - log_ref[pl.ds(head, 1), span])
            value_term = dot(upstream, probs.astype(BF16), 1, 1)
            prob_grad = dot(values, upstream, 0, 0)
            inner = jnp.sum(prob_grad * probs, axis=0, keepdims=True)
            score_grad = (probs * (prob_grad - inner)).astype(BF16)
            dproj_ref[query_rows, span] = (dot(keys, score_grad, 1, 0) * scale).astype(BF16)
            key_term = dot(queries, score_grad, 1, 1)
            key_total = key_term if key_total is None else key_total + key_term
            value_total = value_term if value_total is None else value_total + value_term
        dproj_ref[key_rows] = key_total.astype(BF16)
        dproj_ref[value_rows] = value_total.astype(BF16)
    rows = rows_ref[...]
    grads_ref[: 3 * cols] = dot(dproj_ref[...], rows, 1, 0).astype(BF16)
    grads_ref[3 * cols :] = dot(ctx_ref[...], low, 1, 0).astype(BF16)
    sums_ref[...] = dot(jnp.ones((8, length), BF16), dproj_ref[...], 1, 1)


def attend_back(info, states, proj, ctx, log_total, low, out, deps=()):
    _, length, width = states.shape
    cols = ctx.shape[0]
    return launch(
        attend_back_kernel, info, [states, proj, ctx, log_total, low, out], [slot_rows(states, length)] + [None] * 5,
        [sds((4 * cols, width), BF16), sds((3 * cols, length), BF16), sds((8, 3 * cols), F32)], deps=deps,
        scratch=[pltpu.VMEM((cols, length), BF16)],
    )


def attend_back_heads(info, proj, log_total, low, out, first, last, deps=()):
    cols, length = proj.shape[0] // 3, proj.shape[1]
    scale = HEAD**-0.5

    def kernel(info, proj_ref, log_ref, low_ref, out_ref, dproj_ref):
        @pl.loop(0, last - first)
        def _(step):
            head = step + first
            at = lambda k: pl.ds(pl.multiple_of(k * cols + head * HEAD, HEAD), HEAD)
            into = lambda k: pl.ds(pl.multiple_of((3 * step + k) * HEAD, HEAD), HEAD)
            upstream_all = dot(out_ref[at(0)], low_ref[...], 1, 1).astype(BF16)
            keys, values = proj_ref[at(1)], proj_ref[at(2)]
            key_total = None
            value_total = None
            for block in range(length // QBLOCK):
                span = slice(block * QBLOCK, (block + 1) * QBLOCK)
                queries = proj_ref[at(0), span] * BF16(scale)
                upstream = upstream_all[:, span]
                scores = dot(keys, queries, 0, 0)
                probs = jnp.exp(scores - log_ref[pl.ds(head, 1), span])
                value_term = dot(upstream, probs.astype(BF16), 1, 1)
                prob_grad = dot(values, upstream, 0, 0)
                inner = jnp.sum(prob_grad * probs, axis=0, keepdims=True)
                score_grad = (probs * (prob_grad - inner)).astype(BF16)
                dproj_ref[into(0), span] = (dot(keys, score_grad, 1, 0) * scale).astype(BF16)
                key_term = dot(queries, score_grad, 1, 1)
                key_total = key_term if key_total is None else key_total + key_term
                value_total = value_term if value_total is None else value_total + value_term
            dproj_ref[into(1)] = key_total.astype(BF16)
            dproj_ref[into(2)] = value_total.astype(BF16)

    return launch(
        kernel, info, [proj, log_total, low, out], [None] * 4, [sds((3 * HEAD * (last - first), length), BF16)], deps=deps,
    )[0]


def heads_kernel(info, rows_ref, ctx_ref, low_ref, *refs):
    grads_ref, dproj_ref, sums_ref = refs[-3:]
    cols = ctx_ref.shape[0]
    head = 0
    for ref in refs[:-3]:
        for step in range(ref.shape[0] // (3 * HEAD)):
            for k in range(3):
                at = (3 * step + k) * HEAD
                dproj_ref[k * cols + head * HEAD : k * cols + (head + 1) * HEAD, :] = ref[at : at + HEAD, :]
            head += 1
    grads_ref[: 3 * cols] = dot(dproj_ref[...], rows_ref[...], 1, 0).astype(BF16)
    grads_ref[3 * cols :] = dot(ctx_ref[...], low_ref[...], 1, 0).astype(BF16)
    sums_ref[...] = dot(jnp.ones((8, dproj_ref.shape[1]), BF16), dproj_ref[...], 1, 1)


def gather_heads(info, states, ctx, low, dprojs, deps=()):
    _, length, width = states.shape
    cols = ctx.shape[0]
    return launch(
        heads_kernel, info, [states, ctx, low, *dprojs], [slot_rows(states, length)] + [None] * (2 + len(dprojs)),
        [sds((4 * cols, width), BF16), sds((3 * cols, length), BF16), sds((8, 3 * cols), F32)], deps=deps,
    )


def build(mesh):
    n_dp, n_mp = mesh.shape["dp"], mesh.shape["mp"]
    n_z = n_dp // 2
    z_bits = []
    while n_mp * 2 << len(z_bits) < n_dp * n_mp:
        z_bits.append(n_mp * 2 << len(z_bits))

    def flip(value, bit):
        pairs = [(i, i ^ bit) for i in range(n_dp * n_mp)]
        return lax.ppermute(value, ("dp", "mp"), pairs)

    def swap(values):
        return [flip(v, CORE) for v in values]

    def body(
        states, span_count, qkv_weight, q_bias, v_bias, out_weight, out_bias, gain_one, shift_one,
        up_weight, up_bias, down_weight, down_bias, gain_two, shift_two, cotangent,
    ):
        dp, mp = lax.axis_index("dp"), lax.axis_index("mp")
        place = dp * n_mp + mp
        slot, core = mp // ROW, mp % ROW
        info = jnp.stack([slot, span_count[0], dp % 2, dp // 2]).astype(jnp.int32)
        width, _, cols = qkv_weight.shape
        units = up_weight.shape[1]

        token = [place]

        def halves(value, bit):
            side = (token[0] // bit) % 2
            rows = value.shape[0] // 2
            return tuple(lax.dynamic_slice_in_dim(value, w * rows, rows, 0) for w in (side, 1 - side))

        def add(one, two):
            return (wide(one) + wide(two)).astype(BF16)

        def join(value, bit):
            other = flip(value, bit)
            lower = (token[0] // bit) % 2 == 0
            return jnp.concatenate([jnp.where(lower, value, other), jnp.where(lower, other, value)], axis=0)

        def sync(*values):
            token[0], values = lax.optimization_barrier((token[0], values))
            return values

        def put_together(value, other, bit):
            lower = (token[0] // bit) % 2 == 0
            return jnp.concatenate([jnp.where(lower, value, other), jnp.where(lower, other, value)], axis=0)

        z_near, z_far = n_mp * 2, n_mp * 4

        def z_one(value):
            if n_z == 4:
                mine, theirs = halves(value, z_near)
                return mine, flip(theirs, z_near)
            for bit in z_bits:
                value = add(value, flip(value, bit))
            return value, value

        def z_two(pair):
            if n_z != 4:
                return pair
            value = add(*pair)
            return value, flip(value, z_far)

        def z_three(pair):
            if n_z != 4:
                return pair
            value = add(*pair)
            return value, flip(value, z_near)

        def z_end(pair):
            return put_together(*pair, z_near) if n_z == 4 else pair[0]

        def side_start(value):
            return value, flip(value, SIDE)

        joined = jnp.concatenate([q_bias, v_bias, jnp.zeros((width - 2 * cols,), F32)])
        pack = jnp.stack([out_bias, gain_one, shift_one, down_bias, gain_two, shift_two, up_bias, joined])
        qkv = qkv_weight.transpose(1, 2, 0).reshape(3 * cols, width)
        out = out_weight.T
        pack_o = flip(pack, ROW)
        qkv_o = flip(qkv, ROW)
        out_o = flip(out, ROW)

        proj, ctx, logs = attend(info, states, qkv, pack)
        third = units // 3
        side = dp % 2
        up_send, down_send, qkv_o, pack_o, out_o, _ = lax.optimization_barrier((up_weight, down_weight, qkv_o, pack_o, out_o, logs))
        cut = lambda w, at: lax.dynamic_slice_in_dim(w, at, third, 1)
        outer = flip(jnp.concatenate([cut(up_send, 2 * third * side), cut(down_send, 2 * third * side)], axis=0), ROW)
        proj_o, ctx_o, logs_o = attend(info, states, qkv_o, pack_o, deps=[logs])
        up_send, down_send, ctx_o = lax.optimization_barrier((up_weight, down_weight, ctx_o))
        middle = flip(jnp.concatenate([up_send[:, third : 2 * third], down_send[:, third : 2 * third]], axis=0), ROW)
        terms = project(info, ctx, ctx_o, out, out_o, 4)
        recv = swap(terms)
        first, low, act, slope, part, entry_in = feed_own(
            info, states, terms, recv, pack, up_weight, down_weight,
        )
        outer, low = lax.optimization_barrier((outer, low))
        pieces = [outer, middle, flip(outer, SIDE)]
        act_o, slope_o, *feed_terms = feed_other(info, low, part, pieces, pack_o)
        out_rows, second, branch_low, sums_two = turn(
            info, first, feed_terms, swap(feed_terms), cotangent, pack,
        )

        def half_rows(span):
            size = span.shape[0] // 2
            return lax.dynamic_slice_in_dim(span, core * size, size, 0)

        def both_spans(span, got, again):
            other = put_together(got, again, CORE)
            return put_together(span[None], other[None], ROW)

        fence = lambda *v: lax.optimization_barrier(v)
        down_keep, down_send = cross(info, branch_low, act, act_o)
        down_recv = flip(down_send, SIDE)
        hidden, back_part = back_own(info, branch_low, slope, up_weight, down_weight, deps=[down_keep])
        hidden_o, *back_terms = back_other(info, branch_low, slope_o, back_part, pieces)
        back_recv = swap(back_terms)
        up_own, up_other, unit_sums, unit_sums_o = plain_cross(info, low, hidden, hidden_o)
        up_recv = flip(up_other, ROW)
        entry_grad, attn_low, sums_one = entry(info, pltpu.with_memory_space_constraint(entry_in, pltpu.HBM), pltpu.with_memory_space_constraint(second, pltpu.HBM), pack, back_terms, back_recv, deps=[up_own, down_recv])

        attn_low, down_keep, down_recv = sync(attn_low, down_keep, down_recv)
        down_own, down_other = (add(down_keep[k], down_recv[k]) for k in range(2))
        down = down_own, flip(down_other, ROW)
        heads_other, dproj_o, head_sums_o = attend_back(
            info, states, proj_o, ctx_o, logs_o, attn_low, out_o, deps=[down_other],
        )

        heads_other, up_own, up_recv, attn_low = sync(heads_other, up_own, up_recv, attn_low)
        heads_recv = flip(heads_other, ROW)
        up_keep, up_send = halves(add(up_own, up_recv), SIDE)
        up = up_keep, flip(up_send, SIDE)
        dprojs = [attend_back_heads(info, proj, logs, attn_low, out, 0, 1, deps=[up_send, heads_other])]

        dprojs, down, attn_low = sync(dprojs, down, attn_low)
        down = z_one(add(*down))
        common = [sums_one[:3], sums_two[2:3], sums_two[:2]]
        fill = jnp.zeros((1, width - 2 * cols), F32)
        rows_of = lambda units_row, heads_row: jnp.concatenate(
            common + [units_row[:1], jnp.concatenate([heads_row[:1, :cols], heads_row[:1, 2 * cols :], fill], axis=1)], axis=0
        )
        small_recv = flip(rows_of(unit_sums_o, head_sums_o), ROW)
        dprojs = [*dprojs, attend_back_heads(info, proj, logs, attn_low, out, 1, cols // HEAD, deps=[down[0]])]

        dprojs, heads_recv, small_recv, attn_low = sync(dprojs, heads_recv, small_recv, attn_low)
        heads_own, dproj, head_sums = gather_heads(info, states, ctx, attn_low, dprojs)
        heads_keep, heads_send = halves(add(heads_own, heads_recv), SIDE)
        small = (rows_of(unit_sums, head_sums) + small_recv).astype(BF16)
        small = jnp.concatenate([small, jnp.zeros((24, width), BF16)], axis=0)
        heads_keep = jnp.concatenate([heads_keep, small], axis=0)
        heads_send = jnp.concatenate([heads_send, small], axis=0)
        heads = heads_keep, flip(heads_send, SIDE)

        down, up, dproj, heads_send = sync(down, up, dproj, heads_send)
        down = z_two(down)
        up = z_one(add(*up))
        in_terms = project(info, dproj, dproj_o, qkv, qkv_o, 4, deps=[heads_send, down[0], up[0]])
        in_recv = swap(in_terms)

        heads, down, up, in_recv, out_rows = sync(heads, down, up, in_recv, out_rows)
        heads = z_one(add(*heads))
        down = z_three(down)
        up = z_two(up)
        in_rows = jnp.concatenate([wide(a) + wide(b) for a, b in zip(in_terms, in_recv)], axis=0)
        in_rows = (entry_grad + in_rows).astype(BF16)
        in_got = flip(half_rows(in_rows), ROW)

        heads, down, up = sync(heads, down, up)
        heads = z_two(heads)
        down = side_start(z_end(down))
        up = z_three(up)
        out_got = flip(half_rows(out_rows), ROW)

        heads, up, in_got = sync(heads, up, in_got)
        heads = z_three(heads)
        up = side_start(z_end(up))
        in_again = flip(in_got, CORE)

        heads, = sync(heads)
        heads = z_end(heads)
        half = heads.shape[0] - small.shape[0]
        heads, small = heads[:half], heads[half:]
        heads = side_start(heads)

        down, out_got = sync(down, out_got)
        down_out = wide(put_together(*down, SIDE))
        out_again = flip(out_got, CORE)

        up, in_again, out_again = sync(up, in_again, out_again)
        up_out = wide(put_together(*up, SIDE))
        states_grad = both_spans(in_rows, in_got, in_again)
        states_out = both_spans(out_rows, out_got, out_again)

        heads, up_out, down_out, states_grad, states_out = sync(heads, up_out, down_out, states_grad, states_out)
        heads_out = wide(put_together(*heads, SIDE))
        qkv_out, out_out = heads_out[: 3 * cols], heads_out[3 * cols :]
        small = wide(small)
        parts = [small[k] for k in range(7)] + [small[7, :cols], small[7, cols : 2 * cols]]
        qkv_out = qkv_out.reshape(3, cols, width).transpose(2, 0, 1)
        return (
            states_out, states_grad, qkv_out, parts[7], parts[8], out_out.T, parts[0], parts[1], parts[2],
            up_out, parts[6], down_out, parts[3], parts[4], parts[5],
        )

    return body


def solution(mesh):
    split = P("dp", None, None)
    in_specs = (
        split, P("dp"), P(None, None, "mp"), P("mp"), P("mp"), P(None, "mp"), P(), P(), P(),
        P(None, "mp"), P("mp"), P(None, "mp"), P(), P(), P(), split,
    )
    out_specs = (
        split, split, P(None, None, "mp"), P("mp"), P("mp"), P(None, "mp"), P(), P(), P(),
        P(None, "mp"), P("mp"), P(None, "mp"), P(), P(), P(),
    )
    return jax.shard_map(build(mesh), mesh=mesh, in_specs=in_specs, out_specs=out_specs, check_vma=False)
```

```python
import jax
import jax.numpy as jnp
from jax import lax
from jax.experimental import pallas as pl
from jax.experimental.pallas import tpu as pltpu
from jax.sharding import PartitionSpec as P

HEAD = 64
EPS = 1e-05
F32 = jnp.float32
BF16 = jnp.bfloat16
LIMIT = 24 * 2**20
QBLOCK = 512
CORE, ROW, SIDE = 1, 2, 4


def dot(a, b, ca, cb):
    return lax.dot_general(a, b, (((ca,), (cb,)), ((), ())), preferred_element_type=F32)


def sds(shape, dtype):
    return jax.ShapeDtypeStruct(shape, dtype)


def whole(array):
    shape = array.shape
    return pl.BlockSpec(shape, lambda i, s: (0,) * len(shape))


def tiled(rows, cols):
    return pl.BlockSpec((rows, cols), lambda i, s: (i, 0))


def slot_rows(array, rows):
    return pl.BlockSpec((None, rows, array.shape[2]), lambda i, s: (s[0], i, 0))


def launch(kernel, info, args, in_specs, out_shapes, out_specs=None, grid=1, deps=(), scratch=(), limit=LIMIT):
    count, extra = len(args), len(deps)

    def inner(info_ref, *refs):
        kernel(info_ref, *refs[:count], *refs[count + extra :])

    specs = [whole(a) if s is None else s for a, s in zip(args, in_specs)]
    out_specs = [None] * len(out_shapes) if out_specs is None else out_specs
    return pl.pallas_call(
        inner,
        out_shape=out_shapes,
        grid_spec=pltpu.PrefetchScalarGridSpec(
            num_scalar_prefetch=1,
            grid=(grid,),
            in_specs=specs + [pl.BlockSpec(memory_space=pl.ANY)] * extra,
            out_specs=[whole(a) if s is None else s for a, s in zip(out_shapes, out_specs)],
            scratch_shapes=scratch,
        ),
        compiler_params=pltpu.CompilerParams(vmem_limit_bytes=limit),
        cost_estimate=pl.CostEstimate(flops=1, bytes_accessed=0, transcendentals=0),
    )(info, *args, *deps)


def norm_forward(inputs):
    centre = inputs - jnp.mean(inputs, axis=-1, keepdims=True)
    spread = jnp.mean(centre * centre, axis=-1, keepdims=True)
    scale = lax.rsqrt(spread + EPS)
    return centre * scale, scale


def norm_backward(grad, normed, scale, gain):
    scaled = grad * gain
    mean_one = jnp.mean(scaled, axis=-1, keepdims=True)
    mean_two = jnp.mean(scaled * normed, axis=-1, keepdims=True)
    return scale * (scaled - mean_one - normed * mean_two)


def column(row, width):
    return jnp.broadcast_to(row, (width, row.shape[1])).T[:, :1]


def wide(value):
    return value.astype(F32)


def attend_kernel(info, rows_ref, weight_ref, pack_ref, proj_ref, ctx_ref, log_ref):
    rows = rows_ref[...]
    cols = weight_ref.shape[0] // 3
    q_bias = column(pack_ref[7:8, :cols], 128)
    v_bias = column(pack_ref[7:8, cols : 2 * cols], 128)
    proj_ref[:cols] = (dot(weight_ref[:cols], rows, 1, 1) + q_bias).astype(BF16)
    proj_ref[cols : 2 * cols] = dot(weight_ref[cols : 2 * cols], rows, 1, 1).astype(BF16)
    proj_ref[2 * cols :] = (dot(weight_ref[2 * cols :], rows, 1, 1) + v_bias).astype(BF16)
    length = rows.shape[0]

    @pl.loop(0, cols // HEAD)
    def _(head):
        rows_of = lambda base: pl.ds(pl.multiple_of(base + head * HEAD, HEAD), HEAD)
        keys = proj_ref[rows_of(cols)]
        values = proj_ref[rows_of(2 * cols)]
        for block in range(length // QBLOCK):
            span = slice(block * QBLOCK, (block + 1) * QBLOCK)
            queries = proj_ref[rows_of(0), span] * BF16(HEAD**-0.5)
            scores = dot(keys, queries, 0, 0)
            highest = jnp.max(scores, axis=0, keepdims=True)
            raised = jnp.exp(scores - highest)
            totals = jnp.sum(raised, axis=0, keepdims=True)
            probs = (raised * (1.0 / totals)).astype(BF16)
            ctx_ref[rows_of(0), span] = dot(values, probs, 1, 0).astype(BF16)
            log_ref[pl.ds(head, 1), span] = highest + jnp.log(totals)


def attend(info, states, weight, pack, deps=()):
    length = states.shape[1]
    cols = weight.shape[0] // 3
    return launch(
        attend_kernel, info, [states, weight, pack], [slot_rows(states, length), None, None],
        [kept((3 * cols, length), BF16), sds((cols, length), BF16), sds((8, length), F32)], deps=deps,
    )


def project_kernel(info, left_ref, left_o_ref, right_ref, right_o_ref, *out_refs):
    size = out_refs[0].shape[0]
    for part, into in enumerate(out_refs):
        span = slice(part * size, (part + 1) * size)
        terms = dot(left_ref[:, span], right_ref[...], 0, 0) + dot(left_o_ref[:, span], right_o_ref[...], 0, 0)
        into[...] = terms.astype(BF16)


def project(info, left, left_o, right, right_o, count, deps=()):
    return launch(
        project_kernel, info, [left, left_o, right, right_o], [None] * 4, chunks(left.shape[1], right.shape[1], count), deps=deps,
    )


def read(refs, steps):
    per = len(refs) // steps
    step = pl.program_id(0)
    parts = []
    for t in range(per):
        value = refs[t][...]
        for k in range(1, steps):
            value = jnp.where(step == k, refs[k * per + t][...], value)
        parts.append(value)
    return wide(jnp.concatenate(parts, axis=0) if per > 1 else parts[0])


def write(refs, steps, value):
    per, rows = max(len(refs) // steps, 1), value.shape[0]
    for k in range(steps):

        @pl.when(pl.program_id(0) == k)
        def _():
            if len(refs) < steps:
                at = k % (steps // len(refs)) * rows
                refs[k * len(refs) // steps][at : at + rows] = value
            else:
                for t in range(per):
                    refs[k * per + t][...] = value[t * rows // per : (t + 1) * rows // per]


def chunks(length, width, count):
    return [sds((length // count, width), BF16)] * count


def kept(shape, dtype):
    return pltpu.HBM(shape, dtype)


def unit_pass(low, up_ref, pack_ref, down_ref, act_ref, slope_ref):
    total = None
    half = up_ref.shape[1] // 2
    for part in range(2):
        cols = slice(part * half, (part + 1) * half)
        hidden = dot(low, up_ref[:, cols], 1, 0) + pack_ref[6:7, cols]
        cdf = 0.5 + 0.5 * lax.erf(hidden * (0.5**0.5))
        pdf = jnp.exp(hidden * hidden * -0.5) * ((2 * jnp.pi) ** -0.5)
        act = (hidden * cdf).astype(BF16)
        act_ref[:, cols] = act
        slope_ref[:, cols] = (cdf + hidden * pdf).astype(BF16)
        term = dot(act, down_ref[:, cols], 1, 1)
        total = term if total is None else total + term
    return total


def feed_own_kernel(info, rows_ref, pack_ref, up_ref, down_ref, *refs):
    first_ref, low_ref, act_ref, slope_ref, part_ref, entry_ref = refs[-6:]
    count = (len(refs) - 6) // 2
    inputs = wide(rows_ref[...]) + (read(refs[:count], 4) + read(refs[count : 2 * count], 4) + pack_ref[0:1])
    entry_ref[...] = inputs
    normed, _ = norm_forward(inputs)
    first = normed * pack_ref[1:2] + pack_ref[2:3]
    first_ref[...] = first
    low = first.astype(BF16)
    low_ref[...] = low
    part_ref[...] = unit_pass(low, up_ref, pack_ref, down_ref, act_ref, slope_ref)


def feed_own(info, states, terms, recv, pack, up, down, deps=()):
    _, length, width = states.shape
    half, units = length // 4, up.shape[1]
    return launch(
        feed_own_kernel, info, [states, pack, up, down, *terms, *recv],
        [slot_rows(states, half)] + [None] * (3 + 2 * len(terms)),
        [sds((length, width), F32), sds((length, width), BF16), sds((length, units), BF16), sds((length, units), BF16), sds((length, width), F32), kept((length, width), F32)],
        [tiled(half, width), tiled(half, width), tiled(half, units), tiled(half, units), tiled(half, width), tiled(half, width)], grid=4, deps=deps,
    )


def places(info, size):
    return [pl.multiple_of(2 * size * info[2], 128), size, pl.multiple_of(2 * size * (1 - info[2]), 128)]


def feed_other_kernel(info, low_ref, part_ref, pack_ref, *refs):
    act_ref, slope_ref = refs[3:5]
    low = low_ref[...]
    total = part_ref[...]
    size = refs[0].shape[1]
    width = low.shape[1]
    for ref, place in zip(refs[:3], places(info, size)):
        cols = pl.ds(place, size)
        hidden = dot(low, ref[:width], 1, 0) + pack_ref[6:7, cols]
        cdf = 0.5 + 0.5 * lax.erf(hidden * (0.5**0.5))
        pdf = jnp.exp(hidden * hidden * -0.5) * ((2 * jnp.pi) ** -0.5)
        act = (hidden * cdf).astype(BF16)
        act_ref[:, cols] = act
        slope_ref[:, cols] = (cdf + hidden * pdf).astype(BF16)
        total = total + dot(act, ref[width:], 1, 1)
    write(refs[5:], 4, total.astype(BF16))


def feed_other(info, low, part, pieces, pack, deps=()):
    length, width = low.shape
    half, units = length // 4, 3 * pieces[0].shape[1]
    return launch(
        feed_other_kernel, info, [low, part, pack, *pieces],
        [tiled(half, width), tiled(half, width), None, None, None, None],
        [sds((length, units), BF16), sds((length, units), BF16)] + chunks(length, width, 2),
        [tiled(half, units), tiled(half, units), None, None], grid=4, deps=deps,
    )


def add_rows(ref, row, value):
    ref[row : row + 1, :] += jnp.sum(value, axis=0, keepdims=True)


def clear_first(ref):
    @pl.when(pl.program_id(0) == 0)
    def _():
        ref[...] = jnp.zeros_like(ref)


def turn_kernel(info, first_ref, *refs):
    terms, recv = refs[:2], refs[2:4]
    cot_ref, pack_ref, out_ref, grad_ref, low_ref, sums_ref = refs[4:]
    live = jnp.where(info[0] < info[1], 1.0, 0.0).astype(F32)
    branch = read(terms, 2) + read(recv, 2) + pack_ref[3:4]
    normed, scale = norm_forward(first_ref[...] + branch)
    out_ref[...] = ((normed * pack_ref[4:5] + pack_ref[5:6]) * live).astype(BF16)
    upstream = wide(cot_ref[...]) * live
    grad = norm_backward(upstream, normed, scale, pack_ref[4:5])
    grad_ref[...] = grad
    low_ref[...] = grad.astype(BF16)
    clear_first(sums_ref)
    add_rows(sums_ref, 0, upstream * normed)
    add_rows(sums_ref, 1, upstream)
    add_rows(sums_ref, 2, grad)


def turn(info, first, terms, recv, cotangent, pack, deps=()):
    length, width = first.shape
    half = length // 2
    tile = tiled(half, width)
    return launch(
        turn_kernel, info, [first, *terms, *recv, cotangent, pack],
        [tile] + [None] * 4 + [slot_rows(cotangent, half), None],
        [kept((length, width), BF16), kept((length, width), F32), sds((length, width), BF16), sds((8, width), F32)],
        [tile, tile, tile, None], grid=2, deps=deps,
    )


def cross_kernel(info, left_ref, right_ref, right_o_ref, keep_ref, send_ref):
    side = info[2]
    half = keep_ref.shape[1]
    for which, ref in ((side, keep_ref), (1 - side, send_ref)):
        left = left_ref[:, pl.ds(pl.multiple_of(which * half, 128), half)]
        ref[0] = dot(left, right_ref[...], 0, 0).astype(BF16)
        ref[1] = dot(left, right_o_ref[...], 0, 0).astype(BF16)


def cross(info, left, right, right_o, deps=()):
    shape = sds((2, left.shape[1] // 2, right.shape[1]), BF16)
    return launch(cross_kernel, info, [left, right, right_o], [None] * 3, [shape, shape], deps=deps)


def plain_cross_kernel(info, left_ref, right_ref, right_o_ref, own_ref, other_ref, sums_ref, sums_o_ref):
    ones = jnp.ones((8, right_ref.shape[0]), BF16)
    for right, into, sums in ((right_ref, own_ref, sums_ref), (right_o_ref, other_ref, sums_o_ref)):
        into[...] = dot(left_ref[...], right[...], 0, 0).astype(BF16)
        sums[...] = dot(ones, right[...], 1, 0)


def plain_cross(info, left, right, right_o, deps=()):
    shape = sds((left.shape[1], right.shape[1]), BF16)
    sums = sds((8, right.shape[1]), F32)
    return launch(plain_cross_kernel, info, [left, right, right_o], [None] * 3, [shape, shape, sums, sums], deps=deps)


def back_own_kernel(info, low_ref, slope_ref, up_ref, down_ref, hidden_ref, part_ref):
    low = low_ref[...]
    half = up_ref.shape[1] // 2
    total = None
    for part in range(2):
        cols = slice(part * half, (part + 1) * half)
        hidden = (wide(slope_ref[:, cols]) * dot(low, down_ref[:, cols], 1, 0)).astype(BF16)
        hidden_ref[:, cols] = hidden
        term = dot(hidden, up_ref[:, cols], 1, 1)
        total = term if total is None else total + term
    part_ref[...] = total


def back_own(info, low, slope, up, down, deps=()):
    length, width = low.shape
    half, units = length // 4, slope.shape[1]
    return launch(
        back_own_kernel, info, [low, slope, up, down], [tiled(half, width), tiled(half, units), None, None],
        [sds((length, units), BF16), sds((length, width), F32)], [tiled(half, units), tiled(half, width)], grid=4, deps=deps,
    )


def back_other_kernel(info, low_ref, slope_ref, part_ref, *refs):
    hidden_ref = refs[3]
    low = low_ref[...]
    width = low.shape[1]
    size = refs[0].shape[1]
    total = part_ref[...]
    for ref, place in zip(refs[:3], places(info, size)):
        cols = pl.ds(place, size)
        hidden = (wide(slope_ref[:, cols]) * dot(low, ref[width:], 1, 0)).astype(BF16)
        hidden_ref[:, cols] = hidden
        total = total + dot(hidden, ref[:width], 1, 1)
    write(refs[4:], 4, total.astype(BF16))


def back_other(info, low, slope, part, pieces, deps=()):
    length, width = low.shape
    half, units = length // 4, slope.shape[1]
    return launch(
        back_other_kernel, info, [low, slope, part, *pieces],
        [tiled(half, width), tiled(half, units), tiled(half, width), None, None, None],
        [sds((length, units), BF16)] + chunks(length, width, 2), [tiled(half, units), None, None], grid=4, deps=deps,
    )


def entry_kernel(info, inputs_ref, second_ref, pack_ref, term_a, term_b, recv_a, recv_b, entry_ref, low_ref, sums_ref):
    normed, scale = norm_forward(inputs_ref[...])
    grad = second_ref[...] + (read([term_a, term_b], 2) + read([recv_a, recv_b], 2))
    entry = norm_backward(grad, normed, scale, pack_ref[1:2])
    entry_ref[...] = entry
    low_ref[...] = entry.astype(BF16)
    clear_first(sums_ref)
    add_rows(sums_ref, 0, entry)
    add_rows(sums_ref, 1, grad * normed)
    add_rows(sums_ref, 2, grad)


def entry(info, inputs, second, pack, back_terms, back_recv, deps=()):
    length, width = inputs.shape
    tile = tiled(length // 2, width)
    return launch(
        entry_kernel, info, [inputs, second, pack, *back_terms, *back_recv], [tile, tile] + [None] * 5,
        [kept((length, width), F32), sds((length, width), BF16), sds((8, width), F32)], [tile, tile, None], grid=2, deps=deps,
    )


def attend_back_kernel(info, rows_ref, proj_ref, ctx_ref, log_ref, low_ref, out_ref, grads_ref, dproj_ref, sums_ref, cgrad):
    length = rows_ref.shape[0]
    cols = ctx_ref.shape[0]
    low = low_ref[...]
    cgrad[...] = dot(out_ref[...], low, 1, 1).astype(BF16)
    scale = HEAD**-0.5

    @pl.loop(0, cols // HEAD)
    def _(head):
        query_rows, key_rows, value_rows = (pl.ds(pl.multiple_of(k * cols + head * HEAD, HEAD), HEAD) for k in range(3))
        keys = proj_ref[key_rows]
        values = proj_ref[value_rows]
        key_total = None
        value_total = None
        for block in range(length // QBLOCK):
            span = slice(block * QBLOCK, (block + 1) * QBLOCK)
            queries = proj_ref[query_rows, span] * BF16(scale)
            upstream = cgrad[query_rows, span]
            scores = dot(keys, queries, 0, 0)
            probs = jnp.exp(scores - log_ref[pl.ds(head, 1), span])
            value_term = dot(upstream, probs.astype(BF16), 1, 1)
            prob_grad = dot(values, upstream, 0, 0)
            inner = jnp.sum(prob_grad * probs, axis=0, keepdims=True)
            score_grad = (probs * (prob_grad - inner)).astype(BF16)
            dproj_ref[query_rows, span] = (dot(keys, score_grad, 1, 0) * scale).astype(BF16)
            key_term = dot(queries, score_grad, 1, 1)
            key_total = key_term if key_total is None else key_total + key_term
            value_total = value_term if value_total is None else value_total + value_term
        dproj_ref[key_rows] = key_total.astype(BF16)
        dproj_ref[value_rows] = value_total.astype(BF16)
    rows = rows_ref[...]
    grads_ref[: 3 * cols] = dot(dproj_ref[...], rows, 1, 0).astype(BF16)
    grads_ref[3 * cols :] = dot(ctx_ref[...], low, 1, 0).astype(BF16)
    sums_ref[...] = dot(jnp.ones((8, length), BF16), dproj_ref[...], 1, 1)


def attend_back(info, states, proj, ctx, log_total, low, out, deps=()):
    _, length, width = states.shape
    cols = ctx.shape[0]
    return launch(
        attend_back_kernel, info, [states, proj, ctx, log_total, low, out], [slot_rows(states, length)] + [None] * 5,
        [sds((4 * cols, width), BF16), sds((3 * cols, length), BF16), sds((8, 3 * cols), F32)], deps=deps,
        scratch=[pltpu.VMEM((cols, length), BF16)],
    )


def attend_back_heads(info, proj, log_total, low, out, first, last, deps=()):
    cols, length = proj.shape[0] // 3, proj.shape[1]
    scale = HEAD**-0.5

    def kernel(info, proj_ref, log_ref, low_ref, out_ref, dproj_ref):
        @pl.loop(0, last - first)
        def _(step):
            head = step + first
            at = lambda k: pl.ds(pl.multiple_of(k * cols + head * HEAD, HEAD), HEAD)
            into = lambda k: pl.ds(pl.multiple_of((3 * step + k) * HEAD, HEAD), HEAD)
            upstream_all = dot(out_ref[at(0)], low_ref[...], 1, 1).astype(BF16)
            keys, values = proj_ref[at(1)], proj_ref[at(2)]
            key_total = None
            value_total = None
            for block in range(length // QBLOCK):
                span = slice(block * QBLOCK, (block + 1) * QBLOCK)
                queries = proj_ref[at(0), span] * BF16(scale)
                upstream = upstream_all[:, span]
                scores = dot(keys, queries, 0, 0)
                probs = jnp.exp(scores - log_ref[pl.ds(head, 1), span])
                value_term = dot(upstream, probs.astype(BF16), 1, 1)
                prob_grad = dot(values, upstream, 0, 0)
                inner = jnp.sum(prob_grad * probs, axis=0, keepdims=True)
                score_grad = (probs * (prob_grad - inner)).astype(BF16)
                dproj_ref[into(0), span] = (dot(keys, score_grad, 1, 0) * scale).astype(BF16)
                key_term = dot(queries, score_grad, 1, 1)
                key_total = key_term if key_total is None else key_total + key_term
                value_total = value_term if value_total is None else value_total + value_term
            dproj_ref[into(1)] = key_total.astype(BF16)
            dproj_ref[into(2)] = value_total.astype(BF16)

    return launch(
        kernel, info, [proj, log_total, low, out], [None] * 4, [sds((3 * HEAD * (last - first), length), BF16)], deps=deps,
    )[0]


def heads_kernel(info, rows_ref, ctx_ref, low_ref, *refs):
    grads_ref, dproj_ref, sums_ref = refs[-3:]
    cols = ctx_ref.shape[0]
    head = 0
    for ref in refs[:-3]:
        for step in range(ref.shape[0] // (3 * HEAD)):
            for k in range(3):
                at = (3 * step + k) * HEAD
                dproj_ref[k * cols + head * HEAD : k * cols + (head + 1) * HEAD, :] = ref[at : at + HEAD, :]
            head += 1
    grads_ref[: 3 * cols] = dot(dproj_ref[...], rows_ref[...], 1, 0).astype(BF16)
    grads_ref[3 * cols :] = dot(ctx_ref[...], low_ref[...], 1, 0).astype(BF16)
    sums_ref[...] = dot(jnp.ones((8, dproj_ref.shape[1]), BF16), dproj_ref[...], 1, 1)


def gather_heads(info, states, ctx, low, dprojs, deps=()):
    _, length, width = states.shape
    cols = ctx.shape[0]
    return launch(
        heads_kernel, info, [states, ctx, low, *dprojs], [slot_rows(states, length)] + [None] * (2 + len(dprojs)),
        [sds((4 * cols, width), BF16), sds((3 * cols, length), BF16), sds((8, 3 * cols), F32)], deps=deps,
    )


def build(mesh):
    n_dp, n_mp = mesh.shape["dp"], mesh.shape["mp"]
    n_z = n_dp // 2
    z_bits = []
    while n_mp * 2 << len(z_bits) < n_dp * n_mp:
        z_bits.append(n_mp * 2 << len(z_bits))

    def flip(value, bit):
        pairs = [(i, i ^ bit) for i in range(n_dp * n_mp)]
        return lax.ppermute(value, ("dp", "mp"), pairs)

    def swap(values):
        return [flip(v, CORE) for v in values]

    def body(
        states, span_count, qkv_weight, q_bias, v_bias, out_weight, out_bias, gain_one, shift_one,
        up_weight, up_bias, down_weight, down_bias, gain_two, shift_two, cotangent,
    ):
        dp, mp = lax.axis_index("dp"), lax.axis_index("mp")
        place = dp * n_mp + mp
        slot, core = mp // ROW, mp % ROW
        info = jnp.stack([slot, span_count[0], dp % 2, dp // 2]).astype(jnp.int32)
        width, _, cols = qkv_weight.shape
        units = up_weight.shape[1]

        token = [place]

        def halves(value, bit):
            side = (token[0] // bit) % 2
            rows = value.shape[0] // 2
            return tuple(lax.dynamic_slice_in_dim(value, w * rows, rows, 0) for w in (side, 1 - side))

        def add(one, two):
            return (wide(one) + wide(two)).astype(BF16)

        def join(value, bit):
            other = flip(value, bit)
            lower = (token[0] // bit) % 2 == 0
            return jnp.concatenate([jnp.where(lower, value, other), jnp.where(lower, other, value)], axis=0)

        def sync(*values):
            token[0], values = lax.optimization_barrier((token[0], values))
            return values

        def put_together(value, other, bit):
            lower = (token[0] // bit) % 2 == 0
            return jnp.concatenate([jnp.where(lower, value, other), jnp.where(lower, other, value)], axis=0)

        z_near, z_far = n_mp * 2, n_mp * 4

        def z_one(value):
            if n_z == 4:
                mine, theirs = halves(value, z_near)
                return mine, flip(theirs, z_near)
            for bit in z_bits:
                value = add(value, flip(value, bit))
            return value, value

        def z_two(pair):
            if n_z != 4:
                return pair
            value = add(*pair)
            return value, flip(value, z_far)

        def z_three(pair):
            if n_z != 4:
                return pair
            value = add(*pair)
            return value, flip(value, z_near)

        def z_end(pair):
            return put_together(*pair, z_near) if n_z == 4 else pair[0]

        def side_start(value):
            return value, flip(value, SIDE)

        joined = jnp.concatenate([q_bias, v_bias, jnp.zeros((width - 2 * cols,), F32)])
        pack = jnp.stack([out_bias, gain_one, shift_one, down_bias, gain_two, shift_two, up_bias, joined])
        qkv = qkv_weight.transpose(1, 2, 0).reshape(3 * cols, width)
        out = out_weight.T
        pack_o = flip(pack, ROW)
        qkv_o = flip(qkv, ROW)

        proj, ctx, logs = attend(info, states, qkv, pack)
        third = units // 3
        side = dp % 2
        cut = lambda w, at: lax.dynamic_slice_in_dim(w, at, third, 1)
        outer = jnp.concatenate([cut(up_weight, 2 * third * side), cut(down_weight, 2 * third * side)], axis=0)
        middle = jnp.concatenate([up_weight[:, third : 2 * third], down_weight[:, third : 2 * third]], axis=0)
        outer, middle, qkv_o, pack_o, out_send, _ = lax.optimization_barrier((outer, middle, qkv_o, pack_o, out, logs))
        outer = flip(outer, ROW)
        out_o = flip(out_send, ROW)
        proj_o, ctx_o, logs_o = attend(info, states, qkv_o, pack_o, deps=[logs])
        middle, ctx_o, outer = lax.optimization_barrier((middle, ctx_o, outer))
        middle = flip(middle, ROW)
        forwarded = flip(outer, SIDE)
        terms = project(info, ctx, ctx_o, out, out_o, 8)
        recv = swap(terms)
        first, low, act, slope, part, entry_in = feed_own(
            info, states, terms, recv, pack, up_weight, down_weight,
        )
        pieces = [outer, middle, forwarded]
        act_o, slope_o, *feed_terms = feed_other(info, low, part, pieces, pack_o)
        out_rows, second, branch_low, sums_two = turn(
            info, first, feed_terms, swap(feed_terms), cotangent, pack,
        )

        def half_rows(span):
            size = span.shape[0] // 2
            return lax.dynamic_slice_in_dim(span, core * size, size, 0)

        def both_spans(span, got, again):
            other = put_together(got, again, CORE)
            return put_together(span[None], other[None], ROW)

        fence = lambda *v: lax.optimization_barrier(v)
        down_keep, down_send = cross(info, branch_low, act, act_o)
        down_recv = flip(down_send, SIDE)
        hidden, back_part = back_own(info, branch_low, slope, up_weight, down_weight, deps=[down_keep])
        hidden_o, *back_terms = back_other(info, branch_low, slope_o, back_part, pieces)
        back_recv = swap(back_terms)
        up_own, up_other, unit_sums, unit_sums_o = plain_cross(info, low, hidden, hidden_o)
        up_recv = flip(up_other, ROW)
        entry_grad, attn_low, sums_one = entry(info, pltpu.with_memory_space_constraint(entry_in, pltpu.HBM), pltpu.with_memory_space_constraint(second, pltpu.HBM), pack, back_terms, back_recv, deps=[up_own, down_recv])

        attn_low, down_keep, down_recv = sync(attn_low, down_keep, down_recv)
        down_own, down_other = (add(down_keep[k], down_recv[k]) for k in range(2))
        down = down_own, flip(down_other, ROW)
        heads_other, dproj_o, head_sums_o = attend_back(
            info, states, proj_o, ctx_o, logs_o, attn_low, out_o, deps=[down_other],
        )

        heads_other, up_own, up_recv, attn_low = sync(heads_other, up_own, up_recv, attn_low)
        heads_recv = flip(heads_other, ROW)
        up_keep, up_send = halves(add(up_own, up_recv), SIDE)
        up = up_keep, flip(up_send, SIDE)
        dprojs = [attend_back_heads(info, proj, logs, attn_low, out, 0, 1, deps=[up_send, heads_other])]

        dprojs, down, attn_low = sync(dprojs, down, attn_low)
        down = z_one(add(*down))
        common = [sums_one[:3], sums_two[2:3], sums_two[:2]]
        fill = jnp.zeros((1, width - 2 * cols), F32)
        rows_of = lambda units_row, heads_row: jnp.concatenate(
            common + [units_row[:1], jnp.concatenate([heads_row[:1, :cols], heads_row[:1, 2 * cols :], fill], axis=1)], axis=0
        )
        small_recv = flip(rows_of(unit_sums_o, head_sums_o), ROW)
        dprojs = [*dprojs, attend_back_heads(info, proj, logs, attn_low, out, 1, cols // HEAD, deps=[down[0]])]

        dprojs, heads_recv, small_recv, attn_low = sync(dprojs, heads_recv, small_recv, attn_low)
        heads_own, dproj, head_sums = gather_heads(info, states, ctx, attn_low, dprojs)
        heads_keep, heads_send = halves(add(heads_own, heads_recv), SIDE)
        small = (rows_of(unit_sums, head_sums) + small_recv).astype(BF16)
        small = jnp.concatenate([small, jnp.zeros((24, width), BF16)], axis=0)
        heads_keep = jnp.concatenate([heads_keep, small], axis=0)
        heads_send = jnp.concatenate([heads_send, small], axis=0)
        heads = heads_keep, flip(heads_send, SIDE)

        down, up, dproj, heads_send = sync(down, up, dproj, heads_send)
        down = z_two(down)
        up = z_one(add(*up))
        in_terms = project(info, dproj, dproj_o, qkv, qkv_o, 4, deps=[heads_send, down[0], up[0]])
        in_recv = swap(in_terms)

        heads, down, up, in_terms = sync(heads, down, up, in_terms)
        heads = z_one(add(*heads))
        down = z_three(down)
        up = z_two(up)
        out_rows, = sync(out_rows)
        in_rows = jnp.concatenate([wide(a) + wide(b) for a, b in zip(in_terms, in_recv)], axis=0)
        in_rows = (entry_grad + in_rows).astype(BF16)
        in_got = flip(half_rows(in_rows), ROW)

        heads, down, up = sync(heads, down, up)
        heads = z_two(heads)
        down = side_start(z_end(down))
        up = z_three(up)
        out_got = flip(half_rows(out_rows), ROW)

        heads, up, in_got = sync(heads, up, in_got)
        heads = z_three(heads)
        up = side_start(z_end(up))
        in_again = flip(in_got, CORE)

        heads, = sync(heads)
        heads = z_end(heads)
        half = heads.shape[0] - small.shape[0]
        heads, small = heads[:half], heads[half:]
        heads = side_start(heads)

        down, out_got = sync(down, out_got)
        down_out = wide(put_together(*down, SIDE))
        out_again = flip(out_got, CORE)

        up, in_again, out_again = sync(up, in_again, out_again)
        up_out = wide(put_together(*up, SIDE))
        states_grad = both_spans(in_rows, in_got, in_again)
        states_out = both_spans(out_rows, out_got, out_again)

        heads, up_out, down_out, states_grad, states_out = sync(heads, up_out, down_out, states_grad, states_out)
        heads_out = wide(put_together(*heads, SIDE))
        qkv_out, out_out = heads_out[: 3 * cols], heads_out[3 * cols :]
        small = wide(small)
        parts = [small[k] for k in range(7)] + [small[7, :cols], small[7, cols : 2 * cols]]
        qkv_out = qkv_out.reshape(3, cols, width).transpose(2, 0, 1)
        return (
            states_out, states_grad, qkv_out, parts[7], parts[8], out_out.T, parts[0], parts[1], parts[2],
            up_out, parts[6], down_out, parts[3], parts[4], parts[5],
        )

    return body


def solution(mesh):
    split = P("dp", None, None)
    in_specs = (
        split, P("dp"), P(None, None, "mp"), P("mp"), P("mp"), P(None, "mp"), P(), P(), P(),
        P(None, "mp"), P("mp"), P(None, "mp"), P(), P(), P(), split,
    )
    out_specs = (
        split, split, P(None, None, "mp"), P("mp"), P("mp"), P(None, "mp"), P(), P(), P(),
        P(None, "mp"), P("mp"), P(None, "mp"), P(), P(), P(),
    )
    return jax.shard_map(build(mesh), mesh=mesh, in_specs=in_specs, out_specs=out_specs, check_vma=False)
```

```python
import jax
import jax.numpy as jnp
from jax import lax
from jax.experimental import pallas as pl
from jax.experimental.pallas import tpu as pltpu
from jax.sharding import PartitionSpec as P

HEAD = 64
EPS = 1e-05
F32 = jnp.float32
BF16 = jnp.bfloat16
LIMIT = 24 * 2**20
QBLOCK = 512
CORE, ROW, SIDE = 1, 2, 4


def dot(a, b, ca, cb):
    return lax.dot_general(a, b, (((ca,), (cb,)), ((), ())), preferred_element_type=F32)


def sds(shape, dtype):
    return jax.ShapeDtypeStruct(shape, dtype)


def whole(array):
    shape = array.shape
    return pl.BlockSpec(shape, lambda i, s: (0,) * len(shape))


def tiled(rows, cols):
    return pl.BlockSpec((rows, cols), lambda i, s: (i, 0))


def slot_rows(array, rows):
    return pl.BlockSpec((None, rows, array.shape[2]), lambda i, s: (s[0], i, 0))


def launch(kernel, info, args, in_specs, out_shapes, out_specs=None, grid=1, deps=(), scratch=(), limit=LIMIT):
    count, extra = len(args), len(deps)

    def inner(info_ref, *refs):
        kernel(info_ref, *refs[:count], *refs[count + extra :])

    specs = [whole(a) if s is None else s for a, s in zip(args, in_specs)]
    out_specs = [None] * len(out_shapes) if out_specs is None else out_specs
    return pl.pallas_call(
        inner,
        out_shape=out_shapes,
        grid_spec=pltpu.PrefetchScalarGridSpec(
            num_scalar_prefetch=1,
            grid=(grid,),
            in_specs=specs + [pl.BlockSpec(memory_space=pl.ANY)] * extra,
            out_specs=[whole(a) if s is None else s for a, s in zip(out_shapes, out_specs)],
            scratch_shapes=scratch,
        ),
        compiler_params=pltpu.CompilerParams(vmem_limit_bytes=limit),
        cost_estimate=pl.CostEstimate(flops=1, bytes_accessed=0, transcendentals=0),
    )(info, *args, *deps)


def far(value):
    return pltpu.with_memory_space_constraint(value, pltpu.HBM)


def norm_forward(inputs):
    centre = inputs - jnp.mean(inputs, axis=-1, keepdims=True)
    spread = jnp.mean(centre * centre, axis=-1, keepdims=True)
    scale = lax.rsqrt(spread + EPS)
    return centre * scale, scale


def norm_backward(grad, normed, scale, gain):
    scaled = grad * gain
    mean_one = jnp.mean(scaled, axis=-1, keepdims=True)
    mean_two = jnp.mean(scaled * normed, axis=-1, keepdims=True)
    return scale * (scaled - mean_one - normed * mean_two)


def column(row, width):
    return jnp.broadcast_to(row, (width, row.shape[1])).T[:, :1]


def wide(value):
    return value.astype(F32)


def attend_kernel(info, rows_ref, weight_ref, pack_ref, proj_ref, ctx_ref, log_ref):
    rows = rows_ref[...]
    cols = weight_ref.shape[0] // 3
    q_bias = column(pack_ref[7:8, :cols], 128)
    v_bias = column(pack_ref[7:8, cols : 2 * cols], 128)
    proj_ref[:cols] = (dot(weight_ref[:cols], rows, 1, 1) + q_bias).astype(BF16)
    proj_ref[cols : 2 * cols] = dot(weight_ref[cols : 2 * cols], rows, 1, 1).astype(BF16)
    proj_ref[2 * cols :] = (dot(weight_ref[2 * cols :], rows, 1, 1) + v_bias).astype(BF16)
    length = rows.shape[0]

    @pl.loop(0, cols // HEAD)
    def _(head):
        rows_of = lambda base: pl.ds(pl.multiple_of(base + head * HEAD, HEAD), HEAD)
        keys = proj_ref[rows_of(cols)]
        values = proj_ref[rows_of(2 * cols)]
        for block in range(length // QBLOCK):
            span = slice(block * QBLOCK, (block + 1) * QBLOCK)
            queries = proj_ref[rows_of(0), span] * BF16(HEAD**-0.5)
            scores = dot(keys, queries, 0, 0)
            highest = jnp.max(scores, axis=0, keepdims=True)
            raised = jnp.exp(scores - highest)
            totals = jnp.sum(raised, axis=0, keepdims=True)
            probs = (raised * (1.0 / totals)).astype(BF16)
            ctx_ref[rows_of(0), span] = dot(values, probs, 1, 0).astype(BF16)
            log_ref[pl.ds(head, 1), span] = highest + jnp.log(totals)


def attend(info, states, weight, pack, deps=()):
    length = states.shape[1]
    cols = weight.shape[0] // 3
    return launch(
        attend_kernel, info, [states, weight, pack], [slot_rows(states, length), None, None],
        [kept((3 * cols, length), BF16), sds((cols, length), BF16), sds((8, length), F32)], deps=deps,
    )


def project_kernel(info, left_ref, left_o_ref, right_ref, right_o_ref, *out_refs):
    size = out_refs[0].shape[0]
    for part, into in enumerate(out_refs):
        span = slice(part * size, (part + 1) * size)
        terms = dot(left_ref[:, span], right_ref[...], 0, 0) + dot(left_o_ref[:, span], right_o_ref[...], 0, 0)
        into[...] = terms.astype(BF16)


def project(info, left, left_o, right, right_o, count, deps=()):
    return launch(
        project_kernel, info, [left, left_o, right, right_o], [None] * 4, chunks(left.shape[1], right.shape[1], count), deps=deps,
    )


def read(refs, steps):
    per = len(refs) // steps
    step = pl.program_id(0)
    parts = []
    for t in range(per):
        value = refs[t][...]
        for k in range(1, steps):
            value = jnp.where(step == k, refs[k * per + t][...], value)
        parts.append(value)
    return wide(jnp.concatenate(parts, axis=0) if per > 1 else parts[0])


def write(refs, steps, value):
    per, rows = max(len(refs) // steps, 1), value.shape[0]
    for k in range(steps):

        @pl.when(pl.program_id(0) == k)
        def _():
            if len(refs) < steps:
                at = k % (steps // len(refs)) * rows
                refs[k * len(refs) // steps][at : at + rows] = value
            else:
                for t in range(per):
                    refs[k * per + t][...] = value[t * rows // per : (t + 1) * rows // per]


def chunks(length, width, count):
    return [sds((length // count, width), BF16)] * count


def kept(shape, dtype):
    return pltpu.HBM(shape, dtype)


def unit_pass(low, up_ref, pack_ref, down_ref, act_ref, slope_ref):
    total = None
    half = up_ref.shape[1] // 2
    for part in range(2):
        cols = slice(part * half, (part + 1) * half)
        hidden = dot(low, up_ref[:, cols], 1, 0) + pack_ref[6:7, cols]
        cdf = 0.5 + 0.5 * lax.erf(hidden * (0.5**0.5))
        pdf = jnp.exp(hidden * hidden * -0.5) * ((2 * jnp.pi) ** -0.5)
        act = (hidden * cdf).astype(BF16)
        act_ref[:, cols] = act
        slope_ref[:, cols] = (cdf + hidden * pdf).astype(BF16)
        term = dot(act, down_ref[:, cols], 1, 1)
        total = term if total is None else total + term
    return total


def feed_own_kernel(info, rows_ref, pack_ref, up_ref, down_ref, *refs):
    first_ref, low_ref, act_ref, slope_ref, part_ref, entry_ref = refs[-6:]
    count = (len(refs) - 6) // 2
    inputs = wide(rows_ref[...]) + (read(refs[:count], 4) + read(refs[count : 2 * count], 4) + pack_ref[0:1])
    entry_ref[...] = inputs
    normed, _ = norm_forward(inputs)
    first = normed * pack_ref[1:2] + pack_ref[2:3]
    first_ref[...] = first
    low = first.astype(BF16)
    low_ref[...] = low
    part_ref[...] = unit_pass(low, up_ref, pack_ref, down_ref, act_ref, slope_ref)


def feed_own(info, states, terms, recv, pack, up, down, deps=()):
    _, length, width = states.shape
    half, units = length // 4, up.shape[1]
    return launch(
        feed_own_kernel, info, [states, pack, up, down, *terms, *recv],
        [slot_rows(states, half)] + [None] * (3 + 2 * len(terms)),
        [sds((length, width), F32), sds((length, width), BF16), sds((length, units), BF16), sds((length, units), BF16), sds((length, width), F32), kept((length, width), F32)],
        [tiled(half, width), tiled(half, width), tiled(half, units), tiled(half, units), tiled(half, width), tiled(half, width)], grid=4, deps=deps,
    )


def places(info, size):
    return [pl.multiple_of(2 * size * info[2], 128), size, pl.multiple_of(2 * size * (1 - info[2]), 128)]


def feed_other_kernel(info, low_ref, part_ref, pack_ref, *refs):
    act_ref, slope_ref = refs[3:5]
    low = low_ref[...]
    total = part_ref[...]
    size = refs[0].shape[1]
    width = low.shape[1]
    for ref, place in zip(refs[:3], places(info, size)):
        cols = pl.ds(place, size)
        hidden = dot(low, ref[:width], 1, 0) + pack_ref[6:7, cols]
        cdf = 0.5 + 0.5 * lax.erf(hidden * (0.5**0.5))
        pdf = jnp.exp(hidden * hidden * -0.5) * ((2 * jnp.pi) ** -0.5)
        act = (hidden * cdf).astype(BF16)
        act_ref[:, cols] = act
        slope_ref[:, cols] = (cdf + hidden * pdf).astype(BF16)
        total = total + dot(act, ref[width:], 1, 1)
    write(refs[5:], 4, total.astype(BF16))


def feed_other(info, low, part, pieces, pack, deps=()):
    length, width = low.shape
    half, units = length // 4, 3 * pieces[0].shape[1]
    return launch(
        feed_other_kernel, info, [low, part, pack, *pieces],
        [tiled(half, width), tiled(half, width), None, None, None, None],
        [sds((length, units), BF16), sds((length, units), BF16)] + chunks(length, width, 2),
        [tiled(half, units), tiled(half, units), None, None], grid=4, deps=deps,
    )


def add_rows(ref, row, value):
    ref[row : row + 1, :] += jnp.sum(value, axis=0, keepdims=True)


def clear_first(ref):
    @pl.when(pl.program_id(0) == 0)
    def _():
        ref[...] = jnp.zeros_like(ref)


def turn_kernel(info, first_ref, *refs):
    terms, recv = refs[:2], refs[2:4]
    cot_ref, pack_ref, out_ref, grad_ref, low_ref, sums_ref = refs[4:]
    live = jnp.where(info[0] < info[1], 1.0, 0.0).astype(F32)
    branch = read(terms, 2) + read(recv, 2) + pack_ref[3:4]
    normed, scale = norm_forward(first_ref[...] + branch)
    out_ref[...] = ((normed * pack_ref[4:5] + pack_ref[5:6]) * live).astype(BF16)
    upstream = wide(cot_ref[...]) * live
    grad = norm_backward(upstream, normed, scale, pack_ref[4:5])
    grad_ref[...] = grad
    low_ref[...] = grad.astype(BF16)
    clear_first(sums_ref)
    add_rows(sums_ref, 0, upstream * normed)
    add_rows(sums_ref, 1, upstream)
    add_rows(sums_ref, 2, grad)


def turn(info, first, terms, recv, cotangent, pack, deps=()):
    length, width = first.shape
    half = length // 2
    tile = tiled(half, width)
    return launch(
        turn_kernel, info, [first, *terms, *recv, cotangent, pack],
        [tile] + [None] * 4 + [slot_rows(cotangent, half), None],
        [kept((length, width), BF16), kept((length, width), F32), sds((length, width), BF16), sds((8, width), F32)],
        [tile, tile, tile, None], grid=2, deps=deps,
    )


def cross_kernel(info, left_ref, right_ref, right_o_ref, keep_ref, send_ref):
    side = info[2]
    half = keep_ref.shape[1]
    for which, ref in ((side, keep_ref), (1 - side, send_ref)):
        left = left_ref[:, pl.ds(pl.multiple_of(which * half, 128), half)]
        ref[0] = dot(left, right_ref[...], 0, 0).astype(BF16)
        ref[1] = dot(left, right_o_ref[...], 0, 0).astype(BF16)


def cross(info, left, right, right_o, deps=()):
    shape = sds((2, left.shape[1] // 2, right.shape[1]), BF16)
    return launch(cross_kernel, info, [left, right, right_o], [None] * 3, [shape, shape], deps=deps)


def plain_cross_kernel(info, left_ref, right_ref, right_o_ref, own_ref, other_ref, sums_ref, sums_o_ref):
    ones = jnp.ones((8, right_ref.shape[0]), BF16)
    for right, into, sums in ((right_ref, own_ref, sums_ref), (right_o_ref, other_ref, sums_o_ref)):
        into[...] = dot(left_ref[...], right[...], 0, 0).astype(BF16)
        sums[...] = dot(ones, right[...], 1, 0)


def plain_cross(info, left, right, right_o, deps=()):
    shape = sds((left.shape[1], right.shape[1]), BF16)
    sums = sds((8, right.shape[1]), F32)
    return launch(plain_cross_kernel, info, [left, right, right_o], [None] * 3, [shape, shape, sums, sums], deps=deps)


def back_own_kernel(info, low_ref, slope_ref, up_ref, down_ref, hidden_ref, part_ref):
    low = low_ref[...]
    half = up_ref.shape[1] // 2
    total = None
    for part in range(2):
        cols = slice(part * half, (part + 1) * half)
        hidden = (wide(slope_ref[:, cols]) * dot(low, down_ref[:, cols], 1, 0)).astype(BF16)
        hidden_ref[:, cols] = hidden
        term = dot(hidden, up_ref[:, cols], 1, 1)
        total = term if total is None else total + term
    part_ref[...] = total


def back_own(info, low, slope, up, down, deps=()):
    length, width = low.shape
    half, units = length // 4, slope.shape[1]
    return launch(
        back_own_kernel, info, [low, slope, up, down], [tiled(half, width), tiled(half, units), None, None],
        [sds((length, units), BF16), sds((length, width), F32)], [tiled(half, units), tiled(half, width)], grid=4, deps=deps,
    )


def back_other_kernel(info, low_ref, slope_ref, part_ref, *refs):
    hidden_ref = refs[3]
    low = low_ref[...]
    width = low.shape[1]
    size = refs[0].shape[1]
    total = part_ref[...]
    for ref, place in zip(refs[:3], places(info, size)):
        cols = pl.ds(place, size)
        hidden = (wide(slope_ref[:, cols]) * dot(low, ref[width:], 1, 0)).astype(BF16)
        hidden_ref[:, cols] = hidden
        total = total + dot(hidden, ref[:width], 1, 1)
    write(refs[4:], 4, total.astype(BF16))


def back_other(info, low, slope, part, pieces, deps=()):
    length, width = low.shape
    half, units = length // 4, slope.shape[1]
    return launch(
        back_other_kernel, info, [low, slope, part, *pieces],
        [tiled(half, width), tiled(half, units), tiled(half, width), None, None, None],
        [sds((length, units), BF16)] + chunks(length, width, 2), [tiled(half, units), None, None], grid=4, deps=deps,
    )


def entry_kernel(info, inputs_ref, second_ref, pack_ref, term_a, term_b, recv_a, recv_b, entry_ref, low_ref, sums_ref):
    normed, scale = norm_forward(inputs_ref[...])
    grad = second_ref[...] + (read([term_a, term_b], 2) + read([recv_a, recv_b], 2))
    entry = norm_backward(grad, normed, scale, pack_ref[1:2])
    entry_ref[...] = entry
    low_ref[...] = entry.astype(BF16)
    clear_first(sums_ref)
    add_rows(sums_ref, 0, entry)
    add_rows(sums_ref, 1, grad * normed)
    add_rows(sums_ref, 2, grad)


def entry(info, inputs, second, pack, back_terms, back_recv, deps=()):
    length, width = inputs.shape
    tile = tiled(length // 2, width)
    return launch(
        entry_kernel, info, [inputs, second, pack, *back_terms, *back_recv], [tile, tile] + [None] * 5,
        [kept((length, width), F32), sds((length, width), BF16), sds((8, width), F32)], [tile, tile, None], grid=2, deps=deps,
    )


def attend_back_kernel(info, rows_ref, proj_ref, ctx_ref, log_ref, low_ref, out_ref, grads_ref, dproj_ref, sums_ref, cgrad):
    length = rows_ref.shape[0]
    cols = ctx_ref.shape[0]
    low = low_ref[...]
    cgrad[...] = dot(out_ref[...], low, 1, 1).astype(BF16)
    scale = HEAD**-0.5

    @pl.loop(0, cols // HEAD, unroll=True)
    def _(head):
        query_rows, key_rows, value_rows = (pl.ds(pl.multiple_of(k * cols + head * HEAD, HEAD), HEAD) for k in range(3))
        keys = proj_ref[key_rows]
        values = proj_ref[value_rows]
        key_total = None
        value_total = None
        for block in range(length // QBLOCK):
            span = slice(block * QBLOCK, (block + 1) * QBLOCK)
            queries = proj_ref[query_rows, span] * BF16(scale)
            upstream = cgrad[query_rows, span]
            scores = dot(keys, queries, 0, 0)
            probs = jnp.exp(scores - log_ref[pl.ds(head, 1), span])
            value_term = dot(upstream, probs.astype(BF16), 1, 1)
            prob_grad = dot(values, upstream, 0, 0)
            inner = jnp.sum(prob_grad * probs, axis=0, keepdims=True)
            score_grad = (probs * (prob_grad - inner)).astype(BF16)
            dproj_ref[query_rows, span] = (dot(keys, score_grad, 1, 0) * scale).astype(BF16)
            key_term = dot(queries, score_grad, 1, 1)
            key_total = key_term if key_total is None else key_total + key_term
            value_total = value_term if value_total is None else value_total + value_term
        dproj_ref[key_rows] = key_total.astype(BF16)
        dproj_ref[value_rows] = value_total.astype(BF16)
    rows = rows_ref[...]
    grads_ref[: 3 * cols] = dot(dproj_ref[...], rows, 1, 0).astype(BF16)
    grads_ref[3 * cols :] = dot(ctx_ref[...], low, 1, 0).astype(BF16)
    sums_ref[...] = dot(jnp.ones((8, length), BF16), dproj_ref[...], 1, 1)


def attend_back(info, states, proj, ctx, log_total, low, out, deps=()):
    _, length, width = states.shape
    cols = ctx.shape[0]
    return launch(
        attend_back_kernel, info, [states, proj, ctx, log_total, low, out], [slot_rows(states, length)] + [None] * 5,
        [sds((4 * cols, width), BF16), sds((3 * cols, length), BF16), sds((8, 3 * cols), F32)], deps=deps,
        scratch=[pltpu.VMEM((cols, length), BF16)],
    )


def attend_back_heads(info, proj, log_total, low, out, first, last, deps=()):
    cols, length = proj.shape[0] // 3, proj.shape[1]
    scale = HEAD**-0.5

    def kernel(info, proj_ref, log_ref, low_ref, out_ref, dproj_ref):
        @pl.loop(0, last - first)
        def _(step):
            head = step + first
            at = lambda k: pl.ds(pl.multiple_of(k * cols + head * HEAD, HEAD), HEAD)
            into = lambda k: pl.ds(pl.multiple_of((3 * step + k) * HEAD, HEAD), HEAD)
            upstream_all = dot(out_ref[at(0)], low_ref[...], 1, 1).astype(BF16)
            keys, values = proj_ref[at(1)], proj_ref[at(2)]
            key_total = None
            value_total = None
            for block in range(length // QBLOCK):
                span = slice(block * QBLOCK, (block + 1) * QBLOCK)
                queries = proj_ref[at(0), span] * BF16(scale)
                upstream = upstream_all[:, span]
                scores = dot(keys, queries, 0, 0)
                probs = jnp.exp(scores - log_ref[pl.ds(head, 1), span])
                value_term = dot(upstream, probs.astype(BF16), 1, 1)
                prob_grad = dot(values, upstream, 0, 0)
                inner = jnp.sum(prob_grad * probs, axis=0, keepdims=True)
                score_grad = (probs * (prob_grad - inner)).astype(BF16)
                dproj_ref[into(0), span] = (dot(keys, score_grad, 1, 0) * scale).astype(BF16)
                key_term = dot(queries, score_grad, 1, 1)
                key_total = key_term if key_total is None else key_total + key_term
                value_total = value_term if value_total is None else value_total + value_term
            dproj_ref[into(1)] = key_total.astype(BF16)
            dproj_ref[into(2)] = value_total.astype(BF16)

    return launch(
        kernel, info, [proj, log_total, low, out], [None] * 4, [sds((3 * HEAD * (last - first), length), BF16)], deps=deps,
    )[0]


def sum_heads(info, states, ctx, low, base, recv, dprojs, deps=()):
    _, length, width = states.shape
    cols = ctx.shape[0]

    def kernel(info, rows_ref, ctx_ref, low_ref, base_ref, recv_ref, *refs):
        keep_ref, send_ref, dproj_ref, total, small = refs[-5:]
        head = 0
        for ref in refs[:-5]:
            for step in range(ref.shape[0] // (3 * HEAD)):
                for k in range(3):
                    at = (3 * step + k) * HEAD
                    dproj_ref[k * cols + head * HEAD : k * cols + (head + 1) * HEAD, :] = ref[at : at + HEAD, :]
                head += 1
        total[: 3 * cols] = (dot(dproj_ref[...], rows_ref[...], 1, 0) + wide(recv_ref[: 3 * cols])).astype(BF16)
        total[3 * cols :] = (dot(ctx_ref[...], low_ref[...], 1, 0) + wide(recv_ref[3 * cols :])).astype(BF16)
        sums = dot(jnp.ones((8, length), BF16), dproj_ref[...], 1, 1)[:1]
        small[...] = jnp.zeros_like(small)
        small[:8] = base_ref[...]
        small[7:8, : 2 * cols] += jnp.concatenate([sums[:, :cols], sums[:, 2 * cols :]], axis=1)
        half = total.shape[0] // 2
        for which, ref in ((info[2], keep_ref), (1 - info[2], send_ref)):
            ref[:half] = total[pl.ds(pl.multiple_of(which * half, 32), half), :]
            ref[half:] = small[...].astype(BF16)

    shape = sds((2 * cols + 32, width), BF16)
    return launch(
        kernel, info, [states, ctx, low, base, recv, *dprojs], [slot_rows(states, length)] + [None] * (4 + len(dprojs)),
        [shape, shape, sds((3 * cols, length), BF16)], deps=deps,
        scratch=[pltpu.VMEM((4 * cols, width), BF16), pltpu.VMEM((32, width), F32)],
    )


def build(mesh):
    n_dp, n_mp = mesh.shape["dp"], mesh.shape["mp"]
    n_z = n_dp // 2
    z_bits = []
    while n_mp * 2 << len(z_bits) < n_dp * n_mp:
        z_bits.append(n_mp * 2 << len(z_bits))

    def flip(value, bit):
        pairs = [(i, i ^ bit) for i in range(n_dp * n_mp)]
        return lax.ppermute(value, ("dp", "mp"), pairs)

    def swap(values):
        return [flip(v, CORE) for v in values]

    def body(
        states, span_count, qkv_weight, q_bias, v_bias, out_weight, out_bias, gain_one, shift_one,
        up_weight, up_bias, down_weight, down_bias, gain_two, shift_two, cotangent,
    ):
        dp, mp = lax.axis_index("dp"), lax.axis_index("mp")
        place = dp * n_mp + mp
        slot, core = mp // ROW, mp % ROW
        info = jnp.stack([slot, span_count[0], dp % 2, dp // 2]).astype(jnp.int32)
        width, _, cols = qkv_weight.shape
        units = up_weight.shape[1]

        token = [place]

        def halves(value, bit):
            side = (token[0] // bit) % 2
            rows = value.shape[0] // 2
            return tuple(lax.dynamic_slice_in_dim(value, w * rows, rows, 0) for w in (side, 1 - side))

        def add(one, two):
            return (wide(one) + wide(two)).astype(BF16)

        def join(value, bit):
            other = flip(value, bit)
            lower = (token[0] // bit) % 2 == 0
            return jnp.concatenate([jnp.where(lower, value, other), jnp.where(lower, other, value)], axis=0)

        def sync(*values):
            token[0], values = lax.optimization_barrier((token[0], values))
            return values

        def put_together(value, other, bit):
            lower = (token[0] // bit) % 2 == 0
            return jnp.concatenate([jnp.where(lower, value, other), jnp.where(lower, other, value)], axis=0)

        z_near, z_far = n_mp * 2, n_mp * 4

        def z_one(value):
            if n_z == 4:
                mine, theirs = halves(value, z_near)
                return mine, flip(theirs, z_near)
            for bit in z_bits:
                value = add(value, flip(value, bit))
            return value, value

        def z_two(pair):
            if n_z != 4:
                return pair
            value = add(*pair)
            return value, flip(value, z_far)

        def z_three(pair):
            if n_z != 4:
                return pair
            value = add(*pair)
            return value, flip(value, z_near)

        def z_end(pair):
            return put_together(*pair, z_near) if n_z == 4 else pair[0]

        def side_start(value):
            return value, flip(value, SIDE)

        joined = jnp.concatenate([q_bias, v_bias, jnp.zeros((width - 2 * cols,), F32)])
        pack = jnp.stack([out_bias, gain_one, shift_one, down_bias, gain_two, shift_two, up_bias, joined])
        qkv = qkv_weight.transpose(1, 2, 0).reshape(3 * cols, width)
        out = out_weight.T
        pack_o = flip(pack, ROW)
        qkv_o = flip(qkv, ROW)

        proj, ctx, logs = attend(info, states, qkv, pack)
        third = units // 3
        side = dp % 2
        cut = lambda w, at: lax.dynamic_slice_in_dim(w, at, third, 1)
        outer = jnp.concatenate([cut(up_weight, 2 * third * side), cut(down_weight, 2 * third * side)], axis=0)
        middle = jnp.concatenate([up_weight[:, third : 2 * third], down_weight[:, third : 2 * third]], axis=0)
        outer, middle, qkv_o, pack_o, out_send, _ = lax.optimization_barrier((outer, middle, qkv_o, pack_o, out, logs))
        outer = flip(outer, ROW)
        out_o = flip(out_send, ROW)
        proj_o, ctx_o, logs_o = attend(info, states, qkv_o, pack_o, deps=[logs])
        middle, ctx_o, outer = lax.optimization_barrier((middle, ctx_o, outer))
        middle = flip(middle, ROW)
        forwarded = flip(outer, SIDE)
        terms = project(info, ctx, ctx_o, out, out_o, 8)
        recv = swap(terms)
        first, low, act, slope, part, entry_in = feed_own(
            info, states, terms, recv, pack, up_weight, down_weight,
        )
        pieces = [outer, middle, forwarded]
        act_o, slope_o, *feed_terms = feed_other(info, low, part, pieces, pack_o)
        out_rows, second, branch_low, sums_two = turn(
            info, first, feed_terms, swap(feed_terms), cotangent, pack,
        )

        def half_rows(span):
            size = span.shape[0] // 2
            return lax.dynamic_slice_in_dim(span, core * size, size, 0)

        def both_spans(span, got, again):
            other = put_together(got, again, CORE)
            return put_together(span[None], other[None], ROW)

        fence = lambda *v: lax.optimization_barrier(v)
        down_keep, down_send = cross(info, branch_low, act, act_o)
        down_recv = flip(down_send, SIDE)
        hidden, back_part = back_own(info, branch_low, slope, up_weight, down_weight, deps=[down_keep])
        hidden_o, *back_terms = back_other(info, branch_low, slope_o, back_part, pieces)
        back_recv = swap(back_terms)
        up_own, up_other, unit_sums, unit_sums_o = plain_cross(info, low, hidden, hidden_o)
        up_recv = flip(up_other, ROW)
        entry_grad, attn_low, sums_one = entry(info, pltpu.with_memory_space_constraint(entry_in, pltpu.HBM), pltpu.with_memory_space_constraint(second, pltpu.HBM), pack, back_terms, back_recv, deps=[up_own, down_recv])

        attn_low, down_keep, down_recv = sync(attn_low, down_keep, down_recv)
        down_other = add(down_keep[1], down_recv[1])
        down = down_keep, down_recv, flip(down_other, ROW)
        heads_other, dproj_o, head_sums_o = attend_back(
            info, states, proj_o, ctx_o, logs_o, attn_low, out_o, deps=[down_other],
        )

        heads_other, up_own, up_recv, attn_low = sync(heads_other, up_own, up_recv, attn_low)
        heads_recv = flip(heads_other, ROW)
        up_keep, up_send = halves(add(up_own, up_recv), SIDE)
        up = up_keep, flip(up_send, SIDE)
        dprojs = [attend_back_heads(info, far(proj), logs, far(attn_low), far(out), 0, 1, deps=[up_send, heads_other])]

        dprojs, down, attn_low = sync(dprojs, down, attn_low)
        down = z_one((wide(down[0][0]) + wide(down[1][0]) + wide(down[2])).astype(BF16))
        common = [sums_one[:3], sums_two[2:3], sums_two[:2]]
        fill = jnp.zeros((1, width - 2 * cols), F32)
        rows_of = lambda units_row, heads_row: jnp.concatenate(common + [units_row[:1], heads_row], axis=0)
        heads_row_o = jnp.concatenate([head_sums_o[:1, :cols], head_sums_o[:1, 2 * cols :], fill], axis=1)
        small_recv = flip(rows_of(unit_sums_o, heads_row_o), ROW)
        dprojs = [*dprojs, attend_back_heads(info, far(proj), logs, far(attn_low), far(out), 1, cols // HEAD, deps=[down[0]])]

        base = rows_of(unit_sums, jnp.zeros((1, width), F32))
        dprojs, heads_recv, small_recv, base, attn_low = sync(dprojs, heads_recv, small_recv, base, attn_low)
        heads_keep, heads_send, dproj = sum_heads(info, states, ctx, far(attn_low), base + small_recv, heads_recv, [(d) for d in dprojs])
        small = jnp.zeros((32, width), BF16)
        heads = heads_keep, flip(heads_send, SIDE)

        down, up, dproj, heads_send = sync(down, up, dproj, heads_send)
        down = z_two(down)
        up = z_one(add(*up))
        in_terms = project(info, dproj, dproj_o, qkv, qkv_o, 4, deps=[heads_send, down[0], up[0]])
        in_recv = swap(in_terms)

        heads, down, up, in_terms = sync(heads, down, up, in_terms)
        heads = z_one(add(*heads))
        down = z_three(down)
        up = z_two(up)
        out_rows, = sync(out_rows)
        in_rows = jnp.concatenate([wide(a) + wide(b) for a, b in zip(in_terms, in_recv)], axis=0)
        in_rows = (entry_grad + in_rows).astype(BF16)
        in_got = flip(half_rows(in_rows), ROW)

        heads, down, up = sync(heads, down, up)
        heads = z_two(heads)
        down = side_start(z_end(down))
        up = z_three(up)
        out_got = flip(half_rows(out_rows), ROW)

        heads, up, in_got = sync(heads, up, in_got)
        heads = z_three(heads)
        up = side_start(z_end(up))
        in_again = flip(in_got, CORE)

        heads, = sync(heads)
        heads = z_end(heads)
        half = heads.shape[0] - small.shape[0]
        heads, small = heads[:half], heads[half:]
        heads = side_start(heads)

        down, out_got = sync(down, out_got)
        down_out = wide(put_together(*down, SIDE))
        out_again = flip(out_got, CORE)

        up, in_again, out_again = sync(up, in_again, out_again)
        up_out = wide(put_together(*up, SIDE))
        states_grad = both_spans(in_rows, in_got, in_again)
        states_out = both_spans(out_rows, out_got, out_again)

        heads, up_out, down_out, states_grad, states_out = sync(heads, up_out, down_out, states_grad, states_out)
        heads_out = wide(put_together(*heads, SIDE))
        qkv_out, out_out = heads_out[: 3 * cols], heads_out[3 * cols :]
        small = wide(small)
        parts = [small[k] for k in range(7)] + [small[7, :cols], small[7, cols : 2 * cols]]
        qkv_out = qkv_out.reshape(3, cols, width).transpose(2, 0, 1)
        return (
            states_out, states_grad, qkv_out, parts[7], parts[8], out_out.T, parts[0], parts[1], parts[2],
            up_out, parts[6], down_out, parts[3], parts[4], parts[5],
        )

    return body


def solution(mesh):
    split = P("dp", None, None)
    in_specs = (
        split, P("dp"), P(None, None, "mp"), P("mp"), P("mp"), P(None, "mp"), P(), P(), P(),
        P(None, "mp"), P("mp"), P(None, "mp"), P(), P(), P(), split,
    )
    out_specs = (
        split, split, P(None, None, "mp"), P("mp"), P("mp"), P(None, "mp"), P(), P(), P(),
        P(None, "mp"), P("mp"), P(None, "mp"), P(), P(), P(),
    )
    return jax.shard_map(build(mesh), mesh=mesh, in_specs=in_specs, out_specs=out_specs, check_vma=False)
```

```python
import jax
import jax.numpy as jnp
from jax import lax
from jax.experimental import pallas as pl
from jax.experimental.pallas import tpu as pltpu
from jax.sharding import PartitionSpec as P

HEAD = 64
EPS = 1e-05
F32 = jnp.float32
BF16 = jnp.bfloat16
LIMIT = 24 * 2**20
QBLOCK = 1024
CORE, ROW, SIDE = 1, 2, 4


def dot(a, b, ca, cb):
    return lax.dot_general(a, b, (((ca,), (cb,)), ((), ())), preferred_element_type=F32)


def sds(shape, dtype):
    return jax.ShapeDtypeStruct(shape, dtype)


def whole(array):
    shape = array.shape
    return pl.BlockSpec(shape, lambda i, s: (0,) * len(shape))


def tiled(rows, cols):
    return pl.BlockSpec((rows, cols), lambda i, s: (i, 0))


def slot_rows(array, rows):
    return pl.BlockSpec((None, rows, array.shape[2]), lambda i, s: (s[0], i, 0))


def launch(kernel, info, args, in_specs, out_shapes, out_specs=None, grid=1, deps=(), scratch=(), limit=LIMIT):
    count, extra = len(args), len(deps)

    def inner(info_ref, *refs):
        kernel(info_ref, *refs[:count], *refs[count + extra :])

    specs = [whole(a) if s is None else s for a, s in zip(args, in_specs)]
    out_specs = [None] * len(out_shapes) if out_specs is None else out_specs
    return pl.pallas_call(
        inner,
        out_shape=out_shapes,
        grid_spec=pltpu.PrefetchScalarGridSpec(
            num_scalar_prefetch=1,
            grid=(grid,),
            in_specs=specs + [pl.BlockSpec(memory_space=pl.ANY)] * extra,
            out_specs=[whole(a) if s is None else s for a, s in zip(out_shapes, out_specs)],
            scratch_shapes=scratch,
        ),
        compiler_params=pltpu.CompilerParams(vmem_limit_bytes=limit),
        cost_estimate=pl.CostEstimate(flops=1, bytes_accessed=0, transcendentals=0),
    )(info, *args, *deps)


def far(value):
    return pltpu.with_memory_space_constraint(value, pltpu.HBM)


def norm_forward(inputs):
    centre = inputs - jnp.mean(inputs, axis=-1, keepdims=True)
    spread = jnp.mean(centre * centre, axis=-1, keepdims=True)
    scale = lax.rsqrt(spread + EPS)
    return centre * scale, scale


def norm_backward(grad, normed, scale, gain):
    scaled = grad * gain
    mean_one = jnp.mean(scaled, axis=-1, keepdims=True)
    mean_two = jnp.mean(scaled * normed, axis=-1, keepdims=True)
    return scale * (scaled - mean_one - normed * mean_two)


def column(row, width):
    return jnp.broadcast_to(row, (width, row.shape[1])).T[:, :1]


def wide(value):
    return value.astype(F32)


def attend_kernel(info, rows_ref, weight_ref, pack_ref, proj_ref, ctx_ref, log_ref):
    rows = rows_ref[...]
    cols = weight_ref.shape[0] // 3
    q_bias = column(pack_ref[7:8, :cols], 128)
    v_bias = column(pack_ref[7:8, cols : 2 * cols], 128)
    proj_ref[:cols] = (dot(weight_ref[:cols], rows, 1, 1) + q_bias).astype(BF16)
    proj_ref[cols : 2 * cols] = dot(weight_ref[cols : 2 * cols], rows, 1, 1).astype(BF16)
    proj_ref[2 * cols :] = (dot(weight_ref[2 * cols :], rows, 1, 1) + v_bias).astype(BF16)
    length = rows.shape[0]

    @pl.loop(0, cols // HEAD)
    def _(head):
        rows_of = lambda base: pl.ds(pl.multiple_of(base + head * HEAD, HEAD), HEAD)
        keys = proj_ref[rows_of(cols)]
        values = proj_ref[rows_of(2 * cols)]
        for block in range(length // QBLOCK):
            span = slice(block * QBLOCK, (block + 1) * QBLOCK)
            queries = proj_ref[rows_of(0), span] * BF16(HEAD**-0.5)
            scores = dot(keys, queries, 0, 0)
            highest = jnp.max(scores, axis=0, keepdims=True)
            raised = jnp.exp(scores - highest)
            totals = jnp.sum(raised, axis=0, keepdims=True)
            probs = (raised * (1.0 / totals)).astype(BF16)
            ctx_ref[rows_of(0), span] = dot(values, probs, 1, 0).astype(BF16)
            log_ref[pl.ds(head, 1), span] = highest + jnp.log(totals)


def attend(info, states, weight, pack, deps=()):
    length = states.shape[1]
    cols = weight.shape[0] // 3
    return launch(
        attend_kernel, info, [states, weight, pack], [slot_rows(states, length), None, None],
        [kept((3 * cols, length), BF16), sds((cols, length), BF16), sds((8, length), F32)], deps=deps,
    )


def project_kernel(info, left_ref, left_o_ref, right_ref, right_o_ref, *out_refs):
    size = out_refs[0].shape[0]
    for part, into in enumerate(out_refs):
        span = slice(part * size, (part + 1) * size)
        terms = dot(left_ref[:, span], right_ref[...], 0, 0) + dot(left_o_ref[:, span], right_o_ref[...], 0, 0)
        into[...] = terms.astype(BF16)


def project(info, left, left_o, right, right_o, count, deps=()):
    return launch(
        project_kernel, info, [left, left_o, right, right_o], [None] * 4, chunks(left.shape[1], right.shape[1], count), deps=deps,
    )


def read(refs, steps):
    per = len(refs) // steps
    step = pl.program_id(0)
    parts = []
    for t in range(per):
        value = refs[t][...]
        for k in range(1, steps):
            value = jnp.where(step == k, refs[k * per + t][...], value)
        parts.append(value)
    return wide(jnp.concatenate(parts, axis=0) if per > 1 else parts[0])


def write(refs, steps, value):
    per, rows = max(len(refs) // steps, 1), value.shape[0]
    for k in range(steps):

        @pl.when(pl.program_id(0) == k)
        def _():
            if len(refs) < steps:
                at = k % (steps // len(refs)) * rows
                refs[k * len(refs) // steps][at : at + rows] = value
            else:
                for t in range(per):
                    refs[k * per + t][...] = value[t * rows // per : (t + 1) * rows // per]


def chunks(length, width, count):
    return [sds((length // count, width), BF16)] * count


def kept(shape, dtype):
    return pltpu.HBM(shape, dtype)


def unit_pass(low, up_ref, pack_ref, down_ref, act_ref, slope_ref):
    total = None
    half = up_ref.shape[1] // 2
    for part in range(2):
        cols = slice(part * half, (part + 1) * half)
        hidden = dot(low, up_ref[:, cols], 1, 0) + pack_ref[6:7, cols]
        cdf = 0.5 + 0.5 * lax.erf(hidden * (0.5**0.5))
        pdf = jnp.exp(hidden * hidden * -0.5) * ((2 * jnp.pi) ** -0.5)
        act = (hidden * cdf).astype(BF16)
        act_ref[:, cols] = act
        slope_ref[:, cols] = (cdf + hidden * pdf).astype(BF16)
        term = dot(act, down_ref[:, cols], 1, 1)
        total = term if total is None else total + term
    return total


def feed_own_kernel(info, rows_ref, pack_ref, up_ref, down_ref, *refs):
    first_ref, low_ref, act_ref, slope_ref, part_ref, entry_ref = refs[-6:]
    count = (len(refs) - 6) // 2
    inputs = wide(rows_ref[...]) + (read(refs[:count], 4) + read(refs[count : 2 * count], 4) + pack_ref[0:1])
    entry_ref[...] = inputs
    normed, _ = norm_forward(inputs)
    first = normed * pack_ref[1:2] + pack_ref[2:3]
    first_ref[...] = first
    low = first.astype(BF16)
    low_ref[...] = low
    part_ref[...] = unit_pass(low, up_ref, pack_ref, down_ref, act_ref, slope_ref)


def feed_own(info, states, terms, recv, pack, up, down, deps=()):
    _, length, width = states.shape
    half, units = length // 4, up.shape[1]
    return launch(
        feed_own_kernel, info, [states, pack, up, down, *terms, *recv],
        [slot_rows(states, half)] + [None] * (3 + 2 * len(terms)),
        [sds((length, width), F32), sds((length, width), BF16), sds((length, units), BF16), sds((length, units), BF16), sds((length, width), F32), kept((length, width), F32)],
        [tiled(half, width), tiled(half, width), tiled(half, units), tiled(half, units), tiled(half, width), tiled(half, width)], grid=4, deps=deps,
    )


def places(info, size):
    return [pl.multiple_of(2 * size * info[2], 128), size, pl.multiple_of(2 * size * (1 - info[2]), 128)]


def feed_other_kernel(info, low_ref, part_ref, pack_ref, *refs):
    act_ref, slope_ref = refs[3:5]
    low = low_ref[...]
    total = part_ref[...]
    size = refs[0].shape[1]
    width = low.shape[1]
    for ref, place in zip(refs[:3], places(info, size)):
        cols = pl.ds(place, size)
        hidden = dot(low, ref[:width], 1, 0) + pack_ref[6:7, cols]
        cdf = 0.5 + 0.5 * lax.erf(hidden * (0.5**0.5))
        pdf = jnp.exp(hidden * hidden * -0.5) * ((2 * jnp.pi) ** -0.5)
        act = (hidden * cdf).astype(BF16)
        act_ref[:, cols] = act
        slope_ref[:, cols] = (cdf + hidden * pdf).astype(BF16)
        total = total + dot(act, ref[width:], 1, 1)
    write(refs[5:], 4, total.astype(BF16))


def feed_other(info, low, part, pieces, pack, deps=()):
    length, width = low.shape
    half, units = length // 4, 3 * pieces[0].shape[1]
    return launch(
        feed_other_kernel, info, [low, part, pack, *pieces],
        [tiled(half, width), tiled(half, width), None, None, None, None],
        [sds((length, units), BF16), sds((length, units), BF16)] + chunks(length, width, 2),
        [tiled(half, units), tiled(half, units), None, None], grid=4, deps=deps,
    )


def add_rows(ref, row, value):
    ref[row : row + 1, :] += jnp.sum(value, axis=0, keepdims=True)


def clear_first(ref):
    @pl.when(pl.program_id(0) == 0)
    def _():
        ref[...] = jnp.zeros_like(ref)


def turn_kernel(info, first_ref, *refs):
    terms, recv = refs[:2], refs[2:4]
    cot_ref, pack_ref, out_ref, grad_ref, low_ref, sums_ref = refs[4:]
    live = jnp.where(info[0] < info[1], 1.0, 0.0).astype(F32)
    branch = read(terms, 2) + read(recv, 2) + pack_ref[3:4]
    normed, scale = norm_forward(first_ref[...] + branch)
    out_ref[...] = ((normed * pack_ref[4:5] + pack_ref[5:6]) * live).astype(BF16)
    upstream = wide(cot_ref[...]) * live
    grad = norm_backward(upstream, normed, scale, pack_ref[4:5])
    grad_ref[...] = grad
    low_ref[...] = grad.astype(BF16)
    clear_first(sums_ref)
    add_rows(sums_ref, 0, upstream * normed)
    add_rows(sums_ref, 1, upstream)
    add_rows(sums_ref, 2, grad)


def turn(info, first, terms, recv, cotangent, pack, deps=()):
    length, width = first.shape
    half = length // 2
    tile = tiled(half, width)
    return launch(
        turn_kernel, info, [first, *terms, *recv, cotangent, pack],
        [tile] + [None] * 4 + [slot_rows(cotangent, half), None],
        [kept((length, width), BF16), kept((length, width), F32), sds((length, width), BF16), sds((8, width), F32)],
        [tile, tile, tile, None], grid=2, deps=deps,
    )


def cross_kernel(info, left_ref, right_ref, right_o_ref, keep_ref, send_ref):
    side = info[2]
    half = keep_ref.shape[1]
    for which, ref in ((side, keep_ref), (1 - side, send_ref)):
        left = left_ref[:, pl.ds(pl.multiple_of(which * half, 128), half)]
        ref[0] = dot(left, right_ref[...], 0, 0).astype(BF16)
        ref[1] = dot(left, right_o_ref[...], 0, 0).astype(BF16)


def cross(info, left, right, right_o, deps=()):
    shape = sds((2, left.shape[1] // 2, right.shape[1]), BF16)
    return launch(cross_kernel, info, [left, right, right_o], [None] * 3, [shape, shape], deps=deps)


def plain_cross_kernel(info, left_ref, right_ref, right_o_ref, own_ref, other_ref, sums_ref, sums_o_ref):
    ones = jnp.ones((8, right_ref.shape[0]), BF16)
    for right, into, sums in ((right_ref, own_ref, sums_ref), (right_o_ref, other_ref, sums_o_ref)):
        into[...] = dot(left_ref[...], right[...], 0, 0).astype(BF16)
        sums[...] = dot(ones, right[...], 1, 0)


def plain_cross(info, left, right, right_o, deps=()):
    shape = sds((left.shape[1], right.shape[1]), BF16)
    sums = sds((8, right.shape[1]), F32)
    return launch(plain_cross_kernel, info, [left, right, right_o], [None] * 3, [shape, shape, sums, sums], deps=deps)


def back_own_kernel(info, low_ref, slope_ref, up_ref, down_ref, hidden_ref, part_ref):
    low = low_ref[...]
    half = up_ref.shape[1] // 2
    total = None
    for part in range(2):
        cols = slice(part * half, (part + 1) * half)
        hidden = (wide(slope_ref[:, cols]) * dot(low, down_ref[:, cols], 1, 0)).astype(BF16)
        hidden_ref[:, cols] = hidden
        term = dot(hidden, up_ref[:, cols], 1, 1)
        total = term if total is None else total + term
    part_ref[...] = total


def back_own(info, low, slope, up, down, deps=()):
    length, width = low.shape
    half, units = length // 4, slope.shape[1]
    return launch(
        back_own_kernel, info, [low, slope, up, down], [tiled(half, width), tiled(half, units), None, None],
        [sds((length, units), BF16), sds((length, width), F32)], [tiled(half, units), tiled(half, width)], grid=4, deps=deps,
    )


def back_other_kernel(info, low_ref, slope_ref, part_ref, *refs):
    hidden_ref = refs[3]
    low = low_ref[...]
    width = low.shape[1]
    size = refs[0].shape[1]
    total = part_ref[...]
    for ref, place in zip(refs[:3], places(info, size)):
        cols = pl.ds(place, size)
        hidden = (wide(slope_ref[:, cols]) * dot(low, ref[width:], 1, 0)).astype(BF16)
        hidden_ref[:, cols] = hidden
        total = total + dot(hidden, ref[:width], 1, 1)
    write(refs[4:], 4, total.astype(BF16))


def back_other(info, low, slope, part, pieces, deps=()):
    length, width = low.shape
    half, units = length // 4, slope.shape[1]
    return launch(
        back_other_kernel, info, [low, slope, part, *pieces],
        [tiled(half, width), tiled(half, units), tiled(half, width), None, None, None],
        [sds((length, units), BF16)] + chunks(length, width, 2), [tiled(half, units), None, None], grid=4, deps=deps,
    )


def entry_kernel(info, inputs_ref, second_ref, pack_ref, term_a, term_b, recv_a, recv_b, entry_ref, low_ref, sums_ref):
    normed, scale = norm_forward(inputs_ref[...])
    grad = second_ref[...] + (read([term_a, term_b], 2) + read([recv_a, recv_b], 2))
    entry = norm_backward(grad, normed, scale, pack_ref[1:2])
    entry_ref[...] = entry
    low_ref[...] = entry.astype(BF16)
    clear_first(sums_ref)
    add_rows(sums_ref, 0, entry)
    add_rows(sums_ref, 1, grad * normed)
    add_rows(sums_ref, 2, grad)


def entry(info, inputs, second, pack, back_terms, back_recv, deps=()):
    length, width = inputs.shape
    tile = tiled(length // 2, width)
    return launch(
        entry_kernel, info, [inputs, second, pack, *back_terms, *back_recv], [tile, tile] + [None] * 5,
        [kept((length, width), F32), sds((length, width), BF16), sds((8, width), F32)], [tile, tile, None], grid=2, deps=deps,
    )


def attend_back_kernel(info, rows_ref, proj_ref, ctx_ref, log_ref, low_ref, out_ref, grads_ref, dproj_ref, sums_ref, cgrad):
    length = rows_ref.shape[0]
    cols = ctx_ref.shape[0]
    low = low_ref[...]
    cgrad[...] = dot(out_ref[...], low, 1, 1).astype(BF16)
    scale = HEAD**-0.5

    @pl.loop(0, cols // HEAD, unroll=True)
    def _(head):
        query_rows, key_rows, value_rows = (pl.ds(pl.multiple_of(k * cols + head * HEAD, HEAD), HEAD) for k in range(3))
        keys = proj_ref[key_rows]
        values = proj_ref[value_rows]
        key_total = None
        value_total = None
        for block in range(length // QBLOCK):
            span = slice(block * QBLOCK, (block + 1) * QBLOCK)
            queries = proj_ref[query_rows, span] * BF16(scale)
            upstream = cgrad[query_rows, span]
            scores = dot(keys, queries, 0, 0)
            probs = jnp.exp(scores - log_ref[pl.ds(head, 1), span])
            value_term = dot(upstream, probs.astype(BF16), 1, 1)
            prob_grad = dot(values, upstream, 0, 0)
            inner = jnp.sum(prob_grad * probs, axis=0, keepdims=True)
            score_grad = (probs * (prob_grad - inner)).astype(BF16)
            dproj_ref[query_rows, span] = (dot(keys, score_grad, 1, 0) * scale).astype(BF16)
            key_term = dot(queries, score_grad, 1, 1)
            key_total = key_term if key_total is None else key_total + key_term
            value_total = value_term if value_total is None else value_total + value_term
        dproj_ref[key_rows] = key_total.astype(BF16)
        dproj_ref[value_rows] = value_total.astype(BF16)
    rows = rows_ref[...]
    grads_ref[: 3 * cols] = dot(dproj_ref[...], rows, 1, 0).astype(BF16)
    grads_ref[3 * cols :] = dot(ctx_ref[...], low, 1, 0).astype(BF16)
    sums_ref[...] = dot(jnp.ones((8, length), BF16), dproj_ref[...], 1, 1)


def attend_back(info, states, proj, ctx, log_total, low, out, deps=()):
    _, length, width = states.shape
    cols = ctx.shape[0]
    return launch(
        attend_back_kernel, info, [states, proj, ctx, log_total, low, out], [slot_rows(states, length)] + [None] * 5,
        [sds((4 * cols, width), BF16), sds((3 * cols, length), BF16), sds((8, 3 * cols), F32)], deps=deps,
        scratch=[pltpu.VMEM((cols, length), BF16)],
    )


def attend_back_heads(info, proj, log_total, low, out, first, last, deps=()):
    cols, length = proj.shape[0] // 3, proj.shape[1]
    scale = HEAD**-0.5

    def kernel(info, proj_ref, log_ref, low_ref, out_ref, dproj_ref):
        @pl.loop(0, last - first)
        def _(step):
            head = step + first
            at = lambda k: pl.ds(pl.multiple_of(k * cols + head * HEAD, HEAD), HEAD)
            into = lambda k: pl.ds(pl.multiple_of((3 * step + k) * HEAD, HEAD), HEAD)
            upstream_all = dot(out_ref[at(0)], low_ref[...], 1, 1).astype(BF16)
            keys, values = proj_ref[at(1)], proj_ref[at(2)]
            key_total = None
            value_total = None
            for block in range(length // QBLOCK):
                span = slice(block * QBLOCK, (block + 1) * QBLOCK)
                queries = proj_ref[at(0), span] * BF16(scale)
                upstream = upstream_all[:, span]
                scores = dot(keys, queries, 0, 0)
                probs = jnp.exp(scores - log_ref[pl.ds(head, 1), span])
                value_term = dot(upstream, probs.astype(BF16), 1, 1)
                prob_grad = dot(values, upstream, 0, 0)
                inner = jnp.sum(prob_grad * probs, axis=0, keepdims=True)
                score_grad = (probs * (prob_grad - inner)).astype(BF16)
                dproj_ref[into(0), span] = (dot(keys, score_grad, 1, 0) * scale).astype(BF16)
                key_term = dot(queries, score_grad, 1, 1)
                key_total = key_term if key_total is None else key_total + key_term
                value_total = value_term if value_total is None else value_total + value_term
            dproj_ref[into(1)] = key_total.astype(BF16)
            dproj_ref[into(2)] = value_total.astype(BF16)

    return launch(
        kernel, info, [proj, log_total, low, out], [None] * 4, [sds((3 * HEAD * (last - first), length), BF16)], deps=deps,
    )[0]


def sum_heads(info, states, ctx, low, base, recv, dprojs, deps=()):
    _, length, width = states.shape
    cols = ctx.shape[0]

    def kernel(info, rows_ref, ctx_ref, low_ref, base_ref, recv_ref, *refs):
        keep_ref, send_ref, dproj_ref, total, small = refs[-5:]
        head = 0
        for ref in refs[:-5]:
            for step in range(ref.shape[0] // (3 * HEAD)):
                for k in range(3):
                    at = (3 * step + k) * HEAD
                    dproj_ref[k * cols + head * HEAD : k * cols + (head + 1) * HEAD, :] = ref[at : at + HEAD, :]
                head += 1
        total[: 3 * cols] = (dot(dproj_ref[...], rows_ref[...], 1, 0) + wide(recv_ref[: 3 * cols])).astype(BF16)
        total[3 * cols :] = (dot(ctx_ref[...], low_ref[...], 1, 0) + wide(recv_ref[3 * cols :])).astype(BF16)
        sums = dot(jnp.ones((8, length), BF16), dproj_ref[...], 1, 1)[:1]
        small[...] = jnp.zeros_like(small)
        small[:8] = base_ref[...]
        small[7:8, : 2 * cols] += jnp.concatenate([sums[:, :cols], sums[:, 2 * cols :]], axis=1)
        half = total.shape[0] // 2
        for which, ref in ((info[2], keep_ref), (1 - info[2], send_ref)):
            ref[:half] = total[pl.ds(pl.multiple_of(which * half, 32), half), :]
            ref[half:] = small[...].astype(BF16)

    shape = sds((2 * cols + 32, width), BF16)
    return launch(
        kernel, info, [states, ctx, low, base, recv, *dprojs], [slot_rows(states, length)] + [None] * (4 + len(dprojs)),
        [shape, shape, sds((3 * cols, length), BF16)], deps=deps,
        scratch=[pltpu.VMEM((4 * cols, width), BF16), pltpu.VMEM((32, width), F32)],
    )


def build(mesh):
    n_dp, n_mp = mesh.shape["dp"], mesh.shape["mp"]
    n_z = n_dp // 2
    z_bits = []
    while n_mp * 2 << len(z_bits) < n_dp * n_mp:
        z_bits.append(n_mp * 2 << len(z_bits))

    def flip(value, bit):
        pairs = [(i, i ^ bit) for i in range(n_dp * n_mp)]
        return lax.ppermute(value, ("dp", "mp"), pairs)

    def swap(values):
        return [flip(v, CORE) for v in values]

    def body(
        states, span_count, qkv_weight, q_bias, v_bias, out_weight, out_bias, gain_one, shift_one,
        up_weight, up_bias, down_weight, down_bias, gain_two, shift_two, cotangent,
    ):
        dp, mp = lax.axis_index("dp"), lax.axis_index("mp")
        place = dp * n_mp + mp
        slot, core = mp // ROW, mp % ROW
        info = jnp.stack([slot, span_count[0], dp % 2, dp // 2]).astype(jnp.int32)
        width, _, cols = qkv_weight.shape
        units = up_weight.shape[1]

        token = [place]

        def halves(value, bit):
            side = (token[0] // bit) % 2
            rows = value.shape[0] // 2
            return tuple(lax.dynamic_slice_in_dim(value, w * rows, rows, 0) for w in (side, 1 - side))

        def add(one, two):
            return (wide(one) + wide(two)).astype(BF16)

        def join(value, bit):
            other = flip(value, bit)
            lower = (token[0] // bit) % 2 == 0
            return jnp.concatenate([jnp.where(lower, value, other), jnp.where(lower, other, value)], axis=0)

        def sync(*values):
            token[0], values = lax.optimization_barrier((token[0], values))
            return values

        def put_together(value, other, bit):
            lower = (token[0] // bit) % 2 == 0
            return jnp.concatenate([jnp.where(lower, value, other), jnp.where(lower, other, value)], axis=0)

        z_near, z_far = n_mp * 2, n_mp * 4

        def z_one(value):
            if n_z == 4:
                mine, theirs = halves(value, z_near)
                return mine, flip(theirs, z_near)
            for bit in z_bits:
                value = add(value, flip(value, bit))
            return value, value

        def z_two(pair):
            if n_z != 4:
                return pair
            value = add(*pair)
            return value, flip(value, z_far)

        def z_three(pair):
            if n_z != 4:
                return pair
            value = add(*pair)
            return value, flip(value, z_near)

        def z_end(pair):
            return put_together(*pair, z_near) if n_z == 4 else pair[0]

        def side_start(value):
            return value, flip(value, SIDE)

        joined = jnp.concatenate([q_bias, v_bias, jnp.zeros((width - 2 * cols,), F32)])
        pack = jnp.stack([out_bias, gain_one, shift_one, down_bias, gain_two, shift_two, up_bias, joined])
        qkv = qkv_weight.transpose(1, 2, 0).reshape(3 * cols, width)
        out = out_weight.T
        pack_o = flip(pack, ROW)
        qkv_o = flip(qkv, ROW)

        proj, ctx, logs = attend(info, states, qkv, pack)
        third = units // 3
        side = dp % 2
        cut = lambda w, at: lax.dynamic_slice_in_dim(w, at, third, 1)
        outer = jnp.concatenate([cut(up_weight, 2 * third * side), cut(down_weight, 2 * third * side)], axis=0)
        middle = jnp.concatenate([up_weight[:, third : 2 * third], down_weight[:, third : 2 * third]], axis=0)
        outer, middle, qkv_o, pack_o, out_send, _ = lax.optimization_barrier((outer, middle, qkv_o, pack_o, out, logs))
        outer = flip(outer, ROW)
        out_o = flip(out_send, ROW)
        proj_o, ctx_o, logs_o = attend(info, states, qkv_o, pack_o, deps=[logs])
        middle, ctx_o, outer = lax.optimization_barrier((middle, ctx_o, outer))
        middle = flip(middle, ROW)
        forwarded = flip(outer, SIDE)
        terms = project(info, ctx, ctx_o, out, out_o, 8)
        recv = swap(terms)
        first, low, act, slope, part, entry_in = feed_own(
            info, states, terms, recv, pack, up_weight, down_weight,
        )
        pieces = [outer, middle, forwarded]
        act_o, slope_o, *feed_terms = feed_other(info, low, part, pieces, pack_o)
        out_rows, second, branch_low, sums_two = turn(
            info, first, feed_terms, swap(feed_terms), cotangent, pack,
        )

        def half_rows(span):
            size = span.shape[0] // 2
            return lax.dynamic_slice_in_dim(span, core * size, size, 0)

        def both_spans(span, got, again):
            other = put_together(got, again, CORE)
            return put_together(span[None], other[None], ROW)

        fence = lambda *v: lax.optimization_barrier(v)
        down_keep, down_send = cross(info, branch_low, act, act_o)
        down_recv = flip(down_send, SIDE)
        hidden, back_part = back_own(info, branch_low, slope, up_weight, down_weight, deps=[down_keep])
        hidden_o, *back_terms = back_other(info, branch_low, slope_o, back_part, pieces)
        back_recv = swap(back_terms)
        up_own, up_other, unit_sums, unit_sums_o = plain_cross(info, low, hidden, hidden_o)
        up_recv = flip(up_other, ROW)
        entry_grad, attn_low, sums_one = entry(info, pltpu.with_memory_space_constraint(entry_in, pltpu.HBM), pltpu.with_memory_space_constraint(second, pltpu.HBM), pack, back_terms, back_recv, deps=[up_own])

        heads_other, dproj_o, head_sums_o = attend_back(info, states, proj_o, ctx_o, logs_o, attn_low, out_o)

        heads_other, down_keep, down_recv, attn_low = sync(heads_other, down_keep, down_recv, attn_low)
        heads_recv = flip(heads_other, ROW)
        down_other = add(down_keep[1], down_recv[1])
        common = [sums_one[:3], sums_two[2:3], sums_two[:2]]
        fill = jnp.zeros((1, width - 2 * cols), F32)
        rows_of = lambda units_row, heads_row: jnp.concatenate(common + [units_row[:1], heads_row], axis=0)
        heads_row_o = jnp.concatenate([head_sums_o[:1, :cols], head_sums_o[:1, 2 * cols :], fill], axis=1)
        small_recv = flip(rows_of(unit_sums_o, heads_row_o), ROW)
        dprojs = [attend_back_heads(info, far(proj), logs, far(attn_low), far(out), 0, 1, deps=[down_other, heads_other])]

        dprojs, up_own, up_recv, attn_low, down_other = sync(dprojs, up_own, up_recv, attn_low, down_other)
        down = down_keep, down_recv, flip(down_other, ROW)
        up_keep, up_send = halves(add(up_own, up_recv), SIDE)
        up = up_keep, flip(up_send, SIDE)
        dprojs = [*dprojs, attend_back_heads(info, far(proj), logs, far(attn_low), far(out), 1, cols // HEAD, deps=[up_send])]

        base = rows_of(unit_sums, jnp.zeros((1, width), F32))
        dprojs, up, small_recv, base, attn_low, heads_recv = sync(dprojs, up, small_recv, base, attn_low, heads_recv)
        up = z_one(add(*up))
        heads_keep, heads_send, dproj = sum_heads(
            info, states, ctx, far(attn_low), base + small_recv, heads_recv, dprojs, deps=[up[0]],
        )
        small = jnp.zeros((32, width), BF16)
        heads = heads_keep, flip(heads_send, SIDE)

        up, dproj, heads_send, out_rows = sync(up, dproj, heads_send, out_rows)
        up = z_two(up)
        out_got = flip(half_rows(out_rows), ROW)
        in_terms = project(info, dproj, dproj_o, qkv, qkv_o, 4, deps=[heads_send, up[0]])
        in_recv = swap(in_terms)
        down, in_terms = sync(down, in_terms)
        down = z_one((wide(down[0][0]) + wide(down[1][0]) + wide(down[2])).astype(BF16))

        heads, up = sync(heads, up)
        heads = z_one(add(*heads))
        up = z_three(up)
        in_rows = jnp.concatenate([wide(a) + wide(b) for a, b in zip(in_terms, in_recv)], axis=0)
        in_rows = (entry_grad + in_rows).astype(BF16)
        in_got = flip(half_rows(in_rows), ROW)
        down, = sync(down)
        down = z_two(down)

        heads, down, up, out_got = sync(heads, down, up, out_got)
        heads = z_two(heads)
        out_again = flip(out_got, CORE)
        up = side_start(z_end(up))
        down = z_three(down)

        heads, down, in_got = sync(heads, down, in_got)
        heads = z_three(heads)
        down = side_start(z_end(down))
        in_again = flip(in_got, CORE)

        heads, = sync(heads)
        heads = z_end(heads)
        half = heads.shape[0] - small.shape[0]
        heads, small = heads[:half], heads[half:]
        heads = side_start(heads)

        up, = sync(up)
        up_out = wide(put_together(*up, SIDE))

        down, in_again, out_again = sync(down, in_again, out_again)
        down_out = wide(put_together(*down, SIDE))
        states_grad = both_spans(in_rows, in_got, in_again)
        states_out = both_spans(out_rows, out_got, out_again)

        heads, up_out, down_out, states_grad, states_out = sync(heads, up_out, down_out, states_grad, states_out)
        heads_out = wide(put_together(*heads, SIDE))
        qkv_out, out_out = heads_out[: 3 * cols], heads_out[3 * cols :]
        small = wide(small)
        parts = [small[k] for k in range(7)] + [small[7, :cols], small[7, cols : 2 * cols]]
        qkv_out = qkv_out.reshape(3, cols, width).transpose(2, 0, 1)
        return (
            states_out, states_grad, qkv_out, parts[7], parts[8], out_out.T, parts[0], parts[1], parts[2],
            up_out, parts[6], down_out, parts[3], parts[4], parts[5],
        )

    return body


def solution(mesh):
    split = P("dp", None, None)
    in_specs = (
        split, P("dp"), P(None, None, "mp"), P("mp"), P("mp"), P(None, "mp"), P(), P(), P(),
        P(None, "mp"), P("mp"), P(None, "mp"), P(), P(), P(), split,
    )
    out_specs = (
        split, split, P(None, None, "mp"), P("mp"), P("mp"), P(None, "mp"), P(), P(), P(),
        P(None, "mp"), P("mp"), P(None, "mp"), P(), P(), P(),
    )
    return jax.shard_map(build(mesh), mesh=mesh, in_specs=in_specs, out_specs=out_specs, check_vma=False)
```

```python
import jax
import jax.numpy as jnp
from jax import lax
from jax.experimental import pallas as pl
from jax.experimental.pallas import tpu as pltpu
from jax.sharding import PartitionSpec as P

HEAD = 64
EPS = 1e-05
F32 = jnp.float32
BF16 = jnp.bfloat16
LIMIT = 24 * 2**20
QBLOCK = 1024
CORE, ROW, SIDE = 1, 2, 4


def dot(a, b, ca, cb):
    return lax.dot_general(a, b, (((ca,), (cb,)), ((), ())), preferred_element_type=F32)


def sds(shape, dtype):
    return jax.ShapeDtypeStruct(shape, dtype)


def whole(array):
    shape = array.shape
    return pl.BlockSpec(shape, lambda i, s: (0,) * len(shape))


def tiled(rows, cols):
    return pl.BlockSpec((rows, cols), lambda i, s: (i, 0))


def slot_rows(array, rows):
    return pl.BlockSpec((None, rows, array.shape[2]), lambda i, s: (s[0], i, 0))


def launch(kernel, info, args, in_specs, out_shapes, out_specs=None, grid=1, deps=(), scratch=(), limit=LIMIT):
    count, extra = len(args), len(deps)

    def inner(info_ref, *refs):
        kernel(info_ref, *refs[:count], *refs[count + extra :])

    specs = [whole(a) if s is None else s for a, s in zip(args, in_specs)]
    out_specs = [None] * len(out_shapes) if out_specs is None else out_specs
    return pl.pallas_call(
        inner,
        out_shape=out_shapes,
        grid_spec=pltpu.PrefetchScalarGridSpec(
            num_scalar_prefetch=1,
            grid=(grid,),
            in_specs=specs + [pl.BlockSpec(memory_space=pl.ANY)] * extra,
            out_specs=[whole(a) if s is None else s for a, s in zip(out_shapes, out_specs)],
            scratch_shapes=scratch,
        ),
        compiler_params=pltpu.CompilerParams(vmem_limit_bytes=limit),
        cost_estimate=pl.CostEstimate(flops=1, bytes_accessed=0, transcendentals=0),
    )(info, *args, *deps)


def far(value):
    return pltpu.with_memory_space_constraint(value, pltpu.HBM)


def norm_forward(inputs):
    centre = inputs - jnp.mean(inputs, axis=-1, keepdims=True)
    spread = jnp.mean(centre * centre, axis=-1, keepdims=True)
    scale = lax.rsqrt(spread + EPS)
    return centre * scale, scale


def norm_backward(grad, normed, scale, gain):
    scaled = grad * gain
    mean_one = jnp.mean(scaled, axis=-1, keepdims=True)
    mean_two = jnp.mean(scaled * normed, axis=-1, keepdims=True)
    return scale * (scaled - mean_one - normed * mean_two)


def column(row, width):
    return jnp.broadcast_to(row, (width, row.shape[1])).T[:, :1]


def wide(value):
    return value.astype(F32)


def attend_kernel(info, rows_ref, weight_ref, pack_ref, proj_ref, ctx_ref, log_ref):
    rows = rows_ref[...]
    cols = weight_ref.shape[0] // 3
    q_bias = column(pack_ref[7:8, :cols], 128)
    v_bias = column(pack_ref[7:8, cols : 2 * cols], 128)
    proj_ref[:cols] = (dot(weight_ref[:cols], rows, 1, 1) + q_bias).astype(BF16)
    proj_ref[cols : 2 * cols] = dot(weight_ref[cols : 2 * cols], rows, 1, 1).astype(BF16)
    proj_ref[2 * cols :] = (dot(weight_ref[2 * cols :], rows, 1, 1) + v_bias).astype(BF16)
    length = rows.shape[0]

    @pl.loop(0, cols // HEAD)
    def _(head):
        rows_of = lambda base: pl.ds(pl.multiple_of(base + head * HEAD, HEAD), HEAD)
        keys = proj_ref[rows_of(cols)]
        values = proj_ref[rows_of(2 * cols)]
        for block in range(length // QBLOCK):
            span = slice(block * QBLOCK, (block + 1) * QBLOCK)
            queries = proj_ref[rows_of(0), span] * BF16(HEAD**-0.5)
            scores = dot(keys, queries, 0, 0)
            highest = jnp.max(scores, axis=0, keepdims=True)
            raised = jnp.exp(scores - highest)
            totals = jnp.sum(raised, axis=0, keepdims=True)
            probs = (raised * (1.0 / totals)).astype(BF16)
            ctx_ref[rows_of(0), span] = dot(values, probs, 1, 0).astype(BF16)
            log_ref[pl.ds(head, 1), span] = highest + jnp.log(totals)


def attend(info, states, weight, pack, deps=()):
    length = states.shape[1]
    cols = weight.shape[0] // 3
    return launch(
        attend_kernel, info, [states, weight, pack], [slot_rows(states, length), None, None],
        [kept((3 * cols, length), BF16), sds((cols, length), BF16), sds((8, length), F32)], deps=deps,
    )


def project_kernel(info, left_ref, left_o_ref, right_ref, right_o_ref, *out_refs):
    size = out_refs[0].shape[0]
    for part, into in enumerate(out_refs):
        span = slice(part * size, (part + 1) * size)
        terms = dot(left_ref[:, span], right_ref[...], 0, 0) + dot(left_o_ref[:, span], right_o_ref[...], 0, 0)
        into[...] = terms.astype(BF16)


def project(info, left, left_o, right, right_o, count, deps=()):
    return launch(
        project_kernel, info, [left, left_o, right, right_o], [None] * 4, chunks(left.shape[1], right.shape[1], count), deps=deps,
    )


def read(refs, steps):
    per = len(refs) // steps
    step = pl.program_id(0)
    parts = []
    for t in range(per):
        value = refs[t][...]
        for k in range(1, steps):
            value = jnp.where(step == k, refs[k * per + t][...], value)
        parts.append(value)
    return wide(jnp.concatenate(parts, axis=0) if per > 1 else parts[0])


def write(refs, steps, value):
    per, rows = max(len(refs) // steps, 1), value.shape[0]
    for k in range(steps):

        @pl.when(pl.program_id(0) == k)
        def _():
            if len(refs) < steps:
                at = k % (steps // len(refs)) * rows
                refs[k * len(refs) // steps][at : at + rows] = value
            else:
                for t in range(per):
                    refs[k * per + t][...] = value[t * rows // per : (t + 1) * rows // per]


def chunks(length, width, count):
    return [sds((length // count, width), BF16)] * count


def kept(shape, dtype):
    return pltpu.HBM(shape, dtype)


def unit_pass(low, up_ref, pack_ref, down_ref, act_ref, slope_ref):
    total = None
    half = up_ref.shape[1] // 2
    for part in range(2):
        cols = slice(part * half, (part + 1) * half)
        hidden = dot(low, up_ref[:, cols], 1, 0) + pack_ref[6:7, cols]
        cdf = 0.5 + 0.5 * lax.erf(hidden * (0.5**0.5))
        pdf = jnp.exp(hidden * hidden * -0.5) * ((2 * jnp.pi) ** -0.5)
        act = (hidden * cdf).astype(BF16)
        act_ref[:, cols] = act
        slope_ref[:, cols] = (cdf + hidden * pdf).astype(BF16)
        term = dot(act, down_ref[:, cols], 1, 1)
        total = term if total is None else total + term
    return total


def feed_own_kernel(info, rows_ref, pack_ref, up_ref, down_ref, *refs):
    first_ref, low_ref, act_ref, slope_ref, part_ref, entry_ref = refs[-6:]
    count = (len(refs) - 6) // 2
    inputs = wide(rows_ref[...]) + (read(refs[:count], 4) + read(refs[count : 2 * count], 4) + pack_ref[0:1])
    entry_ref[...] = inputs
    normed, _ = norm_forward(inputs)
    first = normed * pack_ref[1:2] + pack_ref[2:3]
    first_ref[...] = first
    low = first.astype(BF16)
    low_ref[...] = low
    part_ref[...] = unit_pass(low, up_ref, pack_ref, down_ref, act_ref, slope_ref)


def feed_own(info, states, terms, recv, pack, up, down, deps=()):
    _, length, width = states.shape
    half, units = length // 4, up.shape[1]
    return launch(
        feed_own_kernel, info, [states, pack, up, down, *terms, *recv],
        [slot_rows(states, half)] + [None] * (3 + 2 * len(terms)),
        [sds((length, width), F32), sds((length, width), BF16), sds((length, units), BF16), sds((length, units), BF16), sds((length, width), F32), kept((length, width), F32)],
        [tiled(half, width), tiled(half, width), tiled(half, units), tiled(half, units), tiled(half, width), tiled(half, width)], grid=4, deps=deps,
    )


def places(info, size):
    return [pl.multiple_of(2 * size * info[2], 128), size, pl.multiple_of(2 * size * (1 - info[2]), 128)]


def feed_other_kernel(info, low_ref, part_ref, pack_ref, *refs):
    act_ref, slope_ref = refs[3:5]
    low = low_ref[...]
    total = part_ref[...]
    size = refs[0].shape[1]
    width = low.shape[1]
    for ref, place in zip(refs[:3], places(info, size)):
        cols = pl.ds(place, size)
        hidden = dot(low, ref[:width], 1, 0) + pack_ref[6:7, cols]
        cdf = 0.5 + 0.5 * lax.erf(hidden * (0.5**0.5))
        pdf = jnp.exp(hidden * hidden * -0.5) * ((2 * jnp.pi) ** -0.5)
        act = (hidden * cdf).astype(BF16)
        act_ref[:, cols] = act
        slope_ref[:, cols] = (cdf + hidden * pdf).astype(BF16)
        total = total + dot(act, ref[width:], 1, 1)
    write(refs[5:], 4, total.astype(BF16))


def feed_other(info, low, part, pieces, pack, deps=()):
    length, width = low.shape
    half, units = length // 4, 3 * pieces[0].shape[1]
    return launch(
        feed_other_kernel, info, [low, part, pack, *pieces],
        [tiled(half, width), tiled(half, width), None, None, None, None],
        [sds((length, units), BF16), sds((length, units), BF16)] + chunks(length, width, 2),
        [tiled(half, units), tiled(half, units), None, None], grid=4, deps=deps,
    )


def add_rows(ref, row, value):
    ref[row : row + 1, :] += jnp.sum(value, axis=0, keepdims=True)


def clear_first(ref):
    @pl.when(pl.program_id(0) == 0)
    def _():
        ref[...] = jnp.zeros_like(ref)


def turn_kernel(info, first_ref, *refs):
    terms, recv = refs[:2], refs[2:4]
    cot_ref, pack_ref, out_ref, grad_ref, low_ref, sums_ref = refs[4:]
    live = jnp.where(info[0] < info[1], 1.0, 0.0).astype(F32)
    branch = read(terms, 2) + read(recv, 2) + pack_ref[3:4]
    normed, scale = norm_forward(first_ref[...] + branch)
    out_ref[...] = ((normed * pack_ref[4:5] + pack_ref[5:6]) * live).astype(BF16)
    upstream = wide(cot_ref[...]) * live
    grad = norm_backward(upstream, normed, scale, pack_ref[4:5])
    grad_ref[...] = grad
    low_ref[...] = grad.astype(BF16)
    clear_first(sums_ref)
    add_rows(sums_ref, 0, upstream * normed)
    add_rows(sums_ref, 1, upstream)
    add_rows(sums_ref, 2, grad)


def turn(info, first, terms, recv, cotangent, pack, deps=()):
    length, width = first.shape
    half = length // 2
    tile = tiled(half, width)
    return launch(
        turn_kernel, info, [first, *terms, *recv, cotangent, pack],
        [tile] + [None] * 4 + [slot_rows(cotangent, half), None],
        [kept((length, width), BF16), kept((length, width), F32), sds((length, width), BF16), sds((8, width), F32)],
        [tile, tile, tile, None], grid=2, deps=deps,
    )


def cross_kernel(info, left_ref, right_ref, right_o_ref, keep_ref, send_ref):
    side = info[2]
    half = keep_ref.shape[1]
    for which, ref in ((side, keep_ref), (1 - side, send_ref)):
        left = left_ref[:, pl.ds(pl.multiple_of(which * half, 128), half)]
        ref[0] = dot(left, right_ref[...], 0, 0).astype(BF16)
        ref[1] = dot(left, right_o_ref[...], 0, 0).astype(BF16)


def cross(info, left, right, right_o, deps=()):
    shape = sds((2, left.shape[1] // 2, right.shape[1]), BF16)
    return launch(cross_kernel, info, [left, right, right_o], [None] * 3, [shape, shape], deps=deps)


def plain_cross_kernel(info, left_ref, right_ref, right_o_ref, own_ref, other_ref, sums_ref, sums_o_ref):
    ones = jnp.ones((8, right_ref.shape[0]), BF16)
    for right, into, sums in ((right_ref, own_ref, sums_ref), (right_o_ref, other_ref, sums_o_ref)):
        into[...] = dot(left_ref[...], right[...], 0, 0).astype(BF16)
        sums[...] = dot(ones, right[...], 1, 0)


def plain_cross(info, left, right, right_o, deps=()):
    shape = sds((left.shape[1], right.shape[1]), BF16)
    sums = sds((8, right.shape[1]), F32)
    return launch(plain_cross_kernel, info, [left, right, right_o], [None] * 3, [shape, shape, sums, sums], deps=deps)


def back_own_kernel(info, low_ref, slope_ref, up_ref, down_ref, hidden_ref, part_ref):
    low = low_ref[...]
    half = up_ref.shape[1] // 2
    total = None
    for part in range(2):
        cols = slice(part * half, (part + 1) * half)
        hidden = (wide(slope_ref[:, cols]) * dot(low, down_ref[:, cols], 1, 0)).astype(BF16)
        hidden_ref[:, cols] = hidden
        term = dot(hidden, up_ref[:, cols], 1, 1)
        total = term if total is None else total + term
    part_ref[...] = total


def back_own(info, low, slope, up, down, deps=()):
    length, width = low.shape
    half, units = length // 4, slope.shape[1]
    return launch(
        back_own_kernel, info, [low, slope, up, down], [tiled(half, width), tiled(half, units), None, None],
        [sds((length, units), BF16), sds((length, width), F32)], [tiled(half, units), tiled(half, width)], grid=4, deps=deps,
    )


def back_other_kernel(info, low_ref, slope_ref, part_ref, *refs):
    hidden_ref = refs[3]
    low = low_ref[...]
    width = low.shape[1]
    size = refs[0].shape[1]
    total = part_ref[...]
    for ref, place in zip(refs[:3], places(info, size)):
        cols = pl.ds(place, size)
        hidden = (wide(slope_ref[:, cols]) * dot(low, ref[width:], 1, 0)).astype(BF16)
        hidden_ref[:, cols] = hidden
        total = total + dot(hidden, ref[:width], 1, 1)
    write(refs[4:], 4, total.astype(BF16))


def back_other(info, low, slope, part, pieces, deps=()):
    length, width = low.shape
    half, units = length // 4, slope.shape[1]
    return launch(
        back_other_kernel, info, [low, slope, part, *pieces],
        [tiled(half, width), tiled(half, units), tiled(half, width), None, None, None],
        [sds((length, units), BF16)] + chunks(length, width, 2), [tiled(half, units), None, None], grid=4, deps=deps,
    )


def entry_kernel(info, inputs_ref, second_ref, pack_ref, term_a, term_b, recv_a, recv_b, entry_ref, low_ref, sums_ref):
    normed, scale = norm_forward(inputs_ref[...])
    grad = second_ref[...] + (read([term_a, term_b], 2) + read([recv_a, recv_b], 2))
    entry = norm_backward(grad, normed, scale, pack_ref[1:2])
    entry_ref[...] = entry
    low_ref[...] = entry.astype(BF16)
    clear_first(sums_ref)
    add_rows(sums_ref, 0, entry)
    add_rows(sums_ref, 1, grad * normed)
    add_rows(sums_ref, 2, grad)


def entry(info, inputs, second, pack, back_terms, back_recv, deps=()):
    length, width = inputs.shape
    tile = tiled(length // 2, width)
    return launch(
        entry_kernel, info, [inputs, second, pack, *back_terms, *back_recv], [tile, tile] + [None] * 5,
        [kept((length, width), F32), sds((length, width), BF16), sds((8, width), F32)], [tile, tile, None], grid=2, deps=deps,
    )


def attend_back_kernel(info, rows_ref, proj_ref, ctx_ref, log_ref, low_ref, out_ref, grads_ref, dproj_ref, sums_ref, cgrad):
    length = rows_ref.shape[0]
    cols = ctx_ref.shape[0]
    low = low_ref[...]
    cgrad[...] = dot(out_ref[...], low, 1, 1).astype(BF16)
    scale = HEAD**-0.5

    @pl.loop(0, cols // HEAD, unroll=True)
    def _(head):
        query_rows, key_rows, value_rows = (pl.ds(pl.multiple_of(k * cols + head * HEAD, HEAD), HEAD) for k in range(3))
        keys = proj_ref[key_rows]
        values = proj_ref[value_rows]
        key_total = None
        value_total = None
        for block in range(length // QBLOCK):
            span = slice(block * QBLOCK, (block + 1) * QBLOCK)
            queries = proj_ref[query_rows, span] * BF16(scale)
            upstream = cgrad[query_rows, span]
            scores = dot(keys, queries, 0, 0)
            probs = jnp.exp(scores - log_ref[pl.ds(head, 1), span])
            value_term = dot(upstream, probs.astype(BF16), 1, 1)
            prob_grad = dot(values, upstream, 0, 0)
            inner = jnp.sum(prob_grad * probs, axis=0, keepdims=True)
            score_grad = (probs * (prob_grad - inner)).astype(BF16)
            dproj_ref[query_rows, span] = (dot(keys, score_grad, 1, 0) * scale).astype(BF16)
            key_term = dot(queries, score_grad, 1, 1)
            key_total = key_term if key_total is None else key_total + key_term
            value_total = value_term if value_total is None else value_total + value_term
        dproj_ref[key_rows] = key_total.astype(BF16)
        dproj_ref[value_rows] = value_total.astype(BF16)
    rows = rows_ref[...]
    grads_ref[: 3 * cols] = dot(dproj_ref[...], rows, 1, 0).astype(BF16)
    grads_ref[3 * cols :] = dot(ctx_ref[...], low, 1, 0).astype(BF16)
    sums_ref[...] = dot(jnp.ones((8, length), BF16), dproj_ref[...], 1, 1)


def attend_back(info, states, proj, ctx, log_total, low, out, deps=()):
    _, length, width = states.shape
    cols = ctx.shape[0]
    return launch(
        attend_back_kernel, info, [states, proj, ctx, log_total, low, out], [slot_rows(states, length)] + [None] * 5,
        [sds((4 * cols, width), BF16), sds((3 * cols, length), BF16), sds((8, 3 * cols), F32)], deps=deps,
        scratch=[pltpu.VMEM((cols, length), BF16)],
    )


def attend_back_heads(info, proj, log_total, low, out, first, last, deps=()):
    cols, length = proj.shape[0] // 3, proj.shape[1]
    scale = HEAD**-0.5

    def kernel(info, proj_ref, log_ref, low_ref, out_ref, dproj_ref):
        @pl.loop(0, last - first)
        def _(step):
            head = step + first
            at = lambda k: pl.ds(pl.multiple_of(k * cols + head * HEAD, HEAD), HEAD)
            into = lambda k: pl.ds(pl.multiple_of((3 * step + k) * HEAD, HEAD), HEAD)
            upstream_all = dot(out_ref[at(0)], low_ref[...], 1, 1).astype(BF16)
            keys, values = proj_ref[at(1)], proj_ref[at(2)]
            key_total = None
            value_total = None
            for block in range(length // QBLOCK):
                span = slice(block * QBLOCK, (block + 1) * QBLOCK)
                queries = proj_ref[at(0), span] * BF16(scale)
                upstream = upstream_all[:, span]
                scores = dot(keys, queries, 0, 0)
                probs = jnp.exp(scores - log_ref[pl.ds(head, 1), span])
                value_term = dot(upstream, probs.astype(BF16), 1, 1)
                prob_grad = dot(values, upstream, 0, 0)
                inner = jnp.sum(prob_grad * probs, axis=0, keepdims=True)
                score_grad = (probs * (prob_grad - inner)).astype(BF16)
                dproj_ref[into(0), span] = (dot(keys, score_grad, 1, 0) * scale).astype(BF16)
                key_term = dot(queries, score_grad, 1, 1)
                key_total = key_term if key_total is None else key_total + key_term
                value_total = value_term if value_total is None else value_total + value_term
            dproj_ref[into(1)] = key_total.astype(BF16)
            dproj_ref[into(2)] = value_total.astype(BF16)

    return launch(
        kernel, info, [proj, log_total, low, out], [None] * 4, [sds((3 * HEAD * (last - first), length), BF16)], deps=deps,
    )[0]


def sum_heads(info, states, ctx, low, base, recv, dprojs, deps=()):
    _, length, width = states.shape
    cols = ctx.shape[0]

    def kernel(info, rows_ref, ctx_ref, low_ref, base_ref, recv_ref, *refs):
        keep_ref, send_ref, dproj_ref, total, small = refs[-5:]
        head = 0
        for ref in refs[:-5]:
            for step in range(ref.shape[0] // (3 * HEAD)):
                for k in range(3):
                    at = (3 * step + k) * HEAD
                    dproj_ref[k * cols + head * HEAD : k * cols + (head + 1) * HEAD, :] = ref[at : at + HEAD, :]
                head += 1
        total[: 3 * cols] = (dot(dproj_ref[...], rows_ref[...], 1, 0) + wide(recv_ref[: 3 * cols])).astype(BF16)
        total[3 * cols :] = (dot(ctx_ref[...], low_ref[...], 1, 0) + wide(recv_ref[3 * cols :])).astype(BF16)
        sums = dot(jnp.ones((8, length), BF16), dproj_ref[...], 1, 1)[:1]
        small[...] = jnp.zeros_like(small)
        small[:8] = base_ref[...]
        small[7:8, : 2 * cols] += jnp.concatenate([sums[:, :cols], sums[:, 2 * cols :]], axis=1)
        half = total.shape[0] // 2
        for which, ref in ((info[2], keep_ref), (1 - info[2], send_ref)):
            ref[:half] = total[pl.ds(pl.multiple_of(which * half, 32), half), :]
            ref[half:] = small[...].astype(BF16)

    shape = sds((2 * cols + 32, width), BF16)
    return launch(
        kernel, info, [states, ctx, low, base, recv, *dprojs], [slot_rows(states, length)] + [None] * (4 + len(dprojs)),
        [shape, shape, sds((3 * cols, length), BF16)], deps=deps,
        scratch=[pltpu.VMEM((4 * cols, width), BF16), pltpu.VMEM((32, width), F32)],
    )


def build(mesh):
    n_dp, n_mp = mesh.shape["dp"], mesh.shape["mp"]
    n_z = n_dp // 2
    z_bits = []
    while n_mp * 2 << len(z_bits) < n_dp * n_mp:
        z_bits.append(n_mp * 2 << len(z_bits))

    def flip(value, bit):
        pairs = [(i, i ^ bit) for i in range(n_dp * n_mp)]
        return lax.ppermute(value, ("dp", "mp"), pairs)

    def swap(values):
        return [flip(v, CORE) for v in values]

    def body(
        states, span_count, qkv_weight, q_bias, v_bias, out_weight, out_bias, gain_one, shift_one,
        up_weight, up_bias, down_weight, down_bias, gain_two, shift_two, cotangent,
    ):
        dp, mp = lax.axis_index("dp"), lax.axis_index("mp")
        place = dp * n_mp + mp
        slot, core = mp // ROW, mp % ROW
        info = jnp.stack([slot, span_count[0], dp % 2, dp // 2]).astype(jnp.int32)
        width, _, cols = qkv_weight.shape
        units = up_weight.shape[1]

        token = [place]

        def halves(value, bit):
            side = (token[0] // bit) % 2
            rows = value.shape[0] // 2
            return tuple(lax.dynamic_slice_in_dim(value, w * rows, rows, 0) for w in (side, 1 - side))

        def add(one, two):
            return (wide(one) + wide(two)).astype(BF16)

        def join(value, bit):
            other = flip(value, bit)
            lower = (token[0] // bit) % 2 == 0
            return jnp.concatenate([jnp.where(lower, value, other), jnp.where(lower, other, value)], axis=0)

        def sync(*values):
            token[0], values = lax.optimization_barrier((token[0], values))
            return values

        def put_together(value, other, bit):
            lower = (token[0] // bit) % 2 == 0
            return jnp.concatenate([jnp.where(lower, value, other), jnp.where(lower, other, value)], axis=0)

        z_near, z_far = n_mp * 2, n_mp * 4

        def z_one(value):
            if n_z == 4:
                mine, theirs = halves(value, z_near)
                return mine, flip(theirs, z_near)
            for bit in z_bits:
                value = add(value, flip(value, bit))
            return value, value

        def z_two(pair):
            if n_z != 4:
                return pair
            value = add(*pair)
            return value, flip(value, z_far)

        def z_three(pair):
            if n_z != 4:
                return pair
            value = add(*pair)
            return value, flip(value, z_near)

        def z_end(pair):
            return put_together(*pair, z_near) if n_z == 4 else pair[0]

        def side_start(value):
            return value, flip(value, SIDE)

        joined = jnp.concatenate([q_bias, v_bias, jnp.zeros((width - 2 * cols,), F32)])
        pack = jnp.stack([out_bias, gain_one, shift_one, down_bias, gain_two, shift_two, up_bias, joined])
        qkv = qkv_weight.transpose(1, 2, 0).reshape(3 * cols, width)
        out = out_weight.T
        pack_o = flip(pack, ROW)
        qkv_o = flip(qkv, ROW)

        proj, ctx, logs = attend(info, states, qkv, pack)
        third = units // 3
        side = dp % 2
        cut = lambda w, at: lax.dynamic_slice_in_dim(w, at, third, 1)
        outer = jnp.concatenate([cut(up_weight, 2 * third * side), cut(down_weight, 2 * third * side)], axis=0)
        middle = jnp.concatenate([up_weight[:, third : 2 * third], down_weight[:, third : 2 * third]], axis=0)
        outer, middle, qkv_o, pack_o, out_send, _ = lax.optimization_barrier((outer, middle, qkv_o, pack_o, out, logs))
        outer = flip(outer, ROW)
        out_o = flip(out_send, ROW)
        proj_o, ctx_o, logs_o = attend(info, states, qkv_o, pack_o, deps=[logs])
        middle, ctx_o, outer = lax.optimization_barrier((middle, ctx_o, outer))
        middle = flip(middle, ROW)
        forwarded = flip(outer, SIDE)
        terms = project(info, ctx, ctx_o, out, out_o, 8)
        recv = swap(terms)
        first, low, act, slope, part, entry_in = feed_own(
            info, states, terms, recv, pack, up_weight, down_weight,
        )
        pieces = [outer, middle, forwarded]
        act_o, slope_o, *feed_terms = feed_other(info, low, part, pieces, pack_o)
        out_rows, second, branch_low, sums_two = turn(
            info, first, feed_terms, swap(feed_terms), cotangent, pack,
        )

        def half_rows(span):
            size = span.shape[0] // 2
            return lax.dynamic_slice_in_dim(span, core * size, size, 0)

        def both_spans(span, got, again):
            other = put_together(got, again, CORE)
            return put_together(span[None], other[None], ROW)

        fence = lambda *v: lax.optimization_barrier(v)
        down_keep, down_send = cross(info, branch_low, act, act_o)
        down_recv = flip(down_send, SIDE)
        hidden, back_part = back_own(info, branch_low, slope, up_weight, down_weight, deps=[down_keep])
        hidden_o, *back_terms = back_other(info, branch_low, slope_o, back_part, pieces)
        back_recv = swap(back_terms)
        up_own, up_other, unit_sums, unit_sums_o = plain_cross(info, low, hidden, hidden_o)
        up_recv = flip(up_other, ROW)
        entry_grad, attn_low, sums_one = entry(info, pltpu.with_memory_space_constraint(entry_in, pltpu.HBM), pltpu.with_memory_space_constraint(second, pltpu.HBM), pack, back_terms, back_recv, deps=[up_own])

        heads_other, dproj_o, head_sums_o = attend_back(info, states, proj_o, ctx_o, logs_o, attn_low, out_o)

        heads_other, down_keep, down_recv, attn_low = sync(heads_other, down_keep, down_recv, attn_low)
        heads_recv = flip(heads_other, ROW)
        down_other = add(down_keep[1], down_recv[1])
        common = [sums_one[:3], sums_two[2:3], sums_two[:2]]
        fill = jnp.zeros((1, width - 2 * cols), F32)
        rows_of = lambda units_row, heads_row: jnp.concatenate(common + [units_row[:1], heads_row], axis=0)
        heads_row_o = jnp.concatenate([head_sums_o[:1, :cols], head_sums_o[:1, 2 * cols :], fill], axis=1)
        small_recv = flip(rows_of(unit_sums_o, heads_row_o), ROW)
        dprojs = [attend_back_heads(info, far(proj), logs, far(attn_low), far(out), 0, 1, deps=[down_other, heads_other])]

        dprojs, up_own, up_recv, attn_low, down_other = sync(dprojs, up_own, up_recv, attn_low, down_other)
        down = down_keep, down_recv, flip(down_other, ROW)
        up_keep, up_send = halves(add(up_own, up_recv), SIDE)
        up = up_keep, flip(up_send, SIDE)
        dprojs = [*dprojs, attend_back_heads(info, far(proj), logs, far(attn_low), far(out), 1, cols // HEAD, deps=[up_send])]

        base = rows_of(unit_sums, jnp.zeros((1, width), F32))
        dprojs, up, small_recv, base, attn_low, heads_recv = sync(dprojs, up, small_recv, base, attn_low, heads_recv)
        up = z_one(add(*up))
        heads_keep, heads_send, dproj = sum_heads(
            info, states, ctx, far(attn_low), base + small_recv, heads_recv, dprojs, deps=[up[0]],
        )
        small = jnp.zeros((32, width), BF16)
        heads = heads_keep, flip(heads_send, SIDE)

        up, dproj, heads_send, out_rows = sync(up, dproj, heads_send, out_rows)
        up = z_two(up)
        out_got = flip(half_rows(out_rows), ROW)
        down, dproj = sync(down, dproj)
        down = z_one((wide(down[0][0]) + wide(down[1][0]) + wide(down[2])).astype(BF16))
        in_terms = project(info, dproj, dproj_o, qkv, qkv_o, 4, deps=[heads_send, up[0], down[0]])
        in_recv = swap(in_terms)

        up, in_terms = sync(up, in_terms)
        up = z_three(up)
        heads, = sync(heads)
        heads = z_one(add(*heads))
        in_rows = jnp.concatenate([wide(a) + wide(b) for a, b in zip(in_terms, in_recv)], axis=0)
        in_rows = (entry_grad + in_rows).astype(BF16)
        in_got = flip(half_rows(in_rows), ROW)
        down, = sync(down)
        down = z_two(down)

        heads, down, up, out_got = sync(heads, down, up, out_got)
        heads = z_two(heads)
        out_again = flip(out_got, CORE)
        up = side_start(z_end(up))
        down = z_three(down)

        heads, down, in_got = sync(heads, down, in_got)
        heads = z_three(heads)
        down = side_start(z_end(down))
        in_again = flip(in_got, CORE)

        heads, = sync(heads)
        heads = z_end(heads)
        half = heads.shape[0] - small.shape[0]
        heads, small = heads[:half], heads[half:]
        heads = side_start(heads)

        up, = sync(up)
        up_out = wide(put_together(*up, SIDE))

        down, in_again, out_again = sync(down, in_again, out_again)
        down_out = wide(put_together(*down, SIDE))
        states_grad = both_spans(in_rows, in_got, in_again)
        states_out = both_spans(out_rows, out_got, out_again)

        heads, up_out, down_out, states_grad, states_out = sync(heads, up_out, down_out, states_grad, states_out)
        heads_out = wide(put_together(*heads, SIDE))
        qkv_out, out_out = heads_out[: 3 * cols], heads_out[3 * cols :]
        small = wide(small)
        parts = [small[k] for k in range(7)] + [small[7, :cols], small[7, cols : 2 * cols]]
        qkv_out = qkv_out.reshape(3, cols, width).transpose(2, 0, 1)
        return (
            states_out, states_grad, qkv_out, parts[7], parts[8], out_out.T, parts[0], parts[1], parts[2],
            up_out, parts[6], down_out, parts[3], parts[4], parts[5],
        )

    return body


def solution(mesh):
    split = P("dp", None, None)
    in_specs = (
        split, P("dp"), P(None, None, "mp"), P("mp"), P("mp"), P(None, "mp"), P(), P(), P(),
        P(None, "mp"), P("mp"), P(None, "mp"), P(), P(), P(), split,
    )
    out_specs = (
        split, split, P(None, None, "mp"), P("mp"), P("mp"), P(None, "mp"), P(), P(), P(),
        P(None, "mp"), P("mp"), P(None, "mp"), P(), P(), P(),
    )
    return jax.shard_map(build(mesh), mesh=mesh, in_specs=in_specs, out_specs=out_specs, check_vma=False)
```
